512 devices in a mesh: dp: 128 (over z, y, core), mp: 4 (over x).
Axes of the slice: x: 4, y: 8, z: 8, core: 2. Of those that a mesh axis runs over, the one named last changes fastest.
Arguments:
- tokens: int32 [1024, 5, 31], P(('dp', 'mp')), may hold values from 0 to 27
- accept: int32 [1024], P(('dp', 'mp')), may hold values from 0 to 1, as said below
- dest: int32 [153600, 1], P(('dp', 'mp')), may hold values from 0 to 127; in each aligned block of 300 rows (0 to 299, 300 to 599, ...) at most 5 rows name the same one
- mem_keys: bfloat16 [1024, 150, 512], P(('dp', 'mp')), may hold values from -6 to 6
- mem_values: bfloat16 [1024, 150, 512], P(('dp', 'mp')), may hold values from -6 to 6
- embed: bfloat16 [28, 512], replicated, may hold values from -6 to 6
- w_query: bfloat16 [512, 512], replicated, may hold values from -0.25 to 0.25
- w_key: bfloat16 [512, 512], replicated, may hold values from -0.25 to 0.25
- w_value: bfloat16 [512, 512], replicated, may hold values from -0.25 to 0.25
- w_self: bfloat16 [512, 512], replicated, may hold values from -0.25 to 0.25
- cross_query: bfloat16 [512, 512], replicated, may hold values from -0.25 to 0.25
- cross_out: bfloat16 [512, 512], replicated, may hold values from -0.25 to 0.25
- gain_self: float32 [512], replicated, may hold values from 0.5 to 1.5
- gain_cross: float32 [512], replicated, may hold values from 0.5 to 1.5
- w_in: bfloat16 [512, 1024], P(None, 'mp'), may hold values from -0.25 to 0.25
- w_down: bfloat16 [1024, 512], P('mp'), may hold values from -0.1875 to 0.1875
- gain_ff: float32 [512], replicated, may hold values from 0.5 to 1.5
- head: bfloat16 [512, 28], replicated, may hold values from -0.796875 to 0.796875
- momentum: float32 [1024, 1024], P(('dp', 'mp')), may hold values from -2.7 to 2.7
Outputs:
- new_momentum: float32 [1024, 1024], P(('dp', 'mp'))
- slot_loss: float32 [512, 640], P(('dp', 'mp'))
The draws below stay inside these ranges and needn't reach their ends.
Inputs may be any that keep to these rules, and one draw needn't show every extreme that they name: `dest`: at most 5 tokens of one device name the same index, and some name one exactly 5 times. `accept`: among the spectra of the devices of one index of mp, drawn from the seed, exactly one is accepted; every other spectrum is accepted with probability one half.
All inputs are finite; a program needn't handle non-finite values.
Results may differ from the reference program's by a relative error of at most 0.0095.
Values may be sent and summed in bfloat16 or wider, within the bound.
No kernel may reach another device: no remote copies, remote signals or barrier semaphores. Data moves between devices by JAX's collectives and lax.ppermute only.
A program may use at most 64 MiB of HBM per device.

```python
import math
import jax
import jax.numpy as jnp
import numpy as np
from jax import lax

D = 512
HEADS = 8
FF = 1024
V = 28
BEAM = 5
STEPS = 30
PEAKS = 150
SPEC_DEV = 2
ROWS_DEV = 300
CAP = 5
SPECTRA = 1024
N_DP = 128
N_MP = 4


def draw_accept(key, part):
    key = jax.random.fold_in(key, 7)
    coin_key, group_key, chosen_key = jax.random.split(key, 3)
    coin_flips = jax.random.randint(coin_key, (SPECTRA,), 0, 2, dtype=jnp.int32)
    sparse_group = jax.random.randint(group_key, (), 0, N_MP, dtype=jnp.int32)
    chosen_rank = jax.random.randint(chosen_key, (), 0, SPECTRA // N_MP, dtype=jnp.int32)
    position = jnp.arange(SPECTRA, dtype=jnp.int32)
    owner_device = position // SPEC_DEV
    group_id = owner_device % N_MP
    group_rank = owner_device // N_MP * SPEC_DEV + position % SPEC_DEV
    single_one = (group_rank == chosen_rank).astype(jnp.int32)
    return jnp.where(group_id == sparse_group, single_one, coin_flips).astype(jnp.int32)


def draw_momentum(key, part):
    key = jax.random.fold_in(key, 11)
    entry_key = jax.random.fold_in(key, 0)
    values = jnp.clip(0.45 * jax.random.normal(entry_key, (FF, 2 * D), jnp.float32), -2.7, 2.7)
    return values.astype(jnp.float32)


def touch_ends(values, key, least, largest):
    dims = values.shape
    index_at = [jax.random.randint(jax.random.fold_in(key, axis), (), 0, dims[axis]) for axis in range(len(dims))]
    values = values.at[tuple(index_at)].set(least)
    longest = dims.index(max(dims))
    index_at[longest] = (index_at[longest] + 1) % dims[longest]
    return values.at[tuple(index_at)].set(largest)


def levels(own_key, extent, cuts, least, top_value):
    factor_of = 1.0
    for dim, shards_of in cuts:
        steps = jax.random.uniform(jax.random.fold_in(jax.random.fold_in(own_key, 6), dim), (shards_of,), jnp.float32, least / len(cuts), top_value / len(cuts))
        factor_of = factor_of * jnp.repeat(jnp.exp(steps), extent[dim] // shards_of).reshape((-1,) + (1,) * (len(extent) - 1 - dim))
    return factor_of


def assign_block(key, own, number, rows, number_of, top, most, slope):
    order = jax.random.permutation(key, number_of)
    crowded, ordinary = shares(number_of, rows * top, most, slope, True), shares(number_of, rows * top, most, slope, False)
    places = jnp.arange(number_of)

    def named(sizes, turn):
        used = int((sizes > 0).sum())
        fixed = max(1, used // 4)
        moved = fixed + (places - fixed + turn * (used - fixed)) % max(1, number_of - fixed)
        return jnp.zeros((number_of,), jnp.int32).at[order[jnp.where(places < fixed, places, moved)]].set(jnp.asarray(sizes, jnp.int32))

    sizes = jnp.where(number % 4 == 0, named(crowded, number // 4), named(ordinary, number - number // 4 - 1))
    mixed = jax.random.permutation(jax.random.fold_in(own, 3), number_of)
    giver, sink = mixed[0:number_of // 2 * 2:2], mixed[1:number_of // 2 * 2:2]
    slack = jnp.minimum(sizes[giver] - 1, most - sizes[sink]) // 2
    slack = jnp.where((giver == order[0]) | (sink == order[0]) | (sizes[sink] == 0), 0, jnp.maximum(slack, 0))
    moved = jax.random.randint(jax.random.fold_in(own, 4), (number_of // 2,), 0, 1 << 20) % (slack + 1)
    sizes = sizes.at[giver].add(-moved).at[sink].add(moved)
    items = jnp.searchsorted(jnp.cumsum(sizes), jnp.arange(rows * top), side="right").astype(jnp.int32)
    grid = items.reshape(top, rows).T
    grid = grid[jax.random.permutation(jax.random.fold_in(own, 1), rows)]
    turn = jax.random.randint(jax.random.fold_in(own, 2), (rows, 1), 0, top)
    return jnp.take_along_axis(grid, (jnp.arange(top)[None, :] + turn) % top, axis=1)


def shares(number_of, total, bound, lean, full):
    weights = [(1 << 20) // math.isqrt(rank ** lean) + 1 for rank in range(1, number_of + 1)]
    largest = bound if full else min(bound, max(-(-total // number_of), total * weights[0] // sum(weights)))
    least = 1 if total - largest >= number_of - 1 else 0
    counts, spare = [largest] + [least] * (number_of - 1), total - largest - least * (number_of - 1)
    while spare > 0:
        movable = [i for i in range(1, number_of) if counts[i] < largest] or [i for i in range(1, number_of) if counts[i] < bound]
        mass, left = sum([weights[i] for i in movable]), spare
        for i in movable:
            addition = min(bound - counts[i], max(1, left * weights[i] // mass), spare)
            counts[i] = counts[i] + addition
            spare = spare - addition
    return np.array(counts)


def centred(rng, extent, spread, most, shards=(), held_as=jnp.bfloat16):
    result = spread * jax.random.normal(rng, extent, jnp.float32)
    if shards:
        result = result * levels(rng, extent, shards, -0.22, 0.18)
    return jnp.clip(result, -most, most).astype(held_as)


def setup_inputs(seed: int = 0) -> dict:
    seeds = jax.random.split(jax.random.key(seed), 20)
    tokens = touch_ends(jax.random.randint(seeds[0], (SPECTRA, BEAM, STEPS + 1), 0, V), jax.random.fold_in(seeds[0], 1), 0, V - 1).astype(jnp.int32)
    accept = draw_accept(jax.random.fold_in(seeds[19], 71), 0)
    dest_keys = jax.random.split(jax.random.fold_in(seeds[2], 1), (SPECTRA * BEAM * STEPS) // ROWS_DEV)
    dest_turns = jax.random.permutation(jax.random.fold_in(seeds[2], 3), (SPECTRA * BEAM * STEPS) // ROWS_DEV)
    dest = jax.vmap(lambda own, number: assign_block(jax.random.fold_in(seeds[2], 2), own, number, ROWS_DEV, N_DP, 1, CAP, 2))(dest_keys, dest_turns).reshape((SPECTRA * BEAM * STEPS, 1))
    mem_keys = centred(seeds[3], (SPECTRA, PEAKS, D), 1.0, 6.0, ((0, 512),))
    mem_values = centred(seeds[4], (SPECTRA, PEAKS, D), 1.0, 6.0, ((0, 512),))
    embed = centred(seeds[5], (V, D), 1.0, 6.0)
    w_query = centred(seeds[6], (D, D), D ** -0.5, 0.25)
    w_key = centred(seeds[7], (D, D), D ** -0.5, 0.25)
    w_value = centred(seeds[8], (D, D), D ** -0.5, 0.25)
    w_self = centred(seeds[9], (D, D), D ** -0.5, 0.25)
    cross_query = centred(seeds[10], (D, D), D ** -0.5, 0.25)
    cross_out = centred(seeds[11], (D, D), D ** -0.5, 0.25)
    gain_self = jnp.clip(1.0 + 0.1 * jax.random.normal(seeds[12], (D,), jnp.float32), 0.5, 1.5)
    gain_cross = jnp.clip(1.0 + 0.1 * jax.random.normal(seeds[13], (D,), jnp.float32), 0.5, 1.5)
    w_in = centred(seeds[14], (D, FF), D ** -0.5, 0.25, ((1, 4),))
    w_down = centred(seeds[15], (FF, D), FF ** -0.5, 0.1875, ((0, 4),))
    gain_ff = jnp.clip(1.0 + 0.1 * jax.random.normal(seeds[16], (D,), jnp.float32), 0.5, 1.5)
    head = centred(seeds[17], (D, V), 0.133, 0.796875)
    momentum = draw_momentum(jax.random.fold_in(seeds[19], 71), 0)
    return dict(tokens=tokens, accept=accept, dest=dest, mem_keys=mem_keys, mem_values=mem_values, embed=embed, w_query=w_query, w_key=w_key, w_value=w_value, w_self=w_self, cross_query=cross_query, cross_out=cross_out, gain_self=gain_self, gain_cross=gain_cross, w_in=w_in, w_down=w_down, gain_ff=gain_ff, head=head, momentum=momentum)


def layer_norm(values, gain):
    mean = lax.optimization_barrier(jnp.mean(values, -1, keepdims=True))
    centered = values - mean
    variance = lax.optimization_barrier(jnp.mean(centered * centered, -1, keepdims=True))
    return centered * lax.rsqrt(variance + 1e-05) * gain

def head_logp(total, gain_ff, head):
    normed = layer_norm(total, gain_ff)
    logits = jnp.dot(normed, head.astype(total.dtype), precision=lax.Precision.HIGHEST)
    return jax.nn.log_softmax(logits, -1)

def feed(states, w_in, w_down):
    pre = jnp.dot(states, w_in, preferred_element_type=jnp.float32)
    hidden = jax.nn.gelu(pre).astype(jnp.bfloat16)
    total = states.astype(jnp.float32) + jnp.dot(hidden, w_down, preferred_element_type=jnp.float32)
    return (pre, total)

def label_pick(labels, logp):
    vocab = logp.shape[-1]
    picks = (labels[:, None] == jnp.arange(vocab, dtype=jnp.int32)[None, :]).astype(logp.dtype)
    return (lax.optimization_barrier(jnp.sum(picks * logp, -1)), picks)

def decode(tokens, accept, keys, values, embed, w_query, w_key, w_value, w_self, cross_query, cross_out, gain_self, gain_cross, w_in, w_down, gain_ff, head):
    spec, beam, plus = tokens.shape
    steps = plus - 1
    rows = spec * beam * steps
    width = embed.shape[1]
    vocab = embed.shape[0]
    size = width // HEADS
    peaks = keys.shape[1]
    inputs = tokens[:, :, :steps].reshape(rows)
    labels = tokens[:, :, 1:].reshape(rows)
    picks = (inputs[:, None] == jnp.arange(vocab, dtype=jnp.int32)[None, :]).astype(jnp.bfloat16)
    embedded = jnp.dot(picks, embed, preferred_element_type=jnp.float32).astype(jnp.bfloat16)
    query = jnp.dot(embedded, w_query, preferred_element_type=jnp.float32).astype(jnp.bfloat16).reshape(spec * beam, steps, HEADS, size)
    keyed = jnp.dot(embedded, w_key, preferred_element_type=jnp.float32).astype(jnp.bfloat16).reshape(spec * beam, steps, HEADS, size)
    valued = jnp.dot(embedded, w_value, preferred_element_type=jnp.float32).astype(jnp.bfloat16).reshape(spec * beam, steps, HEADS, size)
    scores = jnp.einsum('nqhd,nkhd->nhqk', query.astype(jnp.float32), keyed.astype(jnp.float32)) / jnp.sqrt(jnp.float32(size))
    causal = jnp.arange(steps)[:, None] >= jnp.arange(steps)[None, :]
    scores = jnp.where(causal[None, None], scores, -1e+30)
    probs = jax.nn.softmax(scores, -1).astype(jnp.bfloat16)
    context = jnp.einsum('nhqk,nkhd->nqhd', probs.astype(jnp.float32), valued.astype(jnp.float32)).astype(jnp.bfloat16).reshape(rows, width)
    attended = layer_norm(embedded.astype(jnp.float32) + jnp.dot(context, w_self, preferred_element_type=jnp.float32), gain_self).astype(jnp.bfloat16)
    cross_q = jnp.dot(attended, cross_query, preferred_element_type=jnp.float32).astype(jnp.bfloat16).reshape(spec, beam * steps, HEADS, size)
    mem_k = keys.reshape(spec, peaks, HEADS, size).astype(jnp.float32)
    mem_v = values.reshape(spec, peaks, HEADS, size).astype(jnp.float32)
    cross_s = jnp.einsum('sqhd,skhd->shqk', cross_q.astype(jnp.float32), mem_k) / jnp.sqrt(jnp.float32(size))
    cross_p = jax.nn.softmax(cross_s, -1).astype(jnp.bfloat16)
    cross_c = jnp.einsum('shqk,skhd->sqhd', cross_p.astype(jnp.float32), mem_v).astype(jnp.bfloat16).reshape(rows, width)
    states = layer_norm(attended.astype(jnp.float32) + jnp.dot(cross_c, cross_out, preferred_element_type=jnp.float32), gain_cross).astype(jnp.bfloat16)
    pre, total = feed(states, w_in, w_down)
    taken, unused = label_pick(labels, head_logp(total, gain_ff, head))
    score = taken.reshape(spec, beam, steps).sum(-1)
    beam_weight = jax.nn.softmax(score / steps, -1)
    weight = accept.astype(score.dtype)[:, None, None] * beam_weight[:, :, None] * jnp.ones((1, 1, steps), score.dtype)
    return (states, labels, weight.reshape(rows), pre, total, taken)

def gradient(states, labels, coef, pre, total, w_down, gain_ff, head):

    def loss_of(value):
        taken, unused = label_pick(labels, head_logp(value, gain_ff, head))
        return -jnp.sum(coef * taken)
    unused, pull = jax.vjp(loss_of, total)
    d_total, = pull(jnp.ones((), total.dtype))
    d_out = d_total.astype(jnp.bfloat16)
    hidden = jax.nn.gelu(pre).astype(jnp.bfloat16)
    grad_down = lax.dot_general(hidden, d_out, (((0,), (0,)), ((), ())), preferred_element_type=jnp.float32)
    d_hidden = lax.dot_general(d_out, w_down, (((1,), (1,)), ((), ())), preferred_element_type=jnp.float32)
    unused_g, pull_gelu = jax.vjp(jax.nn.gelu, pre)
    d_pre, = pull_gelu(d_hidden)
    grad_in = lax.dot_general(d_pre.astype(jnp.bfloat16), states, (((0,), (0,)), ((), ())), preferred_element_type=jnp.float32)
    return jnp.concatenate([grad_in, grad_down], 1)

def reference(tokens, accept, dest, mem_keys, mem_values, embed, w_query, w_key, w_value, w_self, cross_query, cross_out, gain_self, gain_cross, w_in, w_down, gain_ff, head, momentum):
    devices = N_DP * N_MP
    slots = N_DP * CAP
    tok = tokens.reshape(devices, SPEC_DEV, BEAM, STEPS + 1)
    acc = accept.reshape(devices, SPEC_DEV)
    keys = mem_keys.reshape(devices, SPEC_DEV, PEAKS, D)
    vals = mem_values.reshape(devices, SPEC_DEV, PEAKS, D)

    def one_device(parts):
        out = decode(parts[0], parts[1], parts[2], parts[3], embed, w_query, w_key, w_value, w_self, cross_query, cross_out, gain_self, gain_cross, w_in, w_down, gain_ff, head)
        return (out[0], out[1], out[2])
    states, labels, weight = lax.map(one_device, (tok, acc, keys, vals))
    target = dest.reshape(devices, ROWS_DEV)
    hits = (target[:, :, None] == jnp.arange(N_DP, dtype=jnp.int32)[None, None, :]).astype(jnp.int32)
    rank = lax.optimization_barrier(jnp.sum(jnp.cumsum(hits, 1) * hits, -1)) - 1
    device = jnp.arange(devices, dtype=jnp.int32)
    source_dp = device // N_MP
    group = device % N_MP
    index = (((target * N_MP + group[:, None]) * N_DP + source_dp[:, None]) * CAP + rank).reshape(-1).astype(jnp.int32)
    buf_states = jnp.zeros((devices * slots, D), states.dtype).at[index].set(states.reshape(-1, D)).reshape(devices, slots, D)
    buf_labels = jnp.zeros((devices * slots,), jnp.int32).at[index].set(labels.reshape(-1)).reshape(devices, slots)
    buf_weight = jnp.zeros((devices * slots,), weight.dtype).at[index].set(weight.reshape(-1)).reshape(devices, slots)

    def train(carry, parts):
        slot_states, slot_labels, slot_weight = parts
        pre, total = feed(slot_states, w_in, w_down)
        taken, unused = label_pick(slot_labels, head_logp(total, gain_ff, head))
        loss = -slot_weight * taken
        coef = slot_weight / jnp.maximum(jnp.sum(slot_weight), 1.0)
        term = gradient(slot_states, slot_labels, coef, pre, total, w_down, gain_ff, head)
        return (carry + term, loss)
    start = jnp.zeros((FF, 2 * D), jnp.float32).astype(momentum.dtype)
    summed, slot_loss = lax.scan(train, start, (buf_states, buf_labels, buf_weight))
    return (0.9 * momentum + summed, slot_loss)
```

```python
import jax
import jax.numpy as jnp
import numpy as np
from jax import lax
from jax.sharding import Mesh
from jax.sharding import PartitionSpec as P

HEADS = 8
CAP = 5
f32 = jnp.float32
bf16 = jnp.bfloat16


def mm(a, b):
    return jnp.dot(a, b, preferred_element_type=f32)


def layer_norm(values, gain):
    mean = jnp.mean(values, -1, keepdims=True)
    centered = values - mean
    variance = jnp.mean(centered * centered, -1, keepdims=True)
    return centered * lax.rsqrt(variance + 1e-05) * gain


def split(v):
    high = v.astype(bf16)
    return high, (v - high.astype(f32)).astype(bf16)


def attend(tokens, keys, values, embed, w_query, w_key, w_value, w_self, cross_query, cross_out, gain_self, gain_cross):
    spec, beam, plus = tokens.shape
    steps = plus - 1
    rows = spec * beam * steps
    width = embed.shape[1]
    vocab = embed.shape[0]
    size = width // HEADS
    peaks = keys.shape[1]
    inputs = tokens[:, :, :steps].reshape(rows)
    picks = (inputs[:, None] == jnp.arange(vocab, dtype=jnp.int32)[None, :]).astype(bf16)
    embedded = mm(picks, embed).astype(bf16)
    query = mm(embedded, w_query).astype(bf16).reshape(spec * beam, steps, HEADS, size)
    keyed = mm(embedded, w_key).astype(bf16).reshape(spec * beam, steps, HEADS, size)
    valued = mm(embedded, w_value).astype(bf16).reshape(spec * beam, steps, HEADS, size)
    scores = jnp.einsum("nqhd,nkhd->nhqk", query, keyed, preferred_element_type=f32) / jnp.sqrt(f32(size))
    causal = jnp.arange(steps)[:, None] >= jnp.arange(steps)[None, :]
    scores = jnp.where(causal[None, None], scores, -1e30)
    probs = jax.nn.softmax(scores, -1).astype(bf16)
    context = (
        jnp.einsum("nhqk,nkhd->nqhd", probs, valued, preferred_element_type=f32).astype(bf16).reshape(rows, width)
    )
    attended = layer_norm(embedded.astype(f32) + mm(context, w_self), gain_self).astype(bf16)
    cross_q = mm(attended, cross_query).astype(bf16).reshape(spec, beam * steps, HEADS, size)
    mem_k = keys.reshape(spec, peaks, HEADS, size)
    mem_v = values.reshape(spec, peaks, HEADS, size)
    cross_s = jnp.einsum("sqhd,skhd->shqk", cross_q, mem_k, preferred_element_type=f32) / jnp.sqrt(f32(size))
    cross_p = jax.nn.softmax(cross_s, -1).astype(bf16)
    cross_c = jnp.einsum("shqk,skhd->sqhd", cross_p, mem_v, preferred_element_type=f32).astype(bf16).reshape(rows, width)
    return layer_norm(attended.astype(f32) + mm(cross_c, cross_out), gain_cross).astype(bf16)


def gather_weights(w_in, w_down):
    depth, part = w_in.shape
    mine_in = w_in.reshape(2, part, part)
    mine_down = jnp.stack([w_down[:, :part], w_down[:, part:]])
    core = lax.axis_index("core")
    first = core == 0
    mine = jnp.where(first, mine_in, mine_down)
    n_x = lax.axis_size("x")
    got = lax.all_to_all(jnp.broadcast_to(mine[None], (n_x,) + mine.shape), "x", 0, 0)
    other = lax.ppermute(got, "core", [(0, 1), (1, 0)])
    all_in = jnp.where(first, got, other)
    all_down = jnp.where(first, other, got)
    all_in = all_in.transpose(1, 2, 0, 3).reshape(depth, n_x * part)
    all_down = all_down.transpose(0, 2, 1, 3).reshape(n_x * part, depth)
    return all_in, all_down


def scatter_sum(term):
    units, cols = term.shape
    n_x = lax.axis_size("x")
    core = lax.axis_index("core")
    pairs = units // (2 * n_x * 2)
    term = term.astype(bf16).reshape(pairs, 2, n_x * 2, cols)
    keep = lax.dynamic_index_in_dim(term, core, 1, False)
    send = lax.dynamic_index_in_dim(term, 1 - core, 1, False)
    other = lax.ppermute(send, "core", [(0, 1), (1, 0)])
    both = (keep.astype(f32) + other.astype(f32)).astype(bf16)
    both = both.reshape(pairs, n_x, 2, cols).transpose(1, 2, 0, 3)
    got = lax.all_to_all(both, "x", 0, 0)
    mine = jnp.sum(got.astype(f32), 0).astype(bf16)
    mine = mine.transpose(1, 0, 2).reshape(pairs, 16, 128)
    got = lax.all_to_all(mine, ("z", "y"), 0, 0)
    return jnp.sum(got.astype(f32), 0).reshape(2, cols)


def per_device(
    tokens, accept, dest, mem_keys, mem_values, embed, w_query, w_key, w_value, w_self, cross_query, cross_out,
    gain_self, gain_cross, w_in, w_down, gain_ff, head, momentum,
):
    spec, beam, plus = tokens.shape
    steps = plus - 1
    rows = spec * beam * steps
    vocab, width = embed.shape
    dp = ("z", "y", "core")
    n_dp = lax.axis_size(dp)

    w_in_all, w_down_all = gather_weights(w_in, w_down)
    states = attend(
        tokens, mem_keys, mem_values, embed, w_query, w_key, w_value, w_self, cross_query, cross_out, gain_self, gain_cross
    )
    labels = tokens[:, :, 1:].reshape(rows)

    pre = mm(states, w_in_all)
    inner = 0.7978845608028654 * (pre + 0.044715 * pre * pre * pre)
    tanh = jnp.tanh(inner)
    hidden = (0.5 * pre * (1.0 + tanh)).astype(bf16)
    slope = 0.5 * (1.0 + tanh) + 0.5 * pre * (1.0 - tanh * tanh) * 0.7978845608028654 * (1.0 + 0.134145 * pre * pre)
    total = states.astype(f32) + mm(hidden, w_down_all)
    mean = jnp.mean(total, -1, keepdims=True)
    centered = total - mean
    scale = lax.rsqrt(jnp.mean(centered * centered, -1, keepdims=True) + 1e-05)
    unit = centered * scale
    high, low = split(unit * gain_ff)
    logits = mm(high, head) + mm(low, head)
    logp = jax.nn.log_softmax(logits, -1)
    is_label = (labels[:, None] == jnp.arange(vocab, dtype=jnp.int32)[None, :]).astype(f32)
    taken = jnp.sum(is_label * logp, -1)
    beam_weight = jax.nn.softmax(taken.reshape(spec, beam, steps).sum(-1) / steps, -1)
    weight = (accept.astype(f32)[:, None, None] * beam_weight[:, :, None] * jnp.ones((1, 1, steps), f32)).reshape(rows)

    target = dest[:, 0]
    hits = (target[:, None] == jnp.arange(n_dp, dtype=jnp.int32)[None, :])
    hits16 = hits.astype(bf16)
    earlier = jnp.asarray(np.tril(np.ones((rows, rows)), -1), bf16)
    rank = jnp.sum(mm(earlier, hits16) * hits.astype(f32), -1).astype(jnp.int32)
    sums = jnp.sum(hits.astype(f32) * weight[:, None], 0)
    loss = -weight * taken
    at_rank = (rank[:, None] == jnp.arange(128, dtype=jnp.int32)[None, :]).astype(f32)
    slots = lax.dot_general(
        hits.astype(f32) * loss[:, None], at_rank, (((0,), (0,)), ((), ())), precision=lax.Precision.HIGHEST
    )
    message = jnp.concatenate([jnp.broadcast_to(sums[None, :], (n_dp, n_dp)), slots], 1)
    got = lax.all_to_all(message[:, None, :], dp, 0, 0)[:, 0]
    slot_loss = got[:, n_dp : n_dp + CAP].reshape(1, n_dp * CAP)
    inverse = 1.0 / jnp.maximum(jnp.sum(got[:, :n_dp], 0), 1.0)
    factor = jnp.sum(hits.astype(f32) * inverse[None, :], -1)

    high, low = split(weight[:, None] * (jnp.exp(logp) - is_label))
    flip = (((1,), (1,)), ((), ()))
    d_unit = gain_ff * (
        lax.dot_general(high, head, flip, preferred_element_type=f32)
        + lax.dot_general(low, head, flip, preferred_element_type=f32)
    )
    d_total = scale * (
        d_unit - jnp.mean(d_unit, -1, keepdims=True) - unit * jnp.mean(d_unit * unit, -1, keepdims=True)
    )
    d_hidden = lax.dot_general(d_total.astype(bf16), w_down_all, flip, preferred_element_type=f32)
    d_pre = (slope * d_hidden * factor[:, None]).astype(bf16)
    d_out = (d_total * factor[:, None]).astype(bf16)
    tall = (((0,), (0,)), ((), ()))
    grad_in = lax.dot_general(d_pre, states, tall, preferred_element_type=f32)
    grad_down = lax.dot_general(hidden, d_out, tall, preferred_element_type=f32)
    share = scatter_sum(jnp.concatenate([grad_in, grad_down], 1))
    return (0.9 * momentum + share, slot_loss)


def solution(mesh):
    n_dp, n_mp = mesh.devices.shape
    side = int(np.sqrt(n_dp // 2))
    fine = Mesh(mesh.devices.reshape(side, side, 2, n_mp), ("z", "y", "core", "x"))
    every = ("z", "y", "core", "x")
    placed = (
        P(every, None, None),
        P(every),
        P(every, None),
        P(every, None, None),
        P(every, None, None),
        P(),
        P(),
        P(),
        P(),
        P(),
        P(),
        P(),
        P(),
        P(),
        P(None, "x"),
        P("x", None),
        P(),
        P(),
        P(every, None),
    )
    return jax.shard_map(
        per_device,
        mesh=fine,
        in_specs=placed,
        out_specs=(P(every, None), P(every, None)),
        check_vma=False,
    )
```

```python
import functools

import jax
import jax.numpy as jnp
import numpy as np
from jax import lax
from jax.experimental import pallas as pl
from jax.experimental.pallas import tpu as pltpu
from jax.sharding import Mesh
from jax.sharding import PartitionSpec as P

HEADS = 8
BEAM = 5
STEPS = 30
CAP = 5
SEG = BEAM * (STEPS + 1)
PAD = 160
ROWS = 2 * PAD
WIDTH = 512
FF = 1024
VOCAB = 28
PEAKS = 150
LANES = 128
N_DP = 128
N_X = 4
PART = FF // N_X
HALF = FF // 2
PAY = 4 * WIDTH + LANES
f32 = jnp.float32
bf16 = jnp.bfloat16
FLIP = (((1,), (1,)), ((), ()))
TALL = (((0,), (0,)), ((), ()))
DP = ("z", "y", "core")
EVERY = ("z", "y", "core", "x")


def mm(a, b):
    return jnp.dot(a, b, preferred_element_type=f32)


def mm_flip(a, b):
    return lax.dot_general(a, b, FLIP, preferred_element_type=f32)


def mm_tall(a, b):
    return lax.dot_general(a, b, TALL, preferred_element_type=f32)


def iota(shape, dim):
    return lax.broadcasted_iota(jnp.int32, shape, dim)


def norm_parts(values):
    mean = jnp.mean(values, -1, keepdims=True)
    centered = values - mean
    scale = lax.rsqrt(jnp.mean(centered * centered, -1, keepdims=True) + 1e-05)
    return centered * scale, scale


def split(v):
    high = v.astype(bf16)
    return high, (v - high.astype(f32)).astype(bf16)


def call(body, outs, scratch=(), cost=4.0, n_smem=0, n_in=0, name=None):
    smem = [pl.BlockSpec(memory_space=pltpu.SMEM)] * n_smem
    vmem = [pl.BlockSpec(memory_space=pltpu.VMEM)] * n_in
    shapes = [jax.ShapeDtypeStruct(s, d) for s, d in outs]
    specs = [pl.BlockSpec(memory_space=pltpu.VMEM)] * len(outs)
    single = len(outs) == 1
    return pl.pallas_call(
        body,
        out_shape=shapes[0] if single else shapes,
        in_specs=smem + vmem,
        out_specs=specs[0] if single else specs,
        scratch_shapes=list(scratch),
        compiler_params=pltpu.CompilerParams(vmem_limit_bytes=40 * 1024 * 1024),
        cost_estimate=pl.CostEstimate(flops=int(cost * 5e8), bytes_accessed=int(cost * 2e6), transcendentals=0),
        name=name,
    )


def prepare_body(core_ref, perm_ref, w_in_ref, w_down_ref, out_ref):
    core = core_ref[0]

    @pl.when(core == 0)
    def _():
        mine = mm(w_in_ref[...], perm_ref[...]).astype(bf16).reshape(2, PART, PART)
        for k in range(N_X):
            out_ref[k] = mine

    @pl.when(core != 0)
    def _():
        mine = mm_tall(perm_ref[...], w_down_ref[...]).astype(bf16)
        for k in range(N_X):
            out_ref[k, 0] = mine[:, :PART]
            out_ref[k, 1] = mine[:, PART:]


def attend_body(
    cols_ref, rows_ref, same_ref, keys_ref, values_ref, embed_ref, w_query_ref, w_key_ref, w_value_ref, w_self_ref,
    cross_query_ref, cross_out_ref, gain_self_ref, gain_cross_ref, states_ref, ctx_ref,
):
    embed = embed_ref[...]
    names = (iota((32, VOCAB), 0) == iota((32, VOCAB), 1)).astype(bf16)
    table = mm(names, embed).astype(bf16)
    picks = (cols_ref[:, 0:1] == iota((ROWS, 32), 1)).astype(bf16)
    picks_t = (rows_ref[0:1, :] == iota((32, ROWS), 0)).astype(bf16)
    embedded = mm(picks, table)
    query = mm(embedded.astype(bf16), w_query_ref[...]).astype(bf16)
    keyed = mm(table, w_key_ref[...])
    valued = mm(table, w_value_ref[...])
    own = iota((HEADS * 32, WIDTH), 0) // 32 == iota((HEADS * 32, WIDTH), 1) // 64
    key_blocks = jnp.where(own, jnp.concatenate([keyed] * HEADS, 0), 0.0).astype(bf16)
    value_blocks = jnp.where(own, jnp.concatenate([valued] * HEADS, 0), 0.0).astype(bf16)
    scores = (mm_flip(key_blocks, query) * 0.125).reshape(HEADS, 32, ROWS)
    counts = mm(picks_t, same_ref[...])[None]
    scores = jnp.where(counts > 0.0, scores, -1e30)
    probs = jnp.exp(scores - jnp.max(scores, 1, keepdims=True)) * counts
    probs = probs / jnp.sum(probs, 1, keepdims=True)
    context = mm_tall(probs.reshape(HEADS * 32, ROWS).astype(bf16), value_blocks).astype(bf16)
    unit, _ = norm_parts(embedded + mm(context, w_self_ref[...]))
    attended = (unit * gain_self_ref[...]).astype(bf16)
    cross_q = mm(attended, cross_query_ref[...]).astype(bf16)
    left = iota((PAD, LANES), 1) < 64
    for s in range(2):
        for pair in range(HEADS // 2):
            lanes = slice(pair * LANES, (pair + 1) * LANES)
            q = cross_q[s * PAD : (s + 1) * PAD, lanes]
            k = keys_ref[s, :, lanes]
            v = values_ref[s, :, lanes]
            both = []
            for mine in (left, jnp.logical_not(left)):
                logit = mm_flip(jnp.where(mine, q, jnp.zeros_like(q)), k) * 0.125
                e = jnp.exp(logit - jnp.max(logit, -1, keepdims=True))
                p = (e / jnp.sum(e, -1, keepdims=True)).astype(bf16)
                both.append(mm(p, v))
            ctx_ref[s * PAD : (s + 1) * PAD, lanes] = jnp.where(left, both[0], both[1]).astype(bf16)
    unit, _ = norm_parts(attended.astype(f32) + mm(ctx_ref[...], cross_out_ref[...]))
    states_ref[...] = (unit * gain_cross_ref[...]).astype(bf16)


def forward_body(
    core_ref, accept_ref, cols_ref, rows_ref, beams_ref, states_ref, got_ref, other_ref, gain_ref, head_ref,
    message_ref, hidden_ref, slope_ref, unit_ref, w_down_ref, signal_ref, scale_ref,
):
    first = core_ref[0] == 0
    states = states_ref[...]
    total = [states[:, :PART].astype(f32), states[:, PART:].astype(f32)]
    for m in range(N_X):
        got, other = got_ref[m], other_ref[m]
        w_in = jnp.where(first, got, other).reshape(WIDTH, PART)
        w_down = jnp.where(first, other, got)
        w_down_ref[m] = w_down
        pre = mm(states, w_in)
        tanh = jnp.tanh(0.7978845608028654 * (pre + 0.044715 * pre * pre * pre))
        hidden = (0.5 * pre * (1.0 + tanh)).astype(bf16)
        slope = 0.5 * (1.0 + tanh) + 0.5 * pre * (1.0 - tanh * tanh) * 0.7978845608028654 * (1.0 + 0.134145 * pre * pre)
        for c in range(2):
            here = slice(c * HALF + m * LANES, c * HALF + (m + 1) * LANES)
            hidden_ref[:, here] = hidden[:, c * LANES : (c + 1) * LANES]
            slope_ref[:, here] = slope[:, c * LANES : (c + 1) * LANES]
        for k in range(2):
            total[k] = total[k] + mm(hidden, w_down[k])
    unit, scale = norm_parts(jnp.concatenate(total, 1))
    unit_ref[...] = unit
    scale_ref[...] = jnp.broadcast_to(scale, (ROWS, LANES))
    high, low = split(unit * gain_ref[...])
    logits = mm(high, head_ref[...]) + mm(low, head_ref[...])
    lane = iota((ROWS, LANES), 1)
    logits = jnp.where(lane < VOCAB, logits, -1e30)
    top = jnp.max(logits, -1, keepdims=True)
    grown = jnp.exp(logits - top)
    mass = jnp.sum(grown, -1, keepdims=True)
    is_label = cols_ref[:, 1:2] == lane
    taken = jnp.sum(jnp.where(is_label, logits, 0.0), -1, keepdims=True) - top - jnp.log(mass)
    beams = beams_ref[...]
    score = jnp.sum(beams * taken, 0, keepdims=True) / STEPS
    place = iota((1, LANES), 1)
    shares = jnp.zeros((1, LANES), f32)
    for s in range(2):
        inside = (place >= s * BEAM) & (place < (s + 1) * BEAM)
        e = jnp.where(inside, jnp.exp(score - jnp.max(jnp.where(inside, score, -1e30), -1, keepdims=True)), 0.0)
        share = e / jnp.sum(e, -1, keepdims=True) * accept_ref[s].astype(f32)
        shares = jnp.where(inside, share, shares)
    weight = jnp.sum(beams * shares, -1, keepdims=True)
    signal_ref[...] = weight * (grown / mass - is_label.astype(f32))
    hits = cols_ref[:, 2:3] == lane
    earlier = (iota((ROWS, ROWS), 0) > iota((ROWS, ROWS), 1)).astype(bf16)
    before = mm(earlier, hits.astype(bf16))
    rank = jnp.sum(jnp.where(hits, before, 0.0), -1, keepdims=True).astype(jnp.int32)
    sums = jnp.sum(jnp.where(hits, weight, 0.0), 0, keepdims=True)
    placed = jnp.where(rank == lane, -weight * taken, 0.0)
    hits_t = (rows_ref[2:3, :] == iota((LANES, ROWS), 0)).astype(bf16)
    high, low = split(placed)
    message_ref[:, 0, :] = jnp.broadcast_to(sums, (N_DP, LANES))
    message_ref[:, 1, :] = mm(hits_t, high) + mm(hits_t, low)


def backward_body(
    core_ref, cols_ref, states_ref, hidden_ref, slope_ref, unit_ref, w_down_ref, signal_ref, scale_ref, gain_ref, head_ref,
    keep_ref, send_ref, d_pre_ref,
):
    core = core_ref[0]
    unit = unit_ref[...]
    high, low = split(signal_ref[...])
    d_unit = gain_ref[...] * (mm_flip(high, head_ref[...]) + mm_flip(low, head_ref[...]))
    along = jnp.mean(d_unit * unit, -1, keepdims=True)
    d_total = scale_ref[:, 0:1] * (d_unit - jnp.mean(d_unit, -1, keepdims=True) - unit * along)
    d_out = d_total.astype(bf16)
    for m in range(N_X):
        d_hidden = mm_flip(d_out[:, :PART], w_down_ref[m, 0]) + mm_flip(d_out[:, PART:], w_down_ref[m, 1])
        for c in range(2):
            here = slice(m * LANES, (m + 1) * LANES)
            there = slice(c * HALF + m * LANES, c * HALF + (m + 1) * LANES)
            d_pre_ref[c, :, here] = (d_hidden[:, c * LANES : (c + 1) * LANES] * slope_ref[:, there]).astype(bf16)
    states = states_ref[...]
    dest = jnp.broadcast_to(cols_ref[:, 2:3], (ROWS, LANES)).astype(f32).astype(bf16)
    for ref, half in ((keep_ref, core), (send_ref, 1 - core)):
        ref[:, 0:WIDTH] = d_pre_ref[half]
        ref[:, WIDTH : 2 * WIDTH] = hidden_ref[:, pl.ds(pl.multiple_of(half * HALF, HALF), HALF)]
        ref[:, 2 * WIDTH : 3 * WIDTH] = states
        ref[:, 3 * WIDTH : 4 * WIDTH] = d_out
        ref[:, 4 * WIDTH :] = dest


def term_body(keep_ref, other_ref, got_ref, term_ref, loss_ref, all_ref):
    sums = jnp.sum(got_ref[:, 0, :], 0, keepdims=True)
    loss_ref[...] = got_ref[:, 1, :]
    inverse = 1.0 / jnp.maximum(sums, 1.0)
    lane = iota((ROWS, LANES), 1).astype(f32)
    for place, ref in ((0, keep_ref), (1, other_ref)):
        rows = slice(place * ROWS, (place + 1) * ROWS)
        hits = ref[:, 4 * WIDTH :].astype(f32) == lane
        factor = jnp.sum(jnp.where(hits, inverse, 0.0), -1, keepdims=True)
        all_ref[rows, : 2 * WIDTH] = ref[:, : 2 * WIDTH]
        all_ref[rows, 2 * WIDTH :] = (ref[:, 2 * WIDTH : 4 * WIDTH].astype(f32) * factor).astype(bf16)
    for k in range(2):
        grad = mm_tall(all_ref[:, k * WIDTH : (k + 1) * WIDTH], all_ref[:, (k + 2) * WIDTH : (k + 3) * WIDTH])
        grad = grad.astype(bf16)
        for m in range(N_X):
            for x in range(N_X):
                start = m * LANES + x * 32
                term_ref[x, m * 32 : (m + 1) * 32, k * WIDTH : (k + 1) * WIDTH] = grad[start : start + 32]


def middle_body(got_ref, out_ref, held_ref):
    total = got_ref[0].astype(f32)
    for k in range(1, N_X):
        total = total + got_ref[k].astype(f32)
    for m in range(N_X):
        for r in range(2):
            for c in range(8):
                block = total[m * 32 + r * 16 : m * 32 + (r + 1) * 16, c * LANES : (c + 1) * LANES]
                held_ref[m * 16 : (m + 1) * 16, r * 8 + c, :] = block
    out_ref[...] = held_ref[...].astype(bf16)


def final_body(got_ref, momentum_ref, out_ref):
    total = jnp.sum(got_ref[...].astype(f32), 0)
    for r in range(2):
        for c in range(8):
            lanes = slice(c * LANES, (c + 1) * LANES)
            out_ref[r : r + 1, lanes] = 0.9 * momentum_ref[r : r + 1, lanes] + total[r * 8 + c : r * 8 + c + 1]


def constants():
    unit = np.arange(PART)
    target = unit.reshape(2, 4, 2, 16).transpose(3, 0, 1, 2).reshape(-1)
    perm = np.zeros((PART, PART), np.float32)
    perm[unit, target] = 1.0
    row = np.arange(ROWS)
    inside = row % PAD
    group = row // PAD * 6 + inside // (STEPS + 1)
    same = (group[:, None] == group[None, :]) & (row[:, None] <= row[None, :])
    valid = (inside < SEG) & (inside % (STEPS + 1) < STEPS)
    beam = np.where(valid, row // PAD * BEAM + inside // (STEPS + 1), -1)
    beams = beam[:, None] == np.arange(LANES)[None, :]
    return jnp.asarray(perm, bf16), jnp.asarray(same, bf16), jnp.asarray(beams, f32)


def per_device(
    tokens, accept, dest, mem_keys, mem_values, embed, w_query, w_key, w_value, w_self, cross_query, cross_out,
    gain_self, gain_cross, w_in, w_down, gain_ff, head, momentum,
):
    perm, same, beams = constants()
    core = lax.axis_index("core").astype(jnp.int32).reshape(1)
    swap = [(0, 1), (1, 0)]

    mine = call(prepare_body, [((N_X, 2, PART, PART), bf16)], n_smem=1, n_in=3, cost=1, name="prepare")(core, perm, w_in, w_down)
    got_w = lax.all_to_all(mine, "x", 0, 0)
    other_w = lax.ppermute(got_w, "core", swap)

    flat = jnp.pad(tokens.reshape(2, SEG), ((0, 0), (0, PAD - SEG))).reshape(ROWS)
    nexts = jnp.concatenate([flat[1:], flat[:1]])
    place = jnp.pad(dest.reshape(2, BEAM, STEPS), ((0, 0), (0, 0), (0, 1)), constant_values=-1).reshape(2, SEG)
    place = jnp.pad(place, ((0, 0), (0, PAD - SEG)), constant_values=-1).reshape(ROWS)
    rows = jnp.stack([flat, nexts, place, place, place, place, place, place])
    cols = rows.T
    states = call(
        attend_body, [((ROWS, WIDTH), bf16)], scratch=[pltpu.VMEM((ROWS, WIDTH), bf16)], n_in=14, cost=8, name="attend"
    )(
        cols, rows, same, mem_keys, mem_values, embed, w_query, w_key, w_value, w_self, cross_query, cross_out,
        gain_self.reshape(1, WIDTH), gain_cross.reshape(1, WIDTH),
    )
    gain = gain_ff.reshape(1, WIDTH)
    head = jnp.pad(head, ((0, 0), (0, LANES - VOCAB)))
    message, hidden, slope, unit, down, signal, scale = call(
        forward_body,
        [
            ((N_DP, 2, LANES), f32),
            ((ROWS, FF), bf16),
            ((ROWS, FF), f32),
            ((ROWS, WIDTH), f32),
            ((N_X, 2, PART, PART), bf16),
            ((ROWS, LANES), f32),
            ((ROWS, LANES), f32),
        ],
        n_smem=2, n_in=8, cost=5, name="forward",
    )(core, accept, cols, rows, beams, states, got_w, other_w, gain, head)
    got = lax.all_to_all(message, DP, 0, 0)
    keep, send = call(
        backward_body,
        [((ROWS, PAY), bf16), ((ROWS, PAY), bf16)],
        scratch=[pltpu.VMEM((2, ROWS, HALF), bf16)],
        n_smem=1, n_in=10, cost=4, name="backward",
    )(core, cols, states, hidden, slope, unit, down, signal, scale, gain, head)
    other = lax.ppermute(send, "core", swap)
    term, loss = call(
        term_body,
        [((N_X, LANES, 2 * WIDTH), bf16), ((N_DP, LANES), f32)],
        scratch=[pltpu.VMEM((2 * ROWS, 4 * WIDTH), bf16)],
        n_in=3, cost=4, name="term",
    )(keep, other, got)
    got = lax.all_to_all(term, "x", 0, 0)
    middle = call(
        middle_body, [((64, 16, LANES), bf16)], scratch=[pltpu.VMEM((64, 16, LANES), f32)], n_in=1, cost=1, name="middle"
    )(got)
    got = lax.all_to_all(middle, ("z", "y"), 0, 0)
    out = call(final_body, [((2, 2 * WIDTH), f32)], n_in=2, cost=1, name="final")(got, momentum)
    return out, loss[:, :CAP].reshape(1, N_DP * CAP)


def solution(mesh):
    n_dp, n_mp = mesh.devices.shape
    side = int(np.sqrt(n_dp // 2))
    fine = Mesh(mesh.devices.reshape(side, side, 2, n_mp), EVERY)
    placed = (
        P(EVERY, None, None),
        P(EVERY),
        P(EVERY, None),
        P(EVERY, None, None),
        P(EVERY, None, None),
        P(),
        P(),
        P(),
        P(),
        P(),
        P(),
        P(),
        P(),
        P(),
        P(None, "x"),
        P("x", None),
        P(),
        P(),
        P(EVERY, None),
    )
    return jax.shard_map(
        per_device,
        mesh=fine,
        in_specs=placed,
        out_specs=(P(EVERY, None), P(EVERY, None)),
        check_vma=False,
    )
```

```python
import jax
import jax.numpy as jnp
import numpy as np
from jax import lax
from jax.experimental import pallas as pl
from jax.experimental.pallas import tpu as pltpu
from jax.sharding import Mesh
from jax.sharding import PartitionSpec as P

HEADS = 8
BEAM = 5
STEPS = 30
CAP = 5
SEG = BEAM * (STEPS + 1)
PAD = 160
ROWS = 2 * PAD
WIDTH = 512
FF = 1024
VOCAB = 28
PEAKS = 150
LANES = 128
N_DP = 128
N_X = 4
PART = FF // N_X
HALF = FF // 2
PAY = 4 * WIDTH + LANES
f32 = jnp.float32
bf16 = jnp.bfloat16
FLIP = (((1,), (1,)), ((), ()))
TALL = (((0,), (0,)), ((), ()))
DP = ("z", "y", "core")
EVERY = ("z", "y", "core", "x")


def mm(a, b):
    return jnp.dot(a, b, preferred_element_type=f32)


def mm_flip(a, b):
    return lax.dot_general(a, b, FLIP, preferred_element_type=f32)


def mm_tall(a, b):
    return lax.dot_general(a, b, TALL, preferred_element_type=f32)


def iota(shape, dim):
    return lax.broadcasted_iota(jnp.int32, shape, dim)


def norm_parts(values):
    mean = jnp.mean(values, -1, keepdims=True)
    centered = values - mean
    scale = lax.rsqrt(jnp.mean(centered * centered, -1, keepdims=True) + 1e-05)
    return centered * scale, scale


def split(v):
    high = v.astype(bf16)
    return high, (v - high.astype(f32)).astype(bf16)


def call(body, outs, scratch=(), cost=4.0, n_smem=0, n_in=0, n_any=0, name=None):
    smem = [pl.BlockSpec(memory_space=pltpu.SMEM)] * n_smem
    vmem = [pl.BlockSpec(memory_space=pltpu.VMEM)] * n_in + [pl.BlockSpec(memory_space=pl.ANY)] * n_any
    shapes = [jax.ShapeDtypeStruct(s, d) for s, d in outs]
    specs = [pl.BlockSpec(memory_space=pltpu.VMEM)] * len(outs)
    single = len(outs) == 1
    return pl.pallas_call(
        body,
        out_shape=shapes[0] if single else shapes,
        in_specs=smem + vmem,
        out_specs=specs[0] if single else specs,
        scratch_shapes=list(scratch),
        compiler_params=pltpu.CompilerParams(vmem_limit_bytes=16 * 1024 * 1024),
        cost_estimate=pl.CostEstimate(flops=int(cost * 5e8), bytes_accessed=int(cost * 2e6), transcendentals=0),
        name=name,
    )


def prepare_body(core_ref, w_in_ref, w_down_ref, out_ref, w_in, w_down, sems):
    loads = [
        pltpu.make_async_copy(w_in_ref, w_in, sems.at[0]),
        pltpu.make_async_copy(w_down_ref, w_down, sems.at[1]),
    ]
    for load in loads:
        load.start()
    unit, place = iota((PART, LANES), 0), iota((PART, LANES), 1)
    wanted = (place % 16) * 16 + core_ref[0] * 8 + place // 16
    chosen = (unit == wanted).astype(bf16)
    loads[0].wait()
    mine_in = lax.dot_general(chosen, w_in[...], (((0,), (1,)), ((), ())), preferred_element_type=f32).astype(bf16)
    loads[1].wait()
    mine_down = mm_tall(chosen, w_down[...]).astype(bf16)
    for k in range(N_X):
        out_ref[k, 0] = mine_in
        out_ref[k, 1] = mine_down


def attend_body(
    cols_ref, rows_ref, same_ref, keys_ref, values_ref, embed_ref, gain_self_ref, gain_cross_ref, w_query_hbm, w_key_hbm,
    w_value_hbm, w_self_hbm, cross_query_hbm, cross_out_hbm, states_ref, at_rank_ref, done_ref, ctx_ref, held, sems,
):
    sources = (w_query_hbm, w_key_hbm, w_value_hbm, w_self_hbm, cross_query_hbm, cross_out_hbm)
    loads = [pltpu.make_async_copy(source, held.at[k], sems.at[k]) for k, source in enumerate(sources)]
    for load in loads:
        load.start()
    lane = iota((ROWS, LANES), 1)
    hits = cols_ref[:, 2:3] == lane
    earlier = (iota((ROWS, ROWS), 0) > iota((ROWS, ROWS), 1)).astype(bf16)
    before = mm(earlier, hits.astype(bf16))
    rank = jnp.sum(jnp.where(hits, before, 0.0), -1, keepdims=True).astype(jnp.int32)
    at_rank_ref[...] = (rank == lane).astype(f32)
    embed = embed_ref[...]
    names = (iota((32, VOCAB), 0) == iota((32, VOCAB), 1)).astype(bf16)
    table = mm(names, embed).astype(bf16)
    picks = (cols_ref[:, 0:1] == iota((ROWS, 32), 1)).astype(bf16)
    picks_t = (rows_ref[0:1, :] == iota((32, ROWS), 0)).astype(bf16)
    embedded = mm(picks, table)
    for load in loads:
        load.wait()
    query = mm(embedded.astype(bf16), held[0]).astype(bf16)
    keyed = mm(table, held[1])
    valued = mm(table, held[2])
    own = iota((HEADS * 32, WIDTH), 0) // 32 == iota((HEADS * 32, WIDTH), 1) // 64
    key_blocks = jnp.where(own, jnp.concatenate([keyed] * HEADS, 0), 0.0).astype(bf16)
    value_blocks = jnp.where(own, jnp.concatenate([valued] * HEADS, 0), 0.0).astype(bf16)
    scores = (mm_flip(key_blocks, query) * 0.125).reshape(HEADS, 32, ROWS)
    counts = mm(picks_t, same_ref[...])[None]
    scores = jnp.where(counts > 0.0, scores, -1e30)
    probs = jnp.exp(scores - jnp.max(scores, 1, keepdims=True)) * counts
    probs = probs / jnp.sum(probs, 1, keepdims=True)
    context = mm_tall(probs.reshape(HEADS * 32, ROWS).astype(bf16), value_blocks).astype(bf16)
    unit, _ = norm_parts(embedded + mm(context, held[3]))
    attended = (unit * gain_self_ref[...]).astype(bf16)
    cross_q = mm(attended, held[4]).astype(bf16)
    left = iota((PAD, LANES), 1) < 64
    for s in range(2):
        for pair in range(HEADS // 2):
            lanes = slice(pair * LANES, (pair + 1) * LANES)
            q = cross_q[s * PAD : (s + 1) * PAD, lanes]
            k = keys_ref[s, :, lanes]
            v = values_ref[s, :, lanes]
            both = []
            for mine in (left, jnp.logical_not(left)):
                logit = mm_flip(jnp.where(mine, q, jnp.zeros_like(q)), k) * 0.125
                e = jnp.exp(logit - jnp.max(logit, -1, keepdims=True))
                p = (e / jnp.sum(e, -1, keepdims=True)).astype(bf16)
                both.append(mm(p, v))
            ctx_ref[s * PAD : (s + 1) * PAD, lanes] = jnp.where(left, both[0], both[1]).astype(bf16)
    unit, _ = norm_parts(attended.astype(f32) + mm(ctx_ref[...], held[5]))
    states = (unit * gain_cross_ref[...]).astype(bf16)
    states_ref[...] = states
    done_ref[...] = states[:16, :LANES]


def half_forward(states, weights_ref, hidden_ref, slope_ref):
    w_in = jnp.concatenate([weights_ref[m, 0] for m in range(N_X)], 0)
    w_down = jnp.concatenate([weights_ref[m, 1] for m in range(N_X)], 0)
    pre = mm_flip(states, w_in)
    tanh = jnp.tanh(0.7978845608028654 * (pre + 0.044715 * pre * pre * pre))
    hidden = (0.5 * pre * (1.0 + tanh)).astype(bf16)
    hidden_ref[...] = hidden
    slope_ref[...] = 0.5 * (1.0 + tanh) + 0.5 * pre * (1.0 - tanh * tanh) * 0.7978845608028654 * (1.0 + 0.134145 * pre * pre)
    return mm(hidden, w_down)


def own_body(states_ref, weights_ref, done_ref, hidden_ref, slope_ref, total_ref):
    states = states_ref[...]
    total_ref[...] = states.astype(f32) + half_forward(states, weights_ref, hidden_ref, slope_ref)


def forward_body(
    accept_ref, cols_ref, at_rank_ref, beams_ref, states_ref, partial_ref, weights_ref, gain_ref, head_ref,
    message_ref, hidden_ref, slope_ref, unit_ref, signal_ref, scale_ref,
):
    unit, scale = norm_parts(partial_ref[...] + half_forward(states_ref[...], weights_ref, hidden_ref, slope_ref))
    unit_ref[...] = unit
    scale_ref[...] = jnp.broadcast_to(scale, (ROWS, LANES))
    high, low = split(unit * gain_ref[...])
    logits = mm(high, head_ref[...]) + mm(low, head_ref[...])
    lane = iota((ROWS, LANES), 1)
    logits = jnp.where(lane < VOCAB, logits, -1e30)
    top = jnp.max(logits, -1, keepdims=True)
    grown = jnp.exp(logits - top)
    mass = jnp.sum(grown, -1, keepdims=True)
    is_label = cols_ref[:, 1:2] == lane
    taken = jnp.sum(jnp.where(is_label, logits, 0.0), -1, keepdims=True) - top - jnp.log(mass)
    beams = beams_ref[...]
    score = jnp.sum(beams * taken, 0, keepdims=True) / STEPS
    place = iota((1, LANES), 1)
    shares = jnp.zeros((1, LANES), f32)
    for s in range(2):
        inside = (place >= s * BEAM) & (place < (s + 1) * BEAM)
        e = jnp.where(inside, jnp.exp(score - jnp.max(jnp.where(inside, score, -1e30), -1, keepdims=True)), 0.0)
        share = e / jnp.sum(e, -1, keepdims=True) * accept_ref[s].astype(f32)
        shares = jnp.where(inside, share, shares)
    weight = jnp.sum(beams * shares, -1, keepdims=True)
    signal_ref[...] = weight * (grown / mass - is_label.astype(f32))
    hits = cols_ref[:, 2:3] == lane
    sums = jnp.sum(jnp.where(hits, weight, 0.0), 0, keepdims=True)
    high, low = split(at_rank_ref[...] * (-weight * taken))
    hits16 = hits.astype(bf16)
    message_ref[:, 0, :] = jnp.broadcast_to(sums, (N_DP, LANES))
    message_ref[:, 1, :] = mm_tall(hits16, high) + mm_tall(hits16, low)


def backward_body(
    cols_ref, states_ref, hidden_ref, slope_ref, weights_ref, hidden_2_ref, slope_2_ref, weights_2_ref, unit_ref, signal_ref,
    scale_ref, gain_ref, head_ref, keep_ref, send_ref,
):
    unit = unit_ref[...]
    high, low = split(signal_ref[...])
    d_unit = gain_ref[...] * (mm_flip(high, head_ref[...]) + mm_flip(low, head_ref[...]))
    along = jnp.mean(d_unit * unit, -1, keepdims=True)
    d_total = scale_ref[:, 0:1] * (d_unit - jnp.mean(d_unit, -1, keepdims=True) - unit * along)
    d_out = d_total.astype(bf16)
    states = states_ref[...]
    dest = jnp.broadcast_to(cols_ref[:, 2:3], (ROWS, LANES)).astype(f32).astype(bf16)
    for ref, hidden, slope, weights in (
        (send_ref, hidden_2_ref, slope_2_ref, weights_2_ref),
        (keep_ref, hidden_ref, slope_ref, weights_ref),
    ):
        w_down = jnp.concatenate([weights[m, 1] for m in range(N_X)], 0)
        ref[:, 0:WIDTH] = (mm_flip(d_out, w_down) * slope[...]).astype(bf16)
        ref[:, WIDTH : 2 * WIDTH] = hidden[...]
        ref[:, 2 * WIDTH : 3 * WIDTH] = states
        ref[:, 3 * WIDTH : 4 * WIDTH] = d_out
        ref[:, 4 * WIDTH :] = dest


def one_term(ref, got_ref, k):
    sums = jnp.sum(got_ref[:, 0, :], 0, keepdims=True)
    inverse = 1.0 / jnp.maximum(sums, 1.0)
    hits = ref[:, 4 * WIDTH :].astype(f32) == iota((ROWS, LANES), 1).astype(f32)
    factor = jnp.sum(jnp.where(hits, inverse, 0.0), -1, keepdims=True)
    scaled = (ref[:, (k + 2) * WIDTH : (k + 3) * WIDTH].astype(f32) * factor).astype(bf16)
    return mm_tall(ref[:, k * WIDTH : (k + 1) * WIDTH], scaled)


def first_body(keep_ref, got_ref, sum_ref, loss_ref):
    loss_ref[...] = got_ref[:, 1, :]
    for k in range(2):
        sum_ref[:, k * WIDTH : (k + 1) * WIDTH] = one_term(keep_ref, got_ref, k)


def term_body(sum_ref, other_ref, got_ref, term_ref):
    for k in range(2):
        lanes = slice(k * WIDTH, (k + 1) * WIDTH)
        grad = (sum_ref[:, lanes] + one_term(other_ref, got_ref, k)).astype(bf16)
        for m in range(N_X):
            for x in range(N_X):
                start = m * LANES + x * 32
                term_ref[x, m * 32 : (m + 1) * 32, lanes] = grad[start : start + 32]


def middle_body(got_ref, out_ref, held_ref):
    total = got_ref[0].astype(f32)
    for k in range(1, N_X):
        total = total + got_ref[k].astype(f32)
    for m in range(N_X):
        for r in range(2):
            for c in range(8):
                block = total[m * 32 + r * 16 : m * 32 + (r + 1) * 16, c * LANES : (c + 1) * LANES]
                held_ref[m * 16 : (m + 1) * 16, r * 8 + c, :] = block
    out_ref[...] = held_ref[...].astype(bf16)


def final_body(got_ref, momentum_ref, out_ref):
    total = jnp.sum(got_ref[...].astype(f32), 0)
    for r in range(2):
        for c in range(8):
            lanes = slice(c * LANES, (c + 1) * LANES)
            out_ref[r : r + 1, lanes] = 0.9 * momentum_ref[r : r + 1, lanes] + total[r * 8 + c : r * 8 + c + 1]


def constants():
    row = np.arange(ROWS)
    inside = row % PAD
    group = row // PAD * 6 + inside // (STEPS + 1)
    same = (group[:, None] == group[None, :]) & (row[:, None] <= row[None, :])
    valid = (inside < SEG) & (inside % (STEPS + 1) < STEPS)
    beam = np.where(valid, row // PAD * BEAM + inside // (STEPS + 1), -1)
    beams = beam[:, None] == np.arange(LANES)[None, :]
    return jnp.asarray(same, bf16), jnp.asarray(beams, f32)


def per_device(
    tokens, accept, dest, mem_keys, mem_values, embed, w_query, w_key, w_value, w_self, cross_query, cross_out,
    gain_self, gain_cross, w_in, w_down, gain_ff, head, momentum,
):
    same, beams = constants()
    core = lax.axis_index("core").astype(jnp.int32).reshape(1)
    swap = [(0, 1), (1, 0)]
    half = (ROWS, HALF)

    mine = call(
        prepare_body,
        [((N_X, 2, LANES, WIDTH), bf16)],
        scratch=[pltpu.VMEM((WIDTH, PART), bf16), pltpu.VMEM((PART, WIDTH), bf16), pltpu.SemaphoreType.DMA((2,))],
        n_smem=1, n_any=2, cost=1, name="prepare",
    )(core, w_in, w_down)
    own_w = lax.all_to_all(mine, "x", 0, 0)

    flat = jnp.pad(tokens.reshape(2, SEG), ((0, 0), (0, PAD - SEG))).reshape(ROWS)
    nexts = jnp.concatenate([flat[1:], flat[:1]])
    place = jnp.pad(dest.reshape(2, BEAM, STEPS), ((0, 0), (0, 0), (0, 1)), constant_values=-1).reshape(2, SEG)
    place = jnp.pad(place, ((0, 0), (0, PAD - SEG)), constant_values=-1).reshape(ROWS)
    rows = jnp.stack([flat, nexts, place, place, place, place, place, place])
    cols = rows.T
    states, at_rank, done = call(
        attend_body,
        [((ROWS, WIDTH), bf16), ((ROWS, LANES), f32), ((16, LANES), bf16)],
        scratch=[
            pltpu.VMEM((ROWS, WIDTH), bf16),
            pltpu.VMEM((6, WIDTH, WIDTH), bf16),
            pltpu.SemaphoreType.DMA((6,)),
        ],
        n_in=8, n_any=6, cost=8, name="attend",
    )(
        cols, rows, same, mem_keys, mem_values, embed, gain_self.reshape(1, WIDTH), gain_cross.reshape(1, WIDTH),
        w_query, w_key, w_value, w_self, cross_query, cross_out,
    )
    own_w, done = lax.optimization_barrier((own_w, done))
    other_w = lax.ppermute(own_w, "core", swap)
    hidden, slope, partial = call(
        own_body, [(half, bf16), (half, f32), ((ROWS, WIDTH), f32)], n_in=3, cost=2, name="own"
    )(states, own_w, done)
    gain = gain_ff.reshape(1, WIDTH)
    head = jnp.pad(head, ((0, 0), (0, LANES - VOCAB)))
    message, hidden_2, slope_2, unit, signal, scale = call(
        forward_body,
        [
            ((N_DP, 2, LANES), f32),
            (half, bf16),
            (half, f32),
            ((ROWS, WIDTH), f32),
            ((ROWS, LANES), f32),
            ((ROWS, LANES), f32),
        ],
        n_smem=1, n_in=8, cost=5, name="forward",
    )(accept, cols, at_rank, beams, states, partial, other_w, gain, head)
    got = lax.all_to_all(message, DP, 0, 0)
    keep, send = call(
        backward_body, [((ROWS, PAY), bf16), ((ROWS, PAY), bf16)], n_in=13, cost=4, name="backward"
    )(cols, states, hidden, slope, own_w, hidden_2, slope_2, other_w, unit, signal, scale, gain, head)
    other = lax.ppermute(send, "core", swap)
    first, loss = call(
        first_body, [((HALF, 2 * WIDTH), f32), ((N_DP, LANES), f32)], n_in=2, cost=20, name="first"
    )(keep, got)
    term = call(term_body, [((N_X, LANES, 2 * WIDTH), bf16)], n_in=3, cost=4, name="term")(first, other, got)
    got = lax.all_to_all(term, "x", 0, 0)
    middle = call(
        middle_body, [((64, 16, LANES), bf16)], scratch=[pltpu.VMEM((64, 16, LANES), f32)], n_in=1, cost=1, name="middle"
    )(got)
    got = lax.all_to_all(middle, ("z", "y"), 0, 0)
    out = call(final_body, [((2, 2 * WIDTH), f32)], n_in=2, cost=1, name="final")(got, momentum)
    return out, loss[:, :CAP].reshape(1, N_DP * CAP)


def solution(mesh):
    n_dp, n_mp = mesh.devices.shape
    side = int(np.sqrt(n_dp // 2))
    fine = Mesh(mesh.devices.reshape(side, side, 2, n_mp), EVERY)
    placed = (
        P(EVERY, None, None),
        P(EVERY),
        P(EVERY, None),
        P(EVERY, None, None),
        P(EVERY, None, None),
        P(),
        P(),
        P(),
        P(),
        P(),
        P(),
        P(),
        P(),
        P(),
        P(None, "x"),
        P("x", None),
        P(),
        P(),
        P(EVERY, None),
    )
    return jax.shard_map(
        per_device,
        mesh=fine,
        in_specs=placed,
        out_specs=(P(EVERY, None), P(EVERY, None)),
        check_vma=False,
    )
```

```python
import jax
import jax.numpy as jnp
import numpy as np
from jax import lax
from jax.experimental import pallas as pl
from jax.experimental.pallas import tpu as pltpu
from jax.sharding import Mesh
from jax.sharding import PartitionSpec as P

HEADS = 8
BEAM = 5
STEPS = 30
CAP = 5
SEG = BEAM * (STEPS + 1)
PAD = 160
ROWS = 2 * PAD
WIDTH = 512
FF = 1024
VOCAB = 28
PEAKS = 150
LANES = 128
N_DP = 128
N_X = 4
PART = FF // N_X
HALF = FF // 2
PAY = 4 * WIDTH + LANES
f32 = jnp.float32
bf16 = jnp.bfloat16
FLIP = (((1,), (1,)), ((), ()))
TALL = (((0,), (0,)), ((), ()))
DP = ("z", "y", "core")
EVERY = ("z", "y", "core", "x")


def mm(a, b):
    return jnp.dot(a, b, preferred_element_type=f32)


def mm_flip(a, b):
    return lax.dot_general(a, b, FLIP, preferred_element_type=f32)


def mm_tall(a, b):
    return lax.dot_general(a, b, TALL, preferred_element_type=f32)


def iota(shape, dim):
    return lax.broadcasted_iota(jnp.int32, shape, dim)


def norm_parts(values):
    mean = jnp.mean(values, -1, keepdims=True)
    centered = values - mean
    scale = lax.rsqrt(jnp.mean(centered * centered, -1, keepdims=True) + 1e-05)
    return centered * scale, scale


def split(v):
    high = v.astype(bf16)
    return high, (v - high.astype(f32)).astype(bf16)


def call(body, outs, scratch=(), cost=4.0, n_smem=0, n_in=0, n_any=0, out_hbm=False, limit=16 << 20, name=None):
    smem = [pl.BlockSpec(memory_space=pltpu.SMEM)] * n_smem
    vmem = [pl.BlockSpec(memory_space=pltpu.VMEM)] * n_in + [pl.BlockSpec(memory_space=pltpu.HBM)] * n_any
    shapes = [jax.ShapeDtypeStruct(s, d) for s, d in outs]
    specs = [pl.BlockSpec(memory_space=pltpu.HBM if out_hbm else pltpu.VMEM)] * len(outs)
    single = len(outs) == 1
    return pl.pallas_call(
        body,
        out_shape=shapes[0] if single else shapes,
        in_specs=smem + vmem,
        out_specs=specs[0] if single else specs,
        scratch_shapes=list(scratch),
        compiler_params=pltpu.CompilerParams(vmem_limit_bytes=limit),
        cost_estimate=pl.CostEstimate(flops=int(cost * 5e8), bytes_accessed=int(cost * 2e6), transcendentals=0),
        name=name,
    )


def prepare_body(core_ref, w_in_hbm, w_down_hbm, out_hbm, w_in, w_down, mine, sems):
    loads = [
        pltpu.make_async_copy(w_in_hbm, w_in, sems.at[0]),
        pltpu.make_async_copy(w_down_hbm, w_down, sems.at[1]),
    ]
    for load in loads:
        load.start()
    unit, place = iota((PART, LANES), 0), iota((PART, LANES), 1)
    wanted = (place % 16) * 16 + core_ref[0] * 8 + place // 16
    chosen = (unit == wanted).astype(bf16)
    loads[0].wait()
    mine[0] = lax.dot_general(chosen, w_in[...], (((0,), (1,)), ((), ())), preferred_element_type=f32).astype(bf16)
    loads[1].wait()
    mine[1] = mm_tall(chosen, w_down[...]).astype(bf16)
    stores = [pltpu.make_async_copy(mine, out_hbm.at[k], sems.at[2 + k]) for k in range(N_X)]
    for store in stores:
        store.start()
    for store in stores:
        store.wait()


def attend_body(
    cols_ref, rows_ref, keys_ref, values_ref, embed_ref, gain_self_ref, gain_cross_ref, w_query_hbm, w_key_hbm,
    w_value_hbm, w_self_hbm, cross_query_hbm, cross_out_hbm, states_ref, at_rank_ref, done_ref, ctx_ref, held, sems,
):
    sources = (w_query_hbm, w_key_hbm, w_value_hbm, w_self_hbm, cross_query_hbm, cross_out_hbm)
    loads = [pltpu.make_async_copy(source, held.at[k], sems.at[k]) for k, source in enumerate(sources)]
    for load in loads:
        load.start()
    lane = iota((ROWS, LANES), 1)
    hits = cols_ref[:, 2:3] == lane
    earlier = (iota((ROWS, ROWS), 0) > iota((ROWS, ROWS), 1)).astype(bf16)
    before = mm(earlier, hits.astype(bf16))
    same = (beam_of(0) == beam_of(1)) & (iota((ROWS, ROWS), 0) <= iota((ROWS, ROWS), 1))
    same = same.astype(bf16)
    rank = jnp.sum(jnp.where(hits, before, 0.0), -1, keepdims=True).astype(jnp.int32)
    at_rank_ref[...] = (rank == lane).astype(f32)
    embed = embed_ref[...]
    names = (iota((32, VOCAB), 0) == iota((32, VOCAB), 1)).astype(bf16)
    table = mm(names, embed).astype(bf16)
    picks = (cols_ref[:, 0:1] == iota((ROWS, 32), 1)).astype(bf16)
    picks_t = (rows_ref[0:1, :] == iota((32, ROWS), 0)).astype(bf16)
    embedded = mm(picks, table)
    for load in loads:
        load.wait()
    query = mm(embedded.astype(bf16), held[0]).astype(bf16)
    keyed = mm(table, held[1])
    valued = mm(table, held[2])
    own = iota((HEADS * 32, WIDTH), 0) // 32 == iota((HEADS * 32, WIDTH), 1) // 64
    key_blocks = jnp.where(own, jnp.concatenate([keyed] * HEADS, 0), 0.0).astype(bf16)
    value_blocks = jnp.where(own, jnp.concatenate([valued] * HEADS, 0), 0.0).astype(bf16)
    scores = (mm_flip(key_blocks, query) * 0.125).reshape(HEADS, 32, ROWS)
    counts = mm(picks_t, same)[None]
    scores = jnp.where(counts > 0.0, scores, -1e30)
    probs = jnp.exp(scores - jnp.max(scores, 1, keepdims=True)) * counts
    probs = probs / jnp.sum(probs, 1, keepdims=True)
    context = mm_tall(probs.reshape(HEADS * 32, ROWS).astype(bf16), value_blocks).astype(bf16)
    unit, _ = norm_parts(embedded + mm(context, held[3]))
    attended = (unit * gain_self_ref[...]).astype(bf16)
    cross_q = mm(attended, held[4]).astype(bf16)
    left = iota((PAD, LANES), 1) < 64
    for s in range(2):
        for pair in range(HEADS // 2):
            lanes = slice(pair * LANES, (pair + 1) * LANES)
            q = cross_q[s * PAD : (s + 1) * PAD, lanes]
            k = keys_ref[s, :, lanes]
            v = values_ref[s, :, lanes]
            both = []
            for mine in (left, jnp.logical_not(left)):
                logit = mm_flip(jnp.where(mine, q, jnp.zeros_like(q)), k) * 0.125
                e = jnp.exp(logit - jnp.max(logit, -1, keepdims=True))
                p = (e / jnp.sum(e, -1, keepdims=True)).astype(bf16)
                both.append(mm(p, v))
            ctx_ref[s * PAD : (s + 1) * PAD, lanes] = jnp.where(left, both[0], both[1]).astype(bf16)
    unit, _ = norm_parts(attended.astype(f32) + mm(ctx_ref[...], held[5]))
    states = (unit * gain_cross_ref[...]).astype(bf16)
    states_ref[...] = states
    done_ref[...] = states[:16, :LANES]


def beam_of(dim):
    shape = (ROWS, 1) if dim == 0 else (1, ROWS)
    row = iota(shape, dim)
    second = (row >= PAD).astype(jnp.int32)
    inside = row - second * PAD
    beam = second * (BEAM + 1)
    for k in range(1, BEAM + 1):
        beam = beam + (inside >= k * (STEPS + 1)).astype(jnp.int32)
    return beam


def wide_head(head_ref):
    return mm((iota((LANES, VOCAB), 0) == iota((LANES, VOCAB), 1)).astype(bf16), head_ref[...]).astype(bf16)


def half_forward(states, weights_ref, hidden_ref, slope_ref):
    w_in = jnp.concatenate([weights_ref[m, 0] for m in range(N_X)], 0)
    w_down = jnp.concatenate([weights_ref[m, 1] for m in range(N_X)], 0)
    pre = mm_flip(states, w_in)
    tanh = jnp.tanh(0.7978845608028654 * (pre + 0.044715 * pre * pre * pre))
    hidden = (0.5 * pre * (1.0 + tanh)).astype(bf16)
    hidden_ref[...] = hidden
    slope_ref[...] = 0.5 * (1.0 + tanh) + 0.5 * pre * (1.0 - tanh * tanh) * 0.7978845608028654 * (1.0 + 0.134145 * pre * pre)
    return mm(hidden, w_down)


def own_body(states_ref, weights_ref, done_ref, hidden_ref, slope_ref, total_ref):
    states = states_ref[...]
    total_ref[...] = states.astype(f32) + half_forward(states, weights_ref, hidden_ref, slope_ref)


def forward_body(
    accept_ref, cols_ref, at_rank_ref, states_ref, partial_ref, weights_ref, gain_ref, head_ref,
    message_ref, hidden_ref, slope_ref, unit_ref, signal_ref, scale_ref,
):
    unit, scale = norm_parts(partial_ref[...] + half_forward(states_ref[...], weights_ref, hidden_ref, slope_ref))
    unit_ref[...] = unit
    scale_ref[...] = jnp.broadcast_to(scale, (ROWS, LANES))
    high, low = split(unit * gain_ref[...])
    head = wide_head(head_ref)
    logits = mm_flip(high, head) + mm_flip(low, head)
    lane = iota((ROWS, LANES), 1)
    logits = jnp.where(lane < VOCAB, logits, -1e30)
    top = jnp.max(logits, -1, keepdims=True)
    grown = jnp.exp(logits - top)
    mass = jnp.sum(grown, -1, keepdims=True)
    is_label = cols_ref[:, 1:2] == lane
    taken = jnp.sum(jnp.where(is_label, logits, 0.0), -1, keepdims=True) - top - jnp.log(mass)
    beam = beam_of(0)
    row = iota((ROWS, 1), 0)
    step = row - (row >= PAD).astype(jnp.int32) * PAD
    beam = beam - (row >= PAD).astype(jnp.int32)
    for k in range(1, BEAM + 1):
        step = step - (step >= STEPS + 1).astype(jnp.int32) * (STEPS + 1)
    inside = jnp.where(row >= PAD, row - PAD, row)
    beams = jnp.where((beam == lane) & (step < STEPS) & (inside < SEG), 1.0, 0.0)
    score = jnp.sum(beams * taken, 0, keepdims=True) / STEPS
    place = iota((1, LANES), 1)
    shares = jnp.zeros((1, LANES), f32)
    for s in range(2):
        inside = (place >= s * BEAM) & (place < (s + 1) * BEAM)
        e = jnp.where(inside, jnp.exp(score - jnp.max(jnp.where(inside, score, -1e30), -1, keepdims=True)), 0.0)
        share = e / jnp.sum(e, -1, keepdims=True) * accept_ref[s].astype(f32)
        shares = jnp.where(inside, share, shares)
    weight = jnp.sum(beams * shares, -1, keepdims=True)
    signal_ref[...] = weight * (grown / mass - is_label.astype(f32))
    hits = cols_ref[:, 2:3] == lane
    sums = jnp.sum(jnp.where(hits, weight, 0.0), 0, keepdims=True)
    high, low = split(at_rank_ref[...] * (-weight * taken))
    hits16 = hits.astype(bf16)
    message_ref[:, 0, :] = jnp.broadcast_to(sums, (N_DP, LANES))
    message_ref[:, 1, :] = mm_tall(hits16, high) + mm_tall(hits16, low)


def backward_body(
    cols_ref, states_ref, hidden_ref, slope_ref, weights_ref, hidden_2_ref, slope_2_ref, weights_2_ref, unit_ref, signal_ref,
    scale_ref, gain_ref, head_ref, keep_ref, send_ref,
):
    unit = unit_ref[...]
    high, low = split(signal_ref[...])
    head = wide_head(head_ref)
    d_unit = gain_ref[...] * (mm(high, head) + mm(low, head))
    along = jnp.mean(d_unit * unit, -1, keepdims=True)
    d_total = scale_ref[:, 0:1] * (d_unit - jnp.mean(d_unit, -1, keepdims=True) - unit * along)
    d_out = d_total.astype(bf16)
    states = states_ref[...]
    dest = jnp.broadcast_to(cols_ref[:, 2:3], (ROWS, LANES)).astype(f32).astype(bf16)
    for ref, hidden, slope, weights in (
        (send_ref, hidden_2_ref, slope_2_ref, weights_2_ref),
        (keep_ref, hidden_ref, slope_ref, weights_ref),
    ):
        w_down = jnp.concatenate([weights[m, 1] for m in range(N_X)], 0)
        ref[:, 0:WIDTH] = (mm_flip(d_out, w_down) * slope[...]).astype(bf16)
        ref[:, WIDTH : 2 * WIDTH] = hidden[...]
        ref[:, 2 * WIDTH : 3 * WIDTH] = states
        ref[:, 3 * WIDTH : 4 * WIDTH] = d_out
        ref[:, 4 * WIDTH :] = dest


def one_term(ref, got_ref, k):
    sums = jnp.sum(got_ref[:, 0, :], 0, keepdims=True)
    inverse = 1.0 / jnp.maximum(sums, 1.0)
    hits = ref[:, 4 * WIDTH :].astype(f32) == iota((ROWS, LANES), 1).astype(f32)
    factor = jnp.sum(jnp.where(hits, inverse, 0.0), -1, keepdims=True)
    scaled = (ref[:, (k + 2) * WIDTH : (k + 3) * WIDTH].astype(f32) * factor).astype(bf16)
    return mm_tall(ref[:, k * WIDTH : (k + 1) * WIDTH], scaled)


def first_body(keep_ref, got_ref, sum_ref, loss_ref):
    loss_ref[...] = got_ref[:, 1, :]
    for k in range(2):
        sum_ref[:, k * WIDTH : (k + 1) * WIDTH] = one_term(keep_ref, got_ref, k)


def term_body(sum_ref, other_ref, got_ref, term_ref):
    for k in range(2):
        lanes = slice(k * WIDTH, (k + 1) * WIDTH)
        grad = (sum_ref[:, lanes] + one_term(other_ref, got_ref, k)).astype(bf16)
        for m in range(N_X):
            for x in range(N_X):
                start = m * LANES + x * 32
                term_ref[x, m * 32 : (m + 1) * 32, lanes] = grad[start : start + 32]


def middle_body(got_ref, out_ref, held_ref):
    total = got_ref[0].astype(f32)
    for k in range(1, N_X):
        total = total + got_ref[k].astype(f32)
    for m in range(N_X):
        for r in range(2):
            for c in range(8):
                block = total[m * 32 + r * 16 : m * 32 + (r + 1) * 16, c * LANES : (c + 1) * LANES]
                held_ref[m * 16 : (m + 1) * 16, r * 8 + c, :] = block
    out_ref[...] = held_ref[...].astype(bf16)


def final_body(got_ref, momentum_ref, out_ref):
    total = jnp.sum(got_ref[...].astype(f32), 0)
    for r in range(2):
        for c in range(8):
            lanes = slice(c * LANES, (c + 1) * LANES)
            out_ref[r : r + 1, lanes] = 0.9 * momentum_ref[r : r + 1, lanes] + total[r * 8 + c : r * 8 + c + 1]


def per_device(
    tokens, accept, dest, mem_keys, mem_values, embed, w_query, w_key, w_value, w_self, cross_query, cross_out,
    gain_self, gain_cross, w_in, w_down, gain_ff, head, momentum,
):
    core = lax.axis_index("core").astype(jnp.int32).reshape(1)
    swap = [(0, 1), (1, 0)]
    half = (ROWS, HALF)

    mine = call(
        prepare_body,
        [((N_X, 2, LANES, WIDTH), bf16)],
        scratch=[
            pltpu.VMEM((WIDTH, PART), bf16),
            pltpu.VMEM((PART, WIDTH), bf16),
            pltpu.VMEM((2, LANES, WIDTH), bf16),
            pltpu.SemaphoreType.DMA((2 + N_X,)),
        ],
        n_smem=1, n_any=2, out_hbm=True, limit=63_300_000, cost=1, name="prepare",
    )(core, w_in, w_down)
    own_w = lax.all_to_all(mine, "x", 0, 0)

    flat = tokens.reshape(2, SEG)
    nexts = lax.pad(flat, jnp.int32(0), ((0, 0, 0), (-1, PAD - SEG + 1, 0))).reshape(ROWS)
    flat = jnp.pad(flat, ((0, 0), (0, PAD - SEG))).reshape(ROWS)
    place = jnp.pad(dest.reshape(2, BEAM, STEPS), ((0, 0), (0, 0), (0, 1)), constant_values=-1).reshape(2, SEG)
    place = jnp.pad(place, ((0, 0), (0, PAD - SEG)), constant_values=-1).reshape(ROWS)
    rows = jnp.stack([flat, nexts, place, place, place, place, place, place])
    cols = rows.T
    states, at_rank, done = call(
        attend_body,
        [((ROWS, WIDTH), bf16), ((ROWS, LANES), f32), ((16, LANES), bf16)],
        scratch=[
            pltpu.VMEM((ROWS, WIDTH), bf16),
            pltpu.VMEM((6, WIDTH, WIDTH), bf16),
            pltpu.SemaphoreType.DMA((6,)),
        ],
        n_in=7, n_any=6, limit=61_300_000, cost=8, name="attend",
    )(
        cols, rows, mem_keys, mem_values, embed, gain_self.reshape(1, WIDTH), gain_cross.reshape(1, WIDTH),
        w_query, w_key, w_value, w_self, cross_query, cross_out,
    )
    own_w, done = lax.optimization_barrier((own_w, done))
    other_w = lax.ppermute(own_w, "core", swap)
    hidden, slope, partial = call(
        own_body, [(half, bf16), (half, f32), ((ROWS, WIDTH), f32)], n_in=3, cost=2, name="own"
    )(states, own_w, done)
    gain = gain_ff.reshape(1, WIDTH)
    head = head.T
    message, hidden_2, slope_2, unit, signal, scale = call(
        forward_body,
        [
            ((N_DP, 2, LANES), f32),
            (half, bf16),
            (half, f32),
            ((ROWS, WIDTH), f32),
            ((ROWS, LANES), f32),
            ((ROWS, LANES), f32),
        ],
        n_smem=1, n_in=7, cost=5, name="forward",
    )(accept, cols, at_rank, states, partial, other_w, gain, head)
    got = lax.all_to_all(message, DP, 0, 0)
    keep, send = call(
        backward_body, [((ROWS, PAY), bf16), ((ROWS, PAY), bf16)], n_in=13, cost=4, name="backward"
    )(cols, states, hidden, slope, own_w, hidden_2, slope_2, other_w, unit, signal, scale, gain, head)
    other = lax.ppermute(send, "core", swap)
    first, loss = call(
        first_body, [((HALF, 2 * WIDTH), f32), ((N_DP, LANES), f32)], n_in=2, cost=20, name="first"
    )(keep, got)
    term = call(term_body, [((N_X, LANES, 2 * WIDTH), bf16)], n_in=3, cost=4, name="term")(first, other, got)
    got = lax.all_to_all(term, "x", 0, 0)
    middle = call(
        middle_body, [((64, 16, LANES), bf16)], scratch=[pltpu.VMEM((64, 16, LANES), f32)], n_in=1, cost=1, name="middle"
    )(got)
    got = lax.all_to_all(middle, ("z", "y"), 0, 0)
    out = call(final_body, [((2, 2 * WIDTH), f32)], n_in=2, cost=1, name="final")(got, momentum)
    return out, loss[:, :CAP].reshape(1, N_DP * CAP)


def solution(mesh):
    n_dp, n_mp = mesh.devices.shape
    side = int(np.sqrt(n_dp // 2))
    fine = Mesh(mesh.devices.reshape(side, side, 2, n_mp), EVERY)
    placed = (
        P(EVERY, None, None),
        P(EVERY),
        P(EVERY, None),
        P(EVERY, None, None),
        P(EVERY, None, None),
        P(),
        P(),
        P(),
        P(),
        P(),
        P(),
        P(),
        P(),
        P(),
        P(None, "x"),
        P("x", None),
        P(),
        P(),
        P(EVERY, None),
    )
    return jax.shard_map(
        per_device,
        mesh=fine,
        in_specs=placed,
        out_specs=(P(EVERY, None), P(EVERY, None)),
        check_vma=False,
    )
```

```python
import jax
import jax.numpy as jnp
import numpy as np
from jax import lax
from jax.experimental import pallas as pl
from jax.experimental.pallas import tpu as pltpu
from jax.sharding import Mesh
from jax.sharding import PartitionSpec as P

HEADS = 8
BEAM = 5
STEPS = 30
CAP = 5
SEG = BEAM * (STEPS + 1)
PAD = 160
ROWS = 2 * PAD
WIDTH = 512
FF = 1024
VOCAB = 28
PEAKS = 150
LANES = 128
N_DP = 128
N_X = 4
PART = FF // N_X
HALF = FF // 2
PAY = 4 * WIDTH + LANES
f32 = jnp.float32
bf16 = jnp.bfloat16
FLIP = (((1,), (1,)), ((), ()))
TALL = (((0,), (0,)), ((), ()))
DP = ("z", "y", "core")
EVERY = ("z", "y", "core", "x")


def mm(a, b):
    return jnp.dot(a, b, preferred_element_type=f32)


def mm_flip(a, b):
    return lax.dot_general(a, b, FLIP, preferred_element_type=f32)


def mm_tall(a, b):
    return lax.dot_general(a, b, TALL, preferred_element_type=f32)


def iota(shape, dim):
    return lax.broadcasted_iota(jnp.int32, shape, dim)


def norm_parts(values):
    mean = jnp.mean(values, -1, keepdims=True)
    centered = values - mean
    scale = lax.rsqrt(jnp.mean(centered * centered, -1, keepdims=True) + 1e-05)
    return centered * scale, scale


def split(v):
    high = v.astype(bf16)
    return high, (v - high.astype(f32)).astype(bf16)


def call(body, outs, scratch=(), cost=4.0, n_smem=0, n_in=0, n_hbm=0, limit=16 << 20, name=None):
    smem = [pl.BlockSpec(memory_space=pltpu.SMEM)] * n_smem
    vmem = [pl.BlockSpec(memory_space=pltpu.VMEM)] * n_in
    hbm = [pl.BlockSpec(memory_space=pltpu.HBM)] * n_hbm
    shapes = [jax.ShapeDtypeStruct(out[0], out[1]) for out in outs]
    specs = [pl.BlockSpec(memory_space=pltpu.HBM if len(out) > 2 else pltpu.VMEM) for out in outs]
    single = len(outs) == 1
    return pl.pallas_call(
        body,
        out_shape=shapes[0] if single else shapes,
        in_specs=smem + vmem + hbm,
        out_specs=specs[0] if single else specs,
        scratch_shapes=list(scratch),
        compiler_params=pltpu.CompilerParams(vmem_limit_bytes=limit),
        cost_estimate=pl.CostEstimate(flops=int(cost * 5e8), bytes_accessed=int(cost * 2e6), transcendentals=0),
        name=name,
    )


def start(sems, first, *pairs):
    copies = [pltpu.make_async_copy(src, dst, sems.at[first + k]) for k, (src, dst) in enumerate(pairs)]
    for copy in copies:
        copy.start()
    return copies


def finish(copies):
    for copy in copies:
        copy.wait()


def prepare_body(core_ref, w_in_hbm, w_down_hbm, out_hbm, w_in, w_down, mine, sems):
    loads = start(sems, 0, (w_in_hbm, w_in), (w_down_hbm, w_down))
    unit, place = iota((PART, LANES), 0), iota((PART, LANES), 1)
    wanted = (place % 16) * 16 + core_ref[0] * 8 + place // 16
    chosen = (unit == wanted).astype(bf16)
    loads[0].wait()
    mine[0] = lax.dot_general(chosen, w_in[...], (((0,), (1,)), ((), ())), preferred_element_type=f32).astype(bf16)
    stores = start(sems, 2, *[(mine.at[0], out_hbm.at[k, 0]) for k in range(N_X)])
    loads[1].wait()
    mine[1] = mm_tall(chosen, w_down[...]).astype(bf16)
    stores += start(sems, 2 + N_X, *[(mine.at[1], out_hbm.at[k, 1]) for k in range(N_X)])
    finish(stores)


def attend_body(
    cols_ref, rows_ref, keys_ref, values_ref, embed_ref, gain_self_ref, gain_cross_ref, w_query_hbm, w_key_hbm,
    w_value_hbm, w_self_hbm, cross_query_hbm, cross_out_hbm, states_ref, at_rank_ref, done_ref, ctx_ref, held, sems,
):
    sources = (w_query_hbm, w_key_hbm, w_value_hbm, w_self_hbm, cross_query_hbm, cross_out_hbm)
    loads = start(sems, 0, *[(source, held.at[k]) for k, source in enumerate(sources)])
    lane = iota((ROWS, LANES), 1)
    hits = cols_ref[:, 2:3] == lane
    earlier = (iota((ROWS, ROWS), 0) > iota((ROWS, ROWS), 1)).astype(bf16)
    before = mm(earlier, hits.astype(bf16))
    same = (beam_of(0) == beam_of(1)) & (iota((ROWS, ROWS), 0) <= iota((ROWS, ROWS), 1))
    same = same.astype(bf16)
    rank = jnp.sum(jnp.where(hits, before, 0.0), -1, keepdims=True).astype(jnp.int32)
    at_rank_ref[...] = (rank == lane).astype(f32)
    embed = embed_ref[...]
    names = (iota((32, VOCAB), 0) == iota((32, VOCAB), 1)).astype(bf16)
    table = mm(names, embed).astype(bf16)
    picks = (cols_ref[:, 0:1] == iota((ROWS, 32), 1)).astype(bf16)
    picks_t = (rows_ref[0:1, :] == iota((32, ROWS), 0)).astype(bf16)
    embedded = mm(picks, table)
    finish(loads)
    query = mm(embedded.astype(bf16), held[0]).astype(bf16)
    keyed = mm(table, held[1])
    valued = mm(table, held[2])
    own = iota((HEADS * 32, WIDTH), 0) // 32 == iota((HEADS * 32, WIDTH), 1) // 64
    key_blocks = jnp.where(own, jnp.concatenate([keyed] * HEADS, 0), 0.0).astype(bf16)
    value_blocks = jnp.where(own, jnp.concatenate([valued] * HEADS, 0), 0.0).astype(bf16)
    scores = (mm_flip(key_blocks, query) * 0.125).reshape(HEADS, 32, ROWS)
    counts = mm(picks_t, same)[None]
    scores = jnp.where(counts > 0.0, scores, -1e30)
    probs = jnp.exp(scores - jnp.max(scores, 1, keepdims=True)) * counts
    probs = probs / jnp.sum(probs, 1, keepdims=True)
    context = mm_tall(probs.reshape(HEADS * 32, ROWS).astype(bf16), value_blocks).astype(bf16)
    unit, _ = norm_parts(embedded + mm(context, held[3]))
    attended = (unit * gain_self_ref[...]).astype(bf16)
    cross_q = mm(attended, held[4]).astype(bf16)
    left = iota((PAD, LANES), 1) < 64
    for s in range(2):
        for pair in range(HEADS // 2):
            lanes = slice(pair * LANES, (pair + 1) * LANES)
            q = cross_q[s * PAD : (s + 1) * PAD, lanes]
            k = keys_ref[s, :, lanes]
            v = values_ref[s, :, lanes]
            both = []
            for mine in (left, jnp.logical_not(left)):
                logit = mm_flip(jnp.where(mine, q, jnp.zeros_like(q)), k) * 0.125
                e = jnp.exp(logit - jnp.max(logit, -1, keepdims=True))
                p = (e / jnp.sum(e, -1, keepdims=True)).astype(bf16)
                both.append(mm(p, v))
            ctx_ref[s * PAD : (s + 1) * PAD, lanes] = jnp.where(left, both[0], both[1]).astype(bf16)
    unit, _ = norm_parts(attended.astype(f32) + mm(ctx_ref[...], held[5]))
    states = (unit * gain_cross_ref[...]).astype(bf16)
    states_ref[...] = states
    done_ref[...] = states[:16, :LANES]


def beam_of(dim):
    shape = (ROWS, 1) if dim == 0 else (1, ROWS)
    row = iota(shape, dim)
    second = (row >= PAD).astype(jnp.int32)
    inside = row - second * PAD
    beam = second * (BEAM + 1)
    for k in range(1, BEAM + 1):
        beam = beam + (inside >= k * (STEPS + 1)).astype(jnp.int32)
    return beam


def wide_head(head_ref):
    return mm((iota((LANES, VOCAB), 0) == iota((LANES, VOCAB), 1)).astype(bf16), head_ref[...]).astype(bf16)


def half_forward(states, weights_ref):
    w_in = jnp.concatenate([weights_ref[m, 0] for m in range(N_X)], 0)
    w_down = jnp.concatenate([weights_ref[m, 1] for m in range(N_X)], 0)
    pre = mm_flip(states, w_in)
    tanh = jnp.tanh(0.7978845608028654 * (pre + 0.044715 * pre * pre * pre))
    hidden = (0.5 * pre * (1.0 + tanh)).astype(bf16)
    return pre, tanh, hidden, w_down, mm(hidden, w_down)


def scores_of(total, gain, head, labels, accept_ref):
    unit, scale = norm_parts(total)
    high, low = split(unit * gain)
    logits = mm_flip(high, head) + mm_flip(low, head)
    lane = iota((ROWS, LANES), 1)
    logits = jnp.where(lane < VOCAB, logits, -1e30)
    top = jnp.max(logits, -1, keepdims=True)
    grown = jnp.exp(logits - top)
    mass = jnp.sum(grown, -1, keepdims=True)
    is_label = labels == lane
    taken = jnp.sum(jnp.where(is_label, logits, 0.0), -1, keepdims=True) - top - jnp.log(mass)
    beam = beam_of(0)
    row = iota((ROWS, 1), 0)
    step = row - (row >= PAD).astype(jnp.int32) * PAD
    beam = beam - (row >= PAD).astype(jnp.int32)
    for k in range(1, BEAM + 1):
        step = step - (step >= STEPS + 1).astype(jnp.int32) * (STEPS + 1)
    inside = jnp.where(row >= PAD, row - PAD, row)
    beams = jnp.where((beam == lane) & (step < STEPS) & (inside < SEG), 1.0, 0.0)
    score = jnp.sum(beams * taken, 0, keepdims=True) / STEPS
    place = iota((1, LANES), 1)
    shares = jnp.zeros((1, LANES), f32)
    for s in range(2):
        inside = (place >= s * BEAM) & (place < (s + 1) * BEAM)
        e = jnp.where(inside, jnp.exp(score - jnp.max(jnp.where(inside, score, -1e30), -1, keepdims=True)), 0.0)
        share = e / jnp.sum(e, -1, keepdims=True) * accept_ref[s].astype(f32)
        shares = jnp.where(inside, share, shares)
    weight = jnp.sum(beams * shares, -1, keepdims=True)
    return unit, scale, taken, weight, grown, mass, is_label


def own_body(states_ref, weights_ref, done_ref, total_ref):
    states = states_ref[...]
    total_ref[...] = states.astype(f32) + half_forward(states, weights_ref)[4]


def forward_body(
    accept_ref, cols_ref, at_rank_ref, states_ref, partial_ref, weights_ref, gain_ref, head_ref, message_ref
):
    total = partial_ref[...] + half_forward(states_ref[...], weights_ref)[4]
    out = scores_of(total, gain_ref[...], wide_head(head_ref), cols_ref[:, 1:2], accept_ref)
    taken, weight = out[2], out[3]
    hits = cols_ref[:, 2:3] == iota((ROWS, LANES), 1)
    sums = jnp.sum(jnp.where(hits, weight, 0.0), 0, keepdims=True)
    high, low = split(at_rank_ref[...] * (-weight * taken))
    hits16 = hits.astype(bf16)
    message_ref[:, 0, :] = jnp.broadcast_to(sums, (N_DP, LANES))
    message_ref[:, 1, :] = mm_tall(hits16, high) + mm_tall(hits16, low)


def backward_body(
    accept_ref, cols_ref, states_ref, own_ref, other_ref, gain_ref, head_ref, keep_ref, send_ref, slopes, downs,
):
    states = states_ref[...]
    total = states.astype(f32)
    hidden_at = slice(WIDTH, 2 * WIDTH)
    for k, weights_ref, ref in ((0, own_ref, keep_ref), (1, other_ref, send_ref)):
        pre, tanh, hidden, w_down, more = half_forward(states, weights_ref)
        slope = 0.5 * (1.0 + tanh) + 0.5 * pre * (1.0 - tanh * tanh) * 0.7978845608028654 * (1.0 + 0.134145 * pre * pre)
        slopes[k] = slope
        downs[k] = w_down
        ref[:, hidden_at] = hidden
        total = total + more
    head, gain = wide_head(head_ref), gain_ref[...]
    unit, scale, _, weight, grown, mass, is_label = scores_of(total, gain, head, cols_ref[:, 1:2], accept_ref)
    high, low = split(weight * (grown / mass - is_label.astype(f32)))
    d_unit = gain * (mm(high, head) + mm(low, head))
    along = jnp.mean(d_unit * unit, -1, keepdims=True)
    d_out = (scale * (d_unit - jnp.mean(d_unit, -1, keepdims=True) - unit * along)).astype(bf16)
    dest = jnp.broadcast_to(cols_ref[:, 2:3], (ROWS, LANES)).astype(f32).astype(bf16)
    for k, ref in ((0, keep_ref), (1, send_ref)):
        ref[:, 0:WIDTH] = (mm_flip(d_out, downs[k]) * slopes[k]).astype(bf16)
        ref[:, 2 * WIDTH : 3 * WIDTH] = states
        ref[:, 3 * WIDTH : 4 * WIDTH] = d_out
        ref[:, 4 * WIDTH :] = dest


def one_term(ref, got_ref, k):
    sums = jnp.sum(got_ref[:, 0, :], 0, keepdims=True)
    inverse = 1.0 / jnp.maximum(sums, 1.0)
    hits = ref[:, 4 * WIDTH :].astype(f32) == iota((ROWS, LANES), 1).astype(f32)
    factor = jnp.sum(jnp.where(hits, inverse, 0.0), -1, keepdims=True)
    scaled = (ref[:, (k + 2) * WIDTH : (k + 3) * WIDTH].astype(f32) * factor).astype(bf16)
    return mm_tall(ref[:, k * WIDTH : (k + 1) * WIDTH], scaled)


def first_body(keep_ref, got_ref, sum_ref, loss_ref):
    loss_ref[...] = got_ref[:, 1, :]
    for k in range(2):
        sum_ref[:, k * WIDTH : (k + 1) * WIDTH] = one_term(keep_ref, got_ref, k)


def term_body(sum_ref, other_ref, got_ref, term_ref):
    for k in range(2):
        lanes = slice(k * WIDTH, (k + 1) * WIDTH)
        grad = (sum_ref[:, lanes] + one_term(other_ref, got_ref, k)).astype(bf16)
        for m in range(N_X):
            for x in range(N_X):
                start = m * LANES + x * 32
                term_ref[x, m * 32 : (m + 1) * 32, lanes] = grad[start : start + 32]


def middle_body(got_ref, out_ref, held_ref):
    total = got_ref[0].astype(f32)
    for k in range(1, N_X):
        total = total + got_ref[k].astype(f32)
    for m in range(N_X):
        for r in range(2):
            for c in range(8):
                block = total[m * 32 + r * 16 : m * 32 + (r + 1) * 16, c * LANES : (c + 1) * LANES]
                held_ref[m * 16 : (m + 1) * 16, r * 8 + c, :] = block
    out_ref[...] = held_ref[...].astype(bf16)


def final_body(got_ref, momentum_ref, out_ref):
    total = jnp.sum(got_ref[...].astype(f32), 0)
    for r in range(2):
        for c in range(8):
            lanes = slice(c * LANES, (c + 1) * LANES)
            out_ref[r : r + 1, lanes] = 0.9 * momentum_ref[r : r + 1, lanes] + total[r * 8 + c : r * 8 + c + 1]


def per_device(
    tokens, accept, dest, mem_keys, mem_values, embed, w_query, w_key, w_value, w_self, cross_query, cross_out,
    gain_self, gain_cross, w_in, w_down, gain_ff, head, momentum,
):
    core = lax.axis_index("core").astype(jnp.int32).reshape(1)
    swap = [(0, 1), (1, 0)]
    half = (ROWS, HALF)

    mine = call(
        prepare_body,
        [((N_X, 2, LANES, WIDTH), bf16, 1)],
        scratch=[
            pltpu.VMEM((WIDTH, PART), bf16),
            pltpu.VMEM((PART, WIDTH), bf16),
            pltpu.VMEM((2, LANES, WIDTH), bf16),
            pltpu.SemaphoreType.DMA((2 + 2 * N_X,)),
        ],
        n_smem=1, n_hbm=2, limit=63_300_000, cost=1, name="prepare",
    )(core, w_in, w_down)
    own_w = lax.all_to_all(mine, "x", 0, 0)

    flat = tokens.reshape(2, SEG)
    nexts = lax.pad(flat, jnp.int32(0), ((0, 0, 0), (-1, PAD - SEG + 1, 0))).reshape(ROWS)
    flat = jnp.pad(flat, ((0, 0), (0, PAD - SEG))).reshape(ROWS)
    place = jnp.pad(dest.reshape(2, BEAM, STEPS), ((0, 0), (0, 0), (0, 1)), constant_values=-1).reshape(2, SEG)
    place = jnp.pad(place, ((0, 0), (0, PAD - SEG)), constant_values=-1).reshape(ROWS)
    rows = jnp.stack([flat, nexts, place, place, place, place, place, place])
    cols = rows.T
    states, at_rank, done = call(
        attend_body,
        [((ROWS, WIDTH), bf16), ((ROWS, LANES), f32), ((16, LANES), bf16)],
        scratch=[
            pltpu.VMEM((ROWS, WIDTH), bf16),
            pltpu.VMEM((6, WIDTH, WIDTH), bf16),
            pltpu.SemaphoreType.DMA((6,)),
        ],
        n_in=7, n_hbm=6, limit=61_300_000, cost=8, name="attend",
    )(
        cols, rows, mem_keys, mem_values, embed, gain_self.reshape(1, WIDTH), gain_cross.reshape(1, WIDTH),
        w_query, w_key, w_value, w_self, cross_query, cross_out,
    )
    own_w, done = lax.optimization_barrier((own_w, done))
    other_w = lax.ppermute(own_w, "core", swap)
    partial = call(own_body, [((ROWS, WIDTH), f32)], n_in=3, cost=2, name="own")(states, own_w, done)
    gain = gain_ff.reshape(1, WIDTH)
    head = head.T
    message = call(forward_body, [((N_DP, 2, LANES), f32)], n_smem=1, n_in=7, cost=5, name="forward")(
        accept, cols, at_rank, states, partial, other_w, gain, head
    )
    got = lax.all_to_all(message, DP, 0, 0)
    keep, send = call(
        backward_body,
        [((ROWS, PAY), bf16), ((ROWS, PAY), bf16)],
        scratch=[pltpu.VMEM((2,) + half, f32), pltpu.VMEM((2, HALF, WIDTH), bf16)],
        n_smem=1, n_in=6, limit=61_300_000, cost=4, name="backward",
    )(accept, cols, states, own_w, other_w, gain, head)
    other = lax.ppermute(send, "core", swap)
    first, loss = call(
        first_body, [((HALF, 2 * WIDTH), f32), ((N_DP, LANES), f32)], n_in=2, cost=40, name="first"
    )(keep, got)
    term = call(term_body, [((N_X, LANES, 2 * WIDTH), bf16)], n_in=3, cost=4, name="term")(first, other, got)
    got = lax.all_to_all(term, "x", 0, 0)
    middle = call(
        middle_body, [((64, 16, LANES), bf16)], scratch=[pltpu.VMEM((64, 16, LANES), f32)], n_in=1, cost=1, name="middle"
    )(got)
    got = lax.all_to_all(middle, ("z", "y"), 0, 0)
    out = call(final_body, [((2, 2 * WIDTH), f32)], n_in=2, cost=1, name="final")(got, momentum)
    return out, loss[:, :CAP].reshape(1, N_DP * CAP)


def solution(mesh):
    n_dp, n_mp = mesh.devices.shape
    side = int(np.sqrt(n_dp // 2))
    fine = Mesh(mesh.devices.reshape(side, side, 2, n_mp), EVERY)
    placed = (
        P(EVERY, None, None),
        P(EVERY),
        P(EVERY, None),
        P(EVERY, None, None),
        P(EVERY, None, None),
        P(),
        P(),
        P(),
        P(),
        P(),
        P(),
        P(),
        P(),
        P(),
        P(None, "x"),
        P("x", None),
        P(),
        P(),
        P(EVERY, None),
    )
    return jax.shard_map(
        per_device,
        mesh=fine,
        in_specs=placed,
        out_specs=(P(EVERY, None), P(EVERY, None)),
        check_vma=False,
    )
```

```python
import jax
import jax.numpy as jnp
import numpy as np
from jax import lax
from jax.experimental import pallas as pl
from jax.experimental.pallas import tpu as pltpu
from jax.sharding import Mesh
from jax.sharding import PartitionSpec as P

HEADS = 8
BEAM = 5
STEPS = 30
CAP = 5
SEG = BEAM * (STEPS + 1)
PAD = 160
ROWS = 2 * PAD
WIDTH = 512
FF = 1024
VOCAB = 28
PEAKS = 150
LANES = 128
N_DP = 128
N_X = 4
PART = FF // N_X
HALF = FF // 2
PAY = 4 * WIDTH + LANES
f32 = jnp.float32
bf16 = jnp.bfloat16
FLIP = (((1,), (1,)), ((), ()))
TALL = (((0,), (0,)), ((), ()))
DP = ("z", "y", "core")
EVERY = ("z", "y", "core", "x")


def mm(a, b):
    return jnp.dot(a, b, preferred_element_type=f32)


def mm_flip(a, b):
    return lax.dot_general(a, b, FLIP, preferred_element_type=f32)


def mm_tall(a, b):
    return lax.dot_general(a, b, TALL, preferred_element_type=f32)


def iota(shape, dim):
    return lax.broadcasted_iota(jnp.int32, shape, dim)


def norm_parts(values):
    mean = jnp.mean(values, -1, keepdims=True)
    centered = values - mean
    scale = lax.rsqrt(jnp.mean(centered * centered, -1, keepdims=True) + 1e-05)
    return centered * scale, scale


def split(v):
    high = v.astype(bf16)
    return high, (v - high.astype(f32)).astype(bf16)


def call(body, outs, scratch=(), cost=4.0, n_smem=0, n_in=0, n_any=0, out_hbm=False, limit=16 << 20, name=None):
    smem = [pl.BlockSpec(memory_space=pltpu.SMEM)] * n_smem
    vmem = [pl.BlockSpec(memory_space=pltpu.VMEM)] * n_in + [pl.BlockSpec(memory_space=pltpu.HBM)] * n_any
    shapes = [jax.ShapeDtypeStruct(s, d) for s, d in outs]
    specs = [pl.BlockSpec(memory_space=pltpu.HBM if out_hbm else pltpu.VMEM)] * len(outs)
    single = len(outs) == 1
    return pl.pallas_call(
        body,
        out_shape=shapes[0] if single else shapes,
        in_specs=smem + vmem,
        out_specs=specs[0] if single else specs,
        scratch_shapes=list(scratch),
        compiler_params=pltpu.CompilerParams(vmem_limit_bytes=limit),
        cost_estimate=pl.CostEstimate(flops=int(cost * 5e8), bytes_accessed=int(cost * 2e6), transcendentals=0),
        name=name,
    )


def start(sems, first, *pairs):
    copies = [pltpu.make_async_copy(src, dst, sems.at[first + k]) for k, (src, dst) in enumerate(pairs)]
    for copy in copies:
        copy.start()
    return copies


def finish(copies):
    for copy in copies:
        copy.wait()


def prepare_body(core_ref, w_in_hbm, w_down_hbm, out_hbm, w_in, w_down, mine, sems):
    loads = start(sems, 0, (w_in_hbm, w_in), (w_down_hbm, w_down))
    unit, place = iota((PART, LANES), 0), iota((PART, LANES), 1)
    wanted = (place % 16) * 16 + core_ref[0] * 8 + place // 16
    chosen = (unit == wanted).astype(bf16)
    loads[0].wait()
    mine[0] = lax.dot_general(chosen, w_in[...], (((0,), (1,)), ((), ())), preferred_element_type=f32).astype(bf16)
    stores = start(sems, 2, *[(mine.at[0], out_hbm.at[k, 0]) for k in range(N_X)])
    loads[1].wait()
    mine[1] = mm_tall(chosen, w_down[...]).astype(bf16)
    stores += start(sems, 2 + N_X, *[(mine.at[1], out_hbm.at[k, 1]) for k in range(N_X)])
    finish(stores)


def attend_body(
    cols_ref, rows_ref, keys_ref, values_ref, embed_ref, gain_self_ref, gain_cross_ref, w_query_hbm, w_key_hbm,
    w_value_hbm, w_self_hbm, cross_query_hbm, cross_out_hbm, states_ref, at_rank_ref, done_ref, ctx_ref, held, sems,
):
    sources = (w_query_hbm, w_key_hbm, w_value_hbm, w_self_hbm, cross_query_hbm, cross_out_hbm)
    loads = [pltpu.make_async_copy(source, held.at[k], sems.at[k]) for k, source in enumerate(sources)]
    for load in loads:
        load.start()
    lane = iota((ROWS, LANES), 1)
    hits = cols_ref[:, 2:3] == lane
    earlier = (iota((ROWS, ROWS), 0) > iota((ROWS, ROWS), 1)).astype(bf16)
    before = mm(earlier, hits.astype(bf16))
    same = (beam_of(0) == beam_of(1)) & (iota((ROWS, ROWS), 0) <= iota((ROWS, ROWS), 1))
    same = same.astype(bf16)
    rank = jnp.sum(jnp.where(hits, before, 0.0), -1, keepdims=True).astype(jnp.int32)
    at_rank_ref[...] = (rank == lane).astype(f32)
    embed = embed_ref[...]
    names = (iota((32, VOCAB), 0) == iota((32, VOCAB), 1)).astype(bf16)
    table = mm(names, embed).astype(bf16)
    picks = (cols_ref[:, 0:1] == iota((ROWS, 32), 1)).astype(bf16)
    picks_t = (rows_ref[0:1, :] == iota((32, ROWS), 0)).astype(bf16)
    embedded = mm(picks, table)
    for load in loads:
        load.wait()
    query = mm(embedded.astype(bf16), held[0]).astype(bf16)
    keyed = mm(table, held[1])
    valued = mm(table, held[2])
    own = iota((HEADS * 32, WIDTH), 0) // 32 == iota((HEADS * 32, WIDTH), 1) // 64
    key_blocks = jnp.where(own, jnp.concatenate([keyed] * HEADS, 0), 0.0).astype(bf16)
    value_blocks = jnp.where(own, jnp.concatenate([valued] * HEADS, 0), 0.0).astype(bf16)
    scores = (mm_flip(key_blocks, query) * 0.125).reshape(HEADS, 32, ROWS)
    counts = mm(picks_t, same)[None]
    scores = jnp.where(counts > 0.0, scores, -1e30)
    probs = jnp.exp(scores - jnp.max(scores, 1, keepdims=True)) * counts
    probs = probs / jnp.sum(probs, 1, keepdims=True)
    context = mm_tall(probs.reshape(HEADS * 32, ROWS).astype(bf16), value_blocks).astype(bf16)
    unit, _ = norm_parts(embedded + mm(context, held[3]))
    attended = (unit * gain_self_ref[...]).astype(bf16)
    cross_q = mm(attended, held[4]).astype(bf16)
    left = iota((PAD, LANES), 1) < 64
    for s in range(2):
        for pair in range(HEADS // 2):
            lanes = slice(pair * LANES, (pair + 1) * LANES)
            q = cross_q[s * PAD : (s + 1) * PAD, lanes]
            k = keys_ref[s, :, lanes]
            v = values_ref[s, :, lanes]
            both = []
            for mine in (left, jnp.logical_not(left)):
                logit = mm_flip(jnp.where(mine, q, jnp.zeros_like(q)), k) * 0.125
                e = jnp.exp(logit - jnp.max(logit, -1, keepdims=True))
                p = (e / jnp.sum(e, -1, keepdims=True)).astype(bf16)
                both.append(mm(p, v))
            ctx_ref[s * PAD : (s + 1) * PAD, lanes] = jnp.where(left, both[0], both[1]).astype(bf16)
    unit, _ = norm_parts(attended.astype(f32) + mm(ctx_ref[...], held[5]))
    states = (unit * gain_cross_ref[...]).astype(bf16)
    states_ref[...] = states
    done_ref[...] = states[:16, :LANES]


def beam_of(dim):
    shape = (ROWS, 1) if dim == 0 else (1, ROWS)
    row = iota(shape, dim)
    second = (row >= PAD).astype(jnp.int32)
    inside = row - second * PAD
    beam = second * (BEAM + 1)
    for k in range(1, BEAM + 1):
        beam = beam + (inside >= k * (STEPS + 1)).astype(jnp.int32)
    return beam


def wide_head(head_ref):
    return mm((iota((LANES, VOCAB), 0) == iota((LANES, VOCAB), 1)).astype(bf16), head_ref[...]).astype(bf16)


def half_forward(states, weights_ref, hidden_ref, slope_ref):
    w_in = jnp.concatenate([weights_ref[m, 0] for m in range(N_X)], 0)
    w_down = jnp.concatenate([weights_ref[m, 1] for m in range(N_X)], 0)
    pre = mm_flip(states, w_in)
    tanh = jnp.tanh(0.7978845608028654 * (pre + 0.044715 * pre * pre * pre))
    hidden = (0.5 * pre * (1.0 + tanh)).astype(bf16)
    hidden_ref[...] = hidden
    slope_ref[...] = 0.5 * (1.0 + tanh) + 0.5 * pre * (1.0 - tanh * tanh) * 0.7978845608028654 * (1.0 + 0.134145 * pre * pre)
    return mm(hidden, w_down)


def own_body(states_ref, weights_ref, done_ref, hidden_ref, slope_ref, total_ref):
    states = states_ref[...]
    total_ref[...] = states.astype(f32) + half_forward(states, weights_ref, hidden_ref, slope_ref)


def train_body(
    accept_ref, cols_ref, at_rank_ref, states_ref, partial_ref, hidden_1_ref, slope_1_ref, own_ref, other_ref, gain_ref, head_ref,
    message_ref, keep_ref, send_ref, hidden_ref, slope_ref, unit_ref,
):
    states = states_ref[...]
    total = partial_ref[...] + half_forward(states, other_ref, hidden_ref, slope_ref)
    unit, scale = norm_parts(total)
    unit_ref[...] = unit
    gain = gain_ref[...]
    high, low = split(unit * gain)
    head = wide_head(head_ref)
    logits = mm_flip(high, head) + mm_flip(low, head)
    lane = iota((ROWS, LANES), 1)
    logits = jnp.where(lane < VOCAB, logits, -1e30)
    top = jnp.max(logits, -1, keepdims=True)
    grown = jnp.exp(logits - top)
    mass = jnp.sum(grown, -1, keepdims=True)
    is_label = cols_ref[:, 1:2] == lane
    taken = jnp.sum(jnp.where(is_label, logits, 0.0), -1, keepdims=True) - top - jnp.log(mass)
    beam = beam_of(0)
    row = iota((ROWS, 1), 0)
    step = row - (row >= PAD).astype(jnp.int32) * PAD
    beam = beam - (row >= PAD).astype(jnp.int32)
    for k in range(1, BEAM + 1):
        step = step - (step >= STEPS + 1).astype(jnp.int32) * (STEPS + 1)
    inside = jnp.where(row >= PAD, row - PAD, row)
    beams = jnp.where((beam == lane) & (step < STEPS) & (inside < SEG), 1.0, 0.0)
    score = jnp.sum(beams * taken, 0, keepdims=True) / STEPS
    place = iota((1, LANES), 1)
    shares = jnp.zeros((1, LANES), f32)
    for s in range(2):
        inside = (place >= s * BEAM) & (place < (s + 1) * BEAM)
        e = jnp.where(inside, jnp.exp(score - jnp.max(jnp.where(inside, score, -1e30), -1, keepdims=True)), 0.0)
        share = e / jnp.sum(e, -1, keepdims=True) * accept_ref[s].astype(f32)
        shares = jnp.where(inside, share, shares)
    weight = jnp.sum(beams * shares, -1, keepdims=True)
    hits = cols_ref[:, 2:3] == lane
    sums = jnp.sum(jnp.where(hits, weight, 0.0), 0, keepdims=True)
    high, low = split(at_rank_ref[...] * (-weight * taken))
    hits16 = hits.astype(bf16)
    message_ref[:, 0, :] = jnp.broadcast_to(sums, (N_DP, LANES))
    message_ref[:, 1, :] = mm_tall(hits16, high) + mm_tall(hits16, low)

    high, low = split(weight * (grown / mass - is_label.astype(f32)))
    unit = unit_ref[...]
    d_unit = gain * (mm(high, head) + mm(low, head))
    along = jnp.mean(d_unit * unit, -1, keepdims=True)
    d_total = scale * (d_unit - jnp.mean(d_unit, -1, keepdims=True) - unit * along)
    d_out = d_total.astype(bf16)
    dest = jnp.broadcast_to(cols_ref[:, 2:3], (ROWS, LANES)).astype(f32).astype(bf16)
    for ref, hidden, slope, weights in (
        (send_ref, hidden_ref, slope_ref, other_ref),
        (keep_ref, hidden_1_ref, slope_1_ref, own_ref),
    ):
        w_down = jnp.concatenate([weights[m, 1] for m in range(N_X)], 0)
        ref[:, 0:WIDTH] = (mm_flip(d_out, w_down) * slope[...]).astype(bf16)
        ref[:, WIDTH : 2 * WIDTH] = hidden[...]
        ref[:, 2 * WIDTH : 3 * WIDTH] = states
        ref[:, 3 * WIDTH : 4 * WIDTH] = d_out
        ref[:, 4 * WIDTH :] = dest


def term_body(keep_ref, other_ref, got_ref, term_ref, loss_ref, all_ref):
    sums = jnp.sum(got_ref[:, 0, :], 0, keepdims=True)
    loss_ref[...] = got_ref[:, 1, :]
    inverse = 1.0 / jnp.maximum(sums, 1.0)
    lane = iota((ROWS, LANES), 1).astype(f32)
    for place, ref in ((0, keep_ref), (1, other_ref)):
        rows = slice(place * ROWS, (place + 1) * ROWS)
        hits = ref[:, 4 * WIDTH :].astype(f32) == lane
        factor = jnp.sum(jnp.where(hits, inverse, 0.0), -1, keepdims=True)
        all_ref[rows, : 2 * WIDTH] = ref[:, : 2 * WIDTH]
        all_ref[rows, 2 * WIDTH :] = (ref[:, 2 * WIDTH : 4 * WIDTH].astype(f32) * factor).astype(bf16)
    for k in range(2):
        grad = mm_tall(all_ref[:, k * WIDTH : (k + 1) * WIDTH], all_ref[:, (k + 2) * WIDTH : (k + 3) * WIDTH])
        grad = grad.astype(bf16)
        for m in range(N_X):
            for x in range(N_X):
                start = m * LANES + x * 32
                term_ref[x, m * 32 : (m + 1) * 32, k * WIDTH : (k + 1) * WIDTH] = grad[start : start + 32]


def middle_body(got_ref, out_ref, held_ref):
    total = got_ref[0].astype(f32)
    for k in range(1, N_X):
        total = total + got_ref[k].astype(f32)
    for m in range(N_X):
        for r in range(2):
            for c in range(8):
                block = total[m * 32 + r * 16 : m * 32 + (r + 1) * 16, c * LANES : (c + 1) * LANES]
                held_ref[m * 16 : (m + 1) * 16, r * 8 + c, :] = block
    out_ref[...] = held_ref[...].astype(bf16)


def final_body(got_ref, momentum_ref, out_ref):
    total = jnp.sum(got_ref[...].astype(f32), 0)
    for r in range(2):
        for c in range(8):
            lanes = slice(c * LANES, (c + 1) * LANES)
            out_ref[r : r + 1, lanes] = 0.9 * momentum_ref[r : r + 1, lanes] + total[r * 8 + c : r * 8 + c + 1]


def per_device(
    tokens, accept, dest, mem_keys, mem_values, embed, w_query, w_key, w_value, w_self, cross_query, cross_out,
    gain_self, gain_cross, w_in, w_down, gain_ff, head, momentum,
):
    core = lax.axis_index("core").astype(jnp.int32).reshape(1)
    swap = [(0, 1), (1, 0)]
    half = (ROWS, HALF)

    mine = call(
        prepare_body,
        [((N_X, 2, LANES, WIDTH), bf16)],
        scratch=[
            pltpu.VMEM((WIDTH, PART), bf16),
            pltpu.VMEM((PART, WIDTH), bf16),
            pltpu.VMEM((2, LANES, WIDTH), bf16),
            pltpu.SemaphoreType.DMA((2 + 2 * N_X,)),
        ],
        n_smem=1, n_any=2, out_hbm=True, limit=63_300_000, cost=1, name="prepare",
    )(core, w_in, w_down)
    own_w = lax.all_to_all(mine, "x", 0, 0)

    flat = tokens.reshape(2, SEG)
    nexts = lax.pad(flat, jnp.int32(0), ((0, 0, 0), (-1, PAD - SEG + 1, 0))).reshape(ROWS)
    flat = jnp.pad(flat, ((0, 0), (0, PAD - SEG))).reshape(ROWS)
    place = jnp.pad(dest.reshape(2, BEAM, STEPS), ((0, 0), (0, 0), (0, 1)), constant_values=-1).reshape(2, SEG)
    place = jnp.pad(place, ((0, 0), (0, PAD - SEG)), constant_values=-1).reshape(ROWS)
    rows = jnp.stack([flat, nexts, place, place, place, place, place, place])
    cols = rows.T
    states, at_rank, done = call(
        attend_body,
        [((ROWS, WIDTH), bf16), ((ROWS, LANES), f32), ((16, LANES), bf16)],
        scratch=[
            pltpu.VMEM((ROWS, WIDTH), bf16),
            pltpu.VMEM((6, WIDTH, WIDTH), bf16),
            pltpu.SemaphoreType.DMA((6,)),
        ],
        n_in=7, n_any=6, limit=61_300_000, cost=8, name="attend",
    )(
        cols, rows, mem_keys, mem_values, embed, gain_self.reshape(1, WIDTH), gain_cross.reshape(1, WIDTH),
        w_query, w_key, w_value, w_self, cross_query, cross_out,
    )
    own_w, done = lax.optimization_barrier((own_w, done))
    other_w = lax.ppermute(own_w, "core", swap)
    hidden, slope, partial = call(
        own_body, [(half, bf16), (half, f32), ((ROWS, WIDTH), f32)], n_in=3, cost=2, name="own"
    )(states, own_w, done)
    gain = gain_ff.reshape(1, WIDTH)
    head = head.T
    message, keep, send = call(
        train_body,
        [((N_DP, 2, LANES), f32), ((ROWS, PAY), bf16), ((ROWS, PAY), bf16)],
        scratch=[pltpu.VMEM(half, bf16), pltpu.VMEM(half, f32), pltpu.VMEM((ROWS, WIDTH), f32)],
        n_smem=1, n_in=10, cost=5, name="train",
    )(accept, cols, at_rank, states, partial, hidden, slope, own_w, other_w, gain, head)
    got = lax.all_to_all(message, DP, 0, 0)
    other = lax.ppermute(send, "core", swap)
    term, loss = call(
        term_body,
        [((N_X, LANES, 2 * WIDTH), bf16), ((N_DP, LANES), f32)],
        scratch=[pltpu.VMEM((2 * ROWS, 4 * WIDTH), bf16)],
        n_in=3, cost=4, name="term",
    )(keep, other, got)
    got = lax.all_to_all(term, "x", 0, 0)
    middle = call(
        middle_body, [((64, 16, LANES), bf16)], scratch=[pltpu.VMEM((64, 16, LANES), f32)], n_in=1, cost=1, name="middle"
    )(got)
    got = lax.all_to_all(middle, ("z", "y"), 0, 0)
    out = call(final_body, [((2, 2 * WIDTH), f32)], n_in=2, cost=1, name="final")(got, momentum)
    return out, loss[:, :CAP].reshape(1, N_DP * CAP)


def solution(mesh):
    n_dp, n_mp = mesh.devices.shape
    side = int(np.sqrt(n_dp // 2))
    fine = Mesh(mesh.devices.reshape(side, side, 2, n_mp), EVERY)
    placed = (
        P(EVERY, None, None),
        P(EVERY),
        P(EVERY, None),
        P(EVERY, None, None),
        P(EVERY, None, None),
        P(),
        P(),
        P(),
        P(),
        P(),
        P(),
        P(),
        P(),
        P(),
        P(None, "x"),
        P("x", None),
        P(),
        P(),
        P(EVERY, None),
    )
    return jax.shard_map(
        per_device,
        mesh=fine,
        in_specs=placed,
        out_specs=(P(EVERY, None), P(EVERY, None)),
        check_vma=False,
    )
```

```python
import jax
import jax.numpy as jnp
import numpy as np
from jax import lax
from jax.experimental import pallas as pl
from jax.experimental.pallas import tpu as pltpu
from jax.sharding import Mesh
from jax.sharding import PartitionSpec as P

HEADS = 8
BEAM = 5
STEPS = 30
CAP = 5
SEG = BEAM * (STEPS + 1)
PAD = 160
ROWS = 2 * PAD
WIDTH = 512
FF = 1024
VOCAB = 28
PEAKS = 150
LANES = 128
N_DP = 128
N_X = 4
PART = FF // N_X
HALF = FF // 2
PAY = 4 * WIDTH + LANES
f32 = jnp.float32
bf16 = jnp.bfloat16
FLIP = (((1,), (1,)), ((), ()))
TALL = (((0,), (0,)), ((), ()))
DP = ("z", "y", "core")
EVERY = ("z", "y", "core", "x")
SIDE = 8


def index(z, y, core, x):
    return ((z * SIDE + y) * 2 + core) * N_X + x


def stages():
    side, half, pair, ring = range(SIDE), range(SIDE // 2), range(2), range(N_X)
    one = [[index(z, y, 0, x) for x in ring] for z in side for y in side]
    two = [[index(z, y, 0, x) for z in side for y in side] for x in ring]
    for a in half:
        for b in half:
            for x in ring:
                one.append([index(2 * a + z, 2 * b + y, 1, x) for z in pair for y in pair])
    for z in pair:
        for y in pair:
            two.append([index(2 * a + z, 2 * b + y, 1, x) for a in half for b in half for x in ring])
    return one, two


STAGE_1, STAGE_2 = stages()


def mm(a, b):
    return jnp.dot(a, b, preferred_element_type=f32)


def mm_flip(a, b):
    return lax.dot_general(a, b, FLIP, preferred_element_type=f32)


def mm_tall(a, b):
    return lax.dot_general(a, b, TALL, preferred_element_type=f32)


def iota(shape, dim):
    return lax.broadcasted_iota(jnp.int32, shape, dim)


def norm_parts(values):
    mean = jnp.mean(values, -1, keepdims=True)
    centered = values - mean
    scale = lax.rsqrt(jnp.mean(centered * centered, -1, keepdims=True) + 1e-05)
    return centered * scale, scale


def split(v):
    high = v.astype(bf16)
    return high, (v - high.astype(f32)).astype(bf16)


def call(body, outs, scratch=(), cost=4.0, n_smem=0, n_in=0, n_any=0, out_hbm=False, limit=16 << 20, name=None):
    smem = [pl.BlockSpec(memory_space=pltpu.SMEM)] * n_smem
    vmem = [pl.BlockSpec(memory_space=pltpu.VMEM)] * n_in + [pl.BlockSpec(memory_space=pltpu.HBM)] * n_any
    shapes = [jax.ShapeDtypeStruct(s, d) for s, d in outs]
    specs = [pl.BlockSpec(memory_space=pltpu.HBM if out_hbm else pltpu.VMEM)] * len(outs)
    single = len(outs) == 1
    return pl.pallas_call(
        body,
        out_shape=shapes[0] if single else shapes,
        in_specs=smem + vmem,
        out_specs=specs[0] if single else specs,
        scratch_shapes=list(scratch),
        compiler_params=pltpu.CompilerParams(vmem_limit_bytes=limit),
        cost_estimate=pl.CostEstimate(flops=int(cost * 5e8), bytes_accessed=int(cost * 2e6), transcendentals=0),
        name=name,
    )


def start(sems, first, *pairs):
    copies = [pltpu.make_async_copy(src, dst, sems.at[first + k]) for k, (src, dst) in enumerate(pairs)]
    for copy in copies:
        copy.start()
    return copies


def finish(copies):
    for copy in copies:
        copy.wait()


def prepare_body(core_ref, w_in_hbm, w_down_hbm, out_hbm, w_in, w_down, mine, sems):
    loads = start(sems, 0, (w_in_hbm, w_in), (w_down_hbm, w_down))
    unit, place = iota((PART, LANES), 0), iota((PART, LANES), 1)
    block, row, rest = place // 32, place // 16 % 2, place % 16
    first = rest * 16 + block * 2 + row
    second = (block // 2 * 8 + rest // 4 * 2 + block % 2) * 16 + 8 + rest % 4 * 2 + row
    wanted = jnp.where(core_ref[0] == 0, first, second)
    chosen = (unit == wanted).astype(bf16)
    loads[0].wait()
    mine[0] = lax.dot_general(chosen, w_in[...], (((0,), (1,)), ((), ())), preferred_element_type=f32).astype(bf16)
    stores = start(sems, 2, *[(mine.at[0], out_hbm.at[k, 0]) for k in range(N_X)])
    loads[1].wait()
    mine[1] = mm_tall(chosen, w_down[...]).astype(bf16)
    stores += start(sems, 2 + N_X, *[(mine.at[1], out_hbm.at[k, 1]) for k in range(N_X)])
    finish(stores)


def attend_body(
    cols_ref, rows_ref, keys_ref, values_ref, embed_ref, gain_self_ref, gain_cross_ref, w_query_hbm, w_key_hbm,
    w_value_hbm, w_self_hbm, cross_query_hbm, cross_out_hbm, states_ref, at_rank_ref, done_ref, ctx_ref, held, sems,
):
    sources = (w_query_hbm, w_key_hbm, w_value_hbm, w_self_hbm, cross_query_hbm, cross_out_hbm)
    loads = [pltpu.make_async_copy(source, held.at[k], sems.at[k]) for k, source in enumerate(sources)]
    for load in loads:
        load.start()
    lane = iota((ROWS, LANES), 1)
    hits = cols_ref[:, 2:3] == lane
    earlier = (iota((ROWS, ROWS), 0) > iota((ROWS, ROWS), 1)).astype(bf16)
    before = mm(earlier, hits.astype(bf16))
    same = (beam_of(0) == beam_of(1)) & (iota((ROWS, ROWS), 0) <= iota((ROWS, ROWS), 1))
    same = same.astype(bf16)
    rank = jnp.sum(jnp.where(hits, before, 0.0), -1, keepdims=True).astype(jnp.int32)
    at_rank_ref[...] = (rank == lane).astype(f32)
    embed = embed_ref[...]
    names = (iota((32, VOCAB), 0) == iota((32, VOCAB), 1)).astype(bf16)
    table = mm(names, embed).astype(bf16)
    picks = (cols_ref[:, 0:1] == iota((ROWS, 32), 1)).astype(bf16)
    picks_t = (rows_ref[0:1, :] == iota((32, ROWS), 0)).astype(bf16)
    embedded = mm(picks, table)
    for load in loads:
        load.wait()
    query = mm(embedded.astype(bf16), held[0]).astype(bf16)
    keyed = mm(table, held[1])
    valued = mm(table, held[2])
    own = iota((HEADS * 32, WIDTH), 0) // 32 == iota((HEADS * 32, WIDTH), 1) // 64
    key_blocks = jnp.where(own, jnp.concatenate([keyed] * HEADS, 0), 0.0).astype(bf16)
    value_blocks = jnp.where(own, jnp.concatenate([valued] * HEADS, 0), 0.0).astype(bf16)
    scores = (mm_flip(key_blocks, query) * 0.125).reshape(HEADS, 32, ROWS)
    counts = mm(picks_t, same)[None]
    scores = jnp.where(counts > 0.0, scores, -1e30)
    probs = jnp.exp(scores - jnp.max(scores, 1, keepdims=True)) * counts
    probs = probs / jnp.sum(probs, 1, keepdims=True)
    context = mm_tall(probs.reshape(HEADS * 32, ROWS).astype(bf16), value_blocks).astype(bf16)
    unit, _ = norm_parts(embedded + mm(context, held[3]))
    attended = (unit * gain_self_ref[...]).astype(bf16)
    cross_q = mm(attended, held[4]).astype(bf16)
    left = iota((PAD, LANES), 1) < 64
    for s in range(2):
        for pair in range(HEADS // 2):
            lanes = slice(pair * LANES, (pair + 1) * LANES)
            q = cross_q[s * PAD : (s + 1) * PAD, lanes]
            k = keys_ref[s, :, lanes]
            v = values_ref[s, :, lanes]
            both = []
            for mine in (left, jnp.logical_not(left)):
                logit = mm_flip(jnp.where(mine, q, jnp.zeros_like(q)), k) * 0.125
                e = jnp.exp(logit - jnp.max(logit, -1, keepdims=True))
                p = (e / jnp.sum(e, -1, keepdims=True)).astype(bf16)
                both.append(mm(p, v))
            ctx_ref[s * PAD : (s + 1) * PAD, lanes] = jnp.where(left, both[0], both[1]).astype(bf16)
    unit, _ = norm_parts(attended.astype(f32) + mm(ctx_ref[...], held[5]))
    states = (unit * gain_cross_ref[...]).astype(bf16)
    states_ref[...] = states
    done_ref[...] = states[:16, :LANES]


def beam_of(dim):
    shape = (ROWS, 1) if dim == 0 else (1, ROWS)
    row = iota(shape, dim)
    second = (row >= PAD).astype(jnp.int32)
    inside = row - second * PAD
    beam = second * (BEAM + 1)
    for k in range(1, BEAM + 1):
        beam = beam + (inside >= k * (STEPS + 1)).astype(jnp.int32)
    return beam


def wide_head(head_ref):
    return mm((iota((LANES, VOCAB), 0) == iota((LANES, VOCAB), 1)).astype(bf16), head_ref[...]).astype(bf16)


def half_forward(states, weights_ref, hidden_ref, slope_ref):
    w_in = jnp.concatenate([weights_ref[m, 0] for m in range(N_X)], 0)
    w_down = jnp.concatenate([weights_ref[m, 1] for m in range(N_X)], 0)
    pre = mm_flip(states, w_in)
    tanh = jnp.tanh(0.7978845608028654 * (pre + 0.044715 * pre * pre * pre))
    hidden = (0.5 * pre * (1.0 + tanh)).astype(bf16)
    hidden_ref[...] = hidden
    slope_ref[...] = 0.5 * (1.0 + tanh) + 0.5 * pre * (1.0 - tanh * tanh) * 0.7978845608028654 * (1.0 + 0.134145 * pre * pre)
    return mm(hidden, w_down)


def own_body(states_ref, weights_ref, done_ref, hidden_ref, slope_ref, total_ref):
    states = states_ref[...]
    total_ref[...] = states.astype(f32) + half_forward(states, weights_ref, hidden_ref, slope_ref)


def train_body(
    accept_ref, cols_ref, at_rank_ref, states_ref, partial_ref, hidden_1_ref, slope_1_ref, own_ref, other_ref, gain_ref, head_ref,
    message_ref, keep_ref, send_ref, hidden_ref, slope_ref, unit_ref,
):
    states = states_ref[...]
    total = partial_ref[...] + half_forward(states, other_ref, hidden_ref, slope_ref)
    unit, scale = norm_parts(total)
    unit_ref[...] = unit
    gain = gain_ref[...]
    high, low = split(unit * gain)
    head = wide_head(head_ref)
    logits = mm_flip(high, head) + mm_flip(low, head)
    lane = iota((ROWS, LANES), 1)
    logits = jnp.where(lane < VOCAB, logits, -1e30)
    top = jnp.max(logits, -1, keepdims=True)
    grown = jnp.exp(logits - top)
    mass = jnp.sum(grown, -1, keepdims=True)
    is_label = cols_ref[:, 1:2] == lane
    taken = jnp.sum(jnp.where(is_label, logits, 0.0), -1, keepdims=True) - top - jnp.log(mass)
    beam = beam_of(0)
    row = iota((ROWS, 1), 0)
    step = row - (row >= PAD).astype(jnp.int32) * PAD
    beam = beam - (row >= PAD).astype(jnp.int32)
    for k in range(1, BEAM + 1):
        step = step - (step >= STEPS + 1).astype(jnp.int32) * (STEPS + 1)
    inside = jnp.where(row >= PAD, row - PAD, row)
    beams = jnp.where((beam == lane) & (step < STEPS) & (inside < SEG), 1.0, 0.0)
    score = jnp.sum(beams * taken, 0, keepdims=True) / STEPS
    place = iota((1, LANES), 1)
    shares = jnp.zeros((1, LANES), f32)
    for s in range(2):
        inside = (place >= s * BEAM) & (place < (s + 1) * BEAM)
        e = jnp.where(inside, jnp.exp(score - jnp.max(jnp.where(inside, score, -1e30), -1, keepdims=True)), 0.0)
        share = e / jnp.sum(e, -1, keepdims=True) * accept_ref[s].astype(f32)
        shares = jnp.where(inside, share, shares)
    weight = jnp.sum(beams * shares, -1, keepdims=True)
    hits = cols_ref[:, 2:3] == lane
    sums = jnp.sum(jnp.where(hits, weight, 0.0), 0, keepdims=True)
    high, low = split(at_rank_ref[...] * (-weight * taken))
    hits16 = hits.astype(bf16)
    message_ref[:, 0, :] = jnp.broadcast_to(sums, (N_DP, LANES))
    message_ref[:, 1, :] = mm_tall(hits16, high) + mm_tall(hits16, low)

    high, low = split(weight * (grown / mass - is_label.astype(f32)))
    unit = unit_ref[...]
    d_unit = gain * (mm(high, head) + mm(low, head))
    along = jnp.mean(d_unit * unit, -1, keepdims=True)
    d_total = scale * (d_unit - jnp.mean(d_unit, -1, keepdims=True) - unit * along)
    d_out = d_total.astype(bf16)
    dest = jnp.broadcast_to(cols_ref[:, 2:3], (ROWS, LANES)).astype(f32).astype(bf16)
    for ref, hidden, slope, weights in (
        (send_ref, hidden_ref, slope_ref, other_ref),
        (keep_ref, hidden_1_ref, slope_1_ref, own_ref),
    ):
        w_down = jnp.concatenate([weights[m, 1] for m in range(N_X)], 0)
        ref[:, 0:WIDTH] = (mm_flip(d_out, w_down) * slope[...]).astype(bf16)
        ref[:, WIDTH : 2 * WIDTH] = hidden[...]
        ref[:, 2 * WIDTH : 3 * WIDTH] = states
        ref[:, 3 * WIDTH : 4 * WIDTH] = d_out
        ref[:, 4 * WIDTH :] = dest


def term_body(keep_ref, other_ref, got_ref, term_ref, loss_ref, all_ref):
    sums = jnp.sum(got_ref[:, 0, :], 0, keepdims=True)
    loss_ref[...] = got_ref[:, 1, :]
    inverse = 1.0 / jnp.maximum(sums, 1.0)
    lane = iota((ROWS, LANES), 1).astype(f32)
    for place, ref in ((0, keep_ref), (1, other_ref)):
        rows = slice(place * ROWS, (place + 1) * ROWS)
        hits = ref[:, 4 * WIDTH :].astype(f32) == lane
        factor = jnp.sum(jnp.where(hits, inverse, 0.0), -1, keepdims=True)
        all_ref[rows, : 2 * WIDTH] = ref[:, : 2 * WIDTH]
        all_ref[rows, 2 * WIDTH :] = (ref[:, 2 * WIDTH : 4 * WIDTH].astype(f32) * factor).astype(bf16)
    for k in range(2):
        grad = mm_tall(all_ref[:, k * WIDTH : (k + 1) * WIDTH], all_ref[:, (k + 2) * WIDTH : (k + 3) * WIDTH])
        grad = grad.astype(bf16)
        for m in range(N_X):
            for x in range(N_X):
                start = m * LANES + x * 32
                term_ref[x, m * 32 : (m + 1) * 32, k * WIDTH : (k + 1) * WIDTH] = grad[start : start + 32]


def middle_body(got_ref, out_ref, held_ref):
    total = got_ref[0].astype(f32)
    for k in range(1, N_X):
        total = total + got_ref[k].astype(f32)
    for m in range(N_X):
        for r in range(2):
            for c in range(8):
                block = total[m * 32 + r * 16 : m * 32 + (r + 1) * 16, c * LANES : (c + 1) * LANES]
                held_ref[m * 16 : (m + 1) * 16, r * 8 + c, :] = block
    out_ref[...] = held_ref[...].astype(bf16)


def final_body(got_ref, momentum_ref, out_ref):
    total = jnp.sum(got_ref[...].astype(f32), 0)
    for r in range(2):
        for c in range(8):
            lanes = slice(c * LANES, (c + 1) * LANES)
            out_ref[r : r + 1, lanes] = 0.9 * momentum_ref[r : r + 1, lanes] + total[r * 8 + c : r * 8 + c + 1]


def per_device(
    tokens, accept, dest, mem_keys, mem_values, embed, w_query, w_key, w_value, w_self, cross_query, cross_out,
    gain_self, gain_cross, w_in, w_down, gain_ff, head, momentum,
):
    core = lax.axis_index("core").astype(jnp.int32).reshape(1)
    swap = [(0, 1), (1, 0)]
    half = (ROWS, HALF)

    mine = call(
        prepare_body,
        [((N_X, 2, LANES, WIDTH), bf16)],
        scratch=[
            pltpu.VMEM((WIDTH, PART), bf16),
            pltpu.VMEM((PART, WIDTH), bf16),
            pltpu.VMEM((2, LANES, WIDTH), bf16),
            pltpu.SemaphoreType.DMA((2 + 2 * N_X,)),
        ],
        n_smem=1, n_any=2, out_hbm=True, limit=63_300_000, cost=1, name="prepare",
    )(core, w_in, w_down)
    own_w = lax.all_to_all(mine, "x", 0, 0)

    flat = tokens.reshape(2, SEG)
    nexts = lax.pad(flat, jnp.int32(0), ((0, 0, 0), (-1, PAD - SEG + 1, 0))).reshape(ROWS)
    flat = jnp.pad(flat, ((0, 0), (0, PAD - SEG))).reshape(ROWS)
    place = jnp.pad(dest.reshape(2, BEAM, STEPS), ((0, 0), (0, 0), (0, 1)), constant_values=-1).reshape(2, SEG)
    place = jnp.pad(place, ((0, 0), (0, PAD - SEG)), constant_values=-1).reshape(ROWS)
    rows = jnp.stack([flat, nexts, place, place, place, place, place, place])
    cols = rows.T
    states, at_rank, done = call(
        attend_body,
        [((ROWS, WIDTH), bf16), ((ROWS, LANES), f32), ((16, LANES), bf16)],
        scratch=[
            pltpu.VMEM((ROWS, WIDTH), bf16),
            pltpu.VMEM((6, WIDTH, WIDTH), bf16),
            pltpu.SemaphoreType.DMA((6,)),
        ],
        n_in=7, n_any=6, limit=61_300_000, cost=8, name="attend",
    )(
        cols, rows, mem_keys, mem_values, embed, gain_self.reshape(1, WIDTH), gain_cross.reshape(1, WIDTH),
        w_query, w_key, w_value, w_self, cross_query, cross_out,
    )
    own_w, done = lax.optimization_barrier((own_w, done))
    other_w = lax.ppermute(own_w, "core", swap)
    hidden, slope, partial = call(
        own_body, [(half, bf16), (half, f32), ((ROWS, WIDTH), f32)], n_in=3, cost=2, name="own"
    )(states, own_w, done)
    gain = gain_ff.reshape(1, WIDTH)
    head = head.T
    message, keep, send = call(
        train_body,
        [((N_DP, 2, LANES), f32), ((ROWS, PAY), bf16), ((ROWS, PAY), bf16)],
        scratch=[pltpu.VMEM(half, bf16), pltpu.VMEM(half, f32), pltpu.VMEM((ROWS, WIDTH), f32)],
        n_smem=1, n_in=10, cost=5, name="train",
    )(accept, cols, at_rank, states, partial, hidden, slope, own_w, other_w, gain, head)
    got = lax.all_to_all(message, DP, 0, 0)
    other = lax.ppermute(send, "core", swap)
    term, loss = call(
        term_body,
        [((N_X, LANES, 2 * WIDTH), bf16), ((N_DP, LANES), f32)],
        scratch=[pltpu.VMEM((2 * ROWS, 4 * WIDTH), bf16)],
        n_in=3, cost=4, name="term",
    )(keep, other, got)
    got = lax.all_to_all(term, EVERY, 0, 0, axis_index_groups=STAGE_1)
    middle = call(
        middle_body, [((64, 16, LANES), bf16)], scratch=[pltpu.VMEM((64, 16, LANES), f32)], n_in=1, cost=1, name="middle"
    )(got)
    got = lax.all_to_all(middle, EVERY, 0, 0, axis_index_groups=STAGE_2)
    out = call(final_body, [((2, 2 * WIDTH), f32)], n_in=2, cost=1, name="final")(got, momentum)
    return out, loss[:, :CAP].reshape(1, N_DP * CAP)


def solution(mesh):
    n_dp, n_mp = mesh.devices.shape
    side = int(np.sqrt(n_dp // 2))
    fine = Mesh(mesh.devices.reshape(side, side, 2, n_mp), EVERY)
    placed = (
        P(EVERY, None, None),
        P(EVERY),
        P(EVERY, None),
        P(EVERY, None, None),
        P(EVERY, None, None),
        P(),
        P(),
        P(),
        P(),
        P(),
        P(),
        P(),
        P(),
        P(),
        P(None, "x"),
        P("x", None),
        P(),
        P(),
        P(EVERY, None),
    )
    return jax.shard_map(
        per_device,
        mesh=fine,
        in_specs=placed,
        out_specs=(P(EVERY, None), P(EVERY, None)),
        check_vma=False,
    )
```

```python
import jax
import jax.numpy as jnp
import numpy as np
from jax import lax
from jax.experimental import pallas as pl
from jax.experimental.pallas import tpu as pltpu
from jax.sharding import Mesh
from jax.sharding import PartitionSpec as P

HEADS = 8
BEAM = 5
STEPS = 30
CAP = 5
SEG = BEAM * (STEPS + 1)
PAD = 160
ROWS = 2 * PAD
WIDTH = 512
FF = 1024
VOCAB = 28
PEAKS = 150
LANES = 128
N_DP = 128
N_X = 4
PART = FF // N_X
HALF = FF // 2
PAY = 4 * WIDTH + LANES
f32 = jnp.float32
bf16 = jnp.bfloat16
FLIP = (((1,), (1,)), ((), ()))
TALL = (((0,), (0,)), ((), ()))
DP = ("z", "y", "core")
EVERY = ("z", "y", "core", "x")
SIDE = 8


def index(z, y, core, x):
    return ((z * SIDE + y) * 2 + core) * N_X + x


def stages():
    side, half, pair, ring = range(SIDE), range(SIDE // 2), range(2), range(N_X)
    one = [[index(z, y, 0, x) for x in ring] for z in side for y in side]
    two = [[index(z, y, 0, x) for z in side for y in side] for x in ring]
    for a in half:
        for b in half:
            for x in ring:
                one.append([index(2 * a + z, 2 * b + y, 1, x) for z in pair for y in pair])
    for z in pair:
        for y in pair:
            two.append([index(2 * a + z, 2 * b + y, 1, x) for a in half for b in half for x in ring])
    return one, two


STAGE_1, STAGE_2 = stages()


def mm(a, b):
    return jnp.dot(a, b, preferred_element_type=f32)


def mm_flip(a, b):
    return lax.dot_general(a, b, FLIP, preferred_element_type=f32)


def mm_tall(a, b):
    return lax.dot_general(a, b, TALL, preferred_element_type=f32)


def iota(shape, dim):
    return lax.broadcasted_iota(jnp.int32, shape, dim)


def norm_parts(values):
    mean = jnp.mean(values, -1, keepdims=True)
    centered = values - mean
    scale = lax.rsqrt(jnp.mean(centered * centered, -1, keepdims=True) + 1e-05)
    return centered * scale, scale


def split(v):
    high = v.astype(bf16)
    return high, (v - high.astype(f32)).astype(bf16)


def call(body, outs, scratch=(), cost=4.0, n_smem=0, n_in=0, n_any=0, out_hbm=False, limit=16 << 20, name=None):
    smem = [pl.BlockSpec(memory_space=pltpu.SMEM)] * n_smem
    vmem = [pl.BlockSpec(memory_space=pltpu.VMEM)] * n_in + [pl.BlockSpec(memory_space=pltpu.HBM)] * n_any
    shapes = [jax.ShapeDtypeStruct(s, d) for s, d in outs]
    specs = [pl.BlockSpec(memory_space=pltpu.HBM if out_hbm else pltpu.VMEM)] * len(outs)
    single = len(outs) == 1
    return pl.pallas_call(
        body,
        out_shape=shapes[0] if single else shapes,
        in_specs=smem + vmem,
        out_specs=specs[0] if single else specs,
        scratch_shapes=list(scratch),
        compiler_params=pltpu.CompilerParams(vmem_limit_bytes=limit),
        cost_estimate=pl.CostEstimate(flops=int(cost * 5e8), bytes_accessed=int(cost * 2e6), transcendentals=0),
        name=name,
    )


def start(sems, first, *pairs):
    copies = [pltpu.make_async_copy(src, dst, sems.at[first + k]) for k, (src, dst) in enumerate(pairs)]
    for copy in copies:
        copy.start()
    return copies


def finish(copies):
    for copy in copies:
        copy.wait()


def prepare_body(core_ref, w_in_hbm, w_down_hbm, out_hbm, w_in, w_down, mine, sems):
    loads = start(sems, 0, (w_in_hbm, w_in), (w_down_hbm, w_down))
    place, unit = iota((LANES, PART), 0), iota((LANES, PART), 1)
    block, row, rest = place // 32, place // 16 % 2, place % 16
    first = rest * 16 + block * 2 + row
    second = (block // 2 * 8 + rest // 4 * 2 + block % 2) * 16 + 8 + rest % 4 * 2 + row
    wanted = jnp.where(core_ref[0] == 0, first, second)
    chosen = (unit == wanted).astype(bf16)
    loads[0].wait()
    mine[0] = mm_flip(chosen, w_in[...]).astype(bf16)
    stores = start(sems, 2, *[(mine.at[0], out_hbm.at[k, 0]) for k in range(N_X)])
    loads[1].wait()
    mine[1] = mm(chosen, w_down[...]).astype(bf16)
    stores += start(sems, 2 + N_X, *[(mine.at[1], out_hbm.at[k, 1]) for k in range(N_X)])
    finish(stores)


def attend_body(
    cols_ref, rows_ref, keys_ref, values_ref, embed_ref, gain_self_ref, gain_cross_ref, w_query_hbm, w_key_hbm,
    w_value_hbm, w_self_hbm, cross_query_hbm, cross_out_hbm, states_ref, at_rank_ref, done_ref, ctx_ref, held, sems,
):
    sources = (w_query_hbm, w_key_hbm, w_value_hbm, w_self_hbm, cross_query_hbm, cross_out_hbm)
    loads = [pltpu.make_async_copy(source, held.at[k], sems.at[k]) for k, source in enumerate(sources)]
    for load in loads:
        load.start()
    lane = iota((ROWS, LANES), 1)
    hits = cols_ref[:, 2:3] == lane
    earlier = (iota((ROWS, ROWS), 0) > iota((ROWS, ROWS), 1)).astype(bf16)
    before = mm(earlier, hits.astype(bf16))
    same = (beam_of(0) == beam_of(1)) & (iota((ROWS, ROWS), 0) <= iota((ROWS, ROWS), 1))
    same = same.astype(bf16)
    rank = jnp.sum(jnp.where(hits, before, 0.0), -1, keepdims=True).astype(jnp.int32)
    at_rank_ref[...] = (rank == lane).astype(bf16)
    embed = embed_ref[...]
    names = (iota((32, VOCAB), 0) == iota((32, VOCAB), 1)).astype(bf16)
    table = mm(names, embed).astype(bf16)
    picks = (cols_ref[:, 0:1] == iota((ROWS, 32), 1)).astype(bf16)
    picks_t = (rows_ref[0:1, :] == iota((32, ROWS), 0)).astype(bf16)
    embedded = mm(picks, table)
    for load in loads:
        load.wait()
    query = mm(embedded.astype(bf16), held[0]).astype(bf16)
    keyed = mm(table, held[1])
    valued = mm(table, held[2])
    own = iota((HEADS * 32, WIDTH), 0) // 32 == iota((HEADS * 32, WIDTH), 1) // 64
    key_blocks = jnp.where(own, jnp.concatenate([keyed] * HEADS, 0), 0.0).astype(bf16)
    value_blocks = jnp.where(own, jnp.concatenate([valued] * HEADS, 0), 0.0).astype(bf16)
    scores = (mm_flip(key_blocks, query) * 0.125).reshape(HEADS, 32, ROWS)
    counts = mm(picks_t, same)[None]
    scores = jnp.where(counts > 0.0, scores, -1e30)
    probs = jnp.exp(scores - jnp.max(scores, 1, keepdims=True)) * counts
    probs = probs / jnp.sum(probs, 1, keepdims=True)
    context = mm_tall(probs.reshape(HEADS * 32, ROWS).astype(bf16), value_blocks).astype(bf16)
    unit, _ = norm_parts(embedded + mm(context, held[3]))
    attended = (unit * gain_self_ref[...]).astype(bf16)
    cross_q = mm(attended, held[4]).astype(bf16)
    left = iota((PAD, LANES), 1) < 64
    for s in range(2):
        for pair in range(HEADS // 2):
            lanes = slice(pair * LANES, (pair + 1) * LANES)
            q = cross_q[s * PAD : (s + 1) * PAD, lanes]
            k = keys_ref[s, :, lanes]
            v = values_ref[s, :, lanes]
            both = []
            for mine in (left, jnp.logical_not(left)):
                logit = mm_flip(jnp.where(mine, q, jnp.zeros_like(q)), k) * 0.125
                e = jnp.exp(logit - jnp.max(logit, -1, keepdims=True))
                p = (e / jnp.sum(e, -1, keepdims=True)).astype(bf16)
                both.append(mm(p, v))
            ctx_ref[s * PAD : (s + 1) * PAD, lanes] = jnp.where(left, both[0], both[1]).astype(bf16)
    unit, _ = norm_parts(attended.astype(f32) + mm(ctx_ref[...], held[5]))
    states = (unit * gain_cross_ref[...]).astype(bf16)
    states_ref[...] = states
    done_ref[...] = states[:16, :LANES]


def beam_of(dim):
    shape = (ROWS, 1) if dim == 0 else (1, ROWS)
    row = iota(shape, dim)
    second = (row >= PAD).astype(jnp.int32)
    inside = row - second * PAD
    beam = second * (BEAM + 1)
    for k in range(1, BEAM + 1):
        beam = beam + (inside >= k * (STEPS + 1)).astype(jnp.int32)
    return beam


def half_forward(states, weights_ref, hidden_ref, slope_ref):
    w_in = jnp.concatenate([weights_ref[m, 0] for m in range(N_X)], 0)
    w_down = jnp.concatenate([weights_ref[m, 1] for m in range(N_X)], 0)
    pre = mm_flip(states, w_in)
    square = pre * pre
    tanh = jnp.tanh(pre * (0.7978845608028654 + 0.035677408136300125 * square))
    gate = 0.5 * (1.0 + tanh)
    hidden = (pre * gate).astype(bf16)
    hidden_ref[...] = hidden
    slope_ref[...] = gate * (1.0 + pre * (1.0 - tanh) * (0.7978845608028654 + 0.10703222440890037 * square))
    return mm(hidden, w_down)


def own_body(states_ref, weights_ref, done_ref, hidden_ref, slope_ref, total_ref):
    states = states_ref[...]
    total_ref[...] = states.astype(f32) + half_forward(states, weights_ref, hidden_ref, slope_ref)


def train_body(
    accept_ref, cols_ref, rows_ref, at_rank_ref, states_ref, partial_ref, hidden_1_ref, slope_1_ref, own_ref, other_ref, gain_ref,
    head_ref, message_ref, keep_ref, send_ref, hidden_ref, slope_ref, unit_ref,
):
    states = states_ref[...]
    total = partial_ref[...] + half_forward(states, other_ref, hidden_ref, slope_ref)
    unit, scale = norm_parts(total)
    unit_ref[...] = unit
    gain = gain_ref[...]
    high, low = split(unit * gain)
    names = (iota((32, VOCAB), 0) == iota((32, VOCAB), 1)).astype(bf16)
    head = mm(names, head_ref[...]).astype(bf16)
    logits = mm_flip(head, high) + mm_flip(head, low)
    word = iota((32, ROWS), 0)
    logits = jnp.where(word < VOCAB, logits, -1e30)
    top = jnp.max(logits, 0, keepdims=True)
    grown = jnp.exp(logits - top)
    mass = jnp.sum(grown, 0, keepdims=True)
    is_label = rows_ref[1:2, :] == word
    taken = jnp.sum(jnp.where(is_label, logits, 0.0), 0, keepdims=True) - top - jnp.log(mass)
    row = iota((1, ROWS), 1)
    second = (row >= PAD).astype(jnp.int32)
    beam = beam_of(1) - second
    inside = row - second * PAD
    step = inside
    for k in range(1, BEAM + 1):
        step = step - (step >= STEPS + 1).astype(jnp.int32) * (STEPS + 1)
    beams = jnp.where((beam == iota((16, ROWS), 0)) & (step < STEPS) & (inside < SEG), 1.0, 0.0)
    score = jnp.sum(beams * taken, 1, keepdims=True) / STEPS
    place = iota((16, 1), 0)
    shares = jnp.zeros((16, 1), f32)
    for s in range(2):
        mine = (place >= s * BEAM) & (place < (s + 1) * BEAM)
        e = jnp.where(mine, jnp.exp(score - jnp.max(jnp.where(mine, score, -1e30), 0, keepdims=True)), 0.0)
        share = e / jnp.sum(e, 0, keepdims=True) * accept_ref[s].astype(f32)
        shares = jnp.where(mine, share, shares)
    weight = jnp.sum(beams * shares, 0, keepdims=True)
    to = rows_ref[2:3, :] == iota((LANES, ROWS), 0)
    high, low = split(-weight * taken)
    zero = jnp.zeros((1, ROWS), bf16)
    at_rank = at_rank_ref[...]
    slots = mm(jnp.where(to, high, zero), at_rank) + mm(jnp.where(to, low, zero), at_rank)
    high, low = split(jnp.broadcast_to(weight, (8, ROWS)))
    hits = (cols_ref[:, 2:3] == iota((ROWS, LANES), 1)).astype(bf16)
    sums = mm(high, hits) + mm(low, hits)
    message_ref[:, 0, :] = jnp.broadcast_to(sums[0:1], (N_DP, LANES))
    message_ref[:, 1, :] = slots

    high, low = split(weight * (grown / mass - is_label.astype(f32)))
    unit = unit_ref[...]
    d_unit = gain * mm_tall(jnp.concatenate([high, low], 0), jnp.concatenate([head, head], 0))
    along = jnp.mean(d_unit * unit, -1, keepdims=True)
    d_total = scale * (d_unit - jnp.mean(d_unit, -1, keepdims=True) - unit * along)
    d_out = d_total.astype(bf16)
    dest = jnp.broadcast_to(cols_ref[:, 2:3], (ROWS, LANES)).astype(f32).astype(bf16)
    for ref, hidden, slope, weights in (
        (send_ref, hidden_ref, slope_ref, other_ref),
        (keep_ref, hidden_1_ref, slope_1_ref, own_ref),
    ):
        w_down = jnp.concatenate([weights[m, 1] for m in range(N_X)], 0)
        ref[:, 0:WIDTH] = (mm_flip(d_out, w_down) * slope[...]).astype(bf16)
        ref[:, WIDTH : 2 * WIDTH] = hidden[...]
        ref[:, 2 * WIDTH : 3 * WIDTH] = states
        ref[:, 3 * WIDTH : 4 * WIDTH] = d_out
        ref[:, 4 * WIDTH :] = dest


def term_body(keep_ref, other_ref, got_ref, term_ref, loss_ref, all_ref):
    sums = jnp.sum(got_ref[:, 0, :], 0, keepdims=True)
    loss_ref[...] = got_ref[:, 1, :]
    inverse = 1.0 / jnp.maximum(sums, 1.0)
    lane = iota((ROWS, LANES), 1).astype(f32)
    for place, ref in ((0, keep_ref), (1, other_ref)):
        rows = slice(place * ROWS, (place + 1) * ROWS)
        hits = ref[:, 4 * WIDTH :].astype(f32) == lane
        factor = jnp.sum(jnp.where(hits, inverse, 0.0), -1, keepdims=True)
        all_ref[rows, : 2 * WIDTH] = ref[:, : 2 * WIDTH]
        all_ref[rows, 2 * WIDTH :] = (ref[:, 2 * WIDTH : 4 * WIDTH].astype(f32) * factor).astype(bf16)
    for k in range(2):
        grad = mm_tall(all_ref[:, k * WIDTH : (k + 1) * WIDTH], all_ref[:, (k + 2) * WIDTH : (k + 3) * WIDTH])
        grad = grad.astype(bf16)
        for m in range(N_X):
            for x in range(N_X):
                start = m * LANES + x * 32
                term_ref[x, m * 32 : (m + 1) * 32, k * WIDTH : (k + 1) * WIDTH] = grad[start : start + 32]


def middle_body(got_ref, out_ref, held_ref):
    for m in range(N_X):
        rows = slice(m * 32, (m + 1) * 32)
        total = got_ref[0, rows].astype(f32) + got_ref[1, rows].astype(f32)
        total = total + (got_ref[2, rows].astype(f32) + got_ref[3, rows].astype(f32))
        here = slice(m * 16, (m + 1) * 16)
        for r in range(2):
            for c in range(8):
                held_ref[here, r * 8 + c, :] = total[r * 16 : (r + 1) * 16, c * LANES : (c + 1) * LANES]
        out_ref[here] = held_ref[here].astype(bf16)


def final_body(got_ref, momentum_ref, loss_ref, out_ref, slots_ref):
    total = jnp.sum(got_ref[...].astype(f32), 0)
    for r in range(2):
        for c in range(8):
            lanes = slice(c * LANES, (c + 1) * LANES)
            out_ref[r : r + 1, lanes] = 0.9 * momentum_ref[r : r + 1, lanes] + total[r * 8 + c : r * 8 + c + 1]
    slot, source = iota((N_DP, N_DP * CAP), 1), iota((N_DP, N_DP * CAP), 0)
    offset = slot - source * CAP
    spread = jnp.zeros((N_DP, N_DP * CAP), f32)
    for k in range(CAP):
        spread = jnp.where(offset == k, loss_ref[:, k : k + 1], spread)
    slots_ref[...] = jnp.sum(spread, 0, keepdims=True)


def per_device(
    tokens, accept, dest, mem_keys, mem_values, embed, w_query, w_key, w_value, w_self, cross_query, cross_out,
    gain_self, gain_cross, w_in, w_down, gain_ff, head, momentum,
):
    core = lax.axis_index("core").astype(jnp.int32).reshape(1)
    swap = [(0, 1), (1, 0)]
    half = (ROWS, HALF)

    mine = call(
        prepare_body,
        [((N_X, 2, LANES, WIDTH), bf16)],
        scratch=[
            pltpu.VMEM((WIDTH, PART), bf16),
            pltpu.VMEM((PART, WIDTH), bf16),
            pltpu.VMEM((2, LANES, WIDTH), bf16),
            pltpu.SemaphoreType.DMA((2 + 2 * N_X,)),
        ],
        n_smem=1, n_any=2, out_hbm=True, limit=63_300_000, cost=1, name="prepare",
    )(core, w_in, w_down)
    own_w = lax.all_to_all(mine, "x", 0, 0)

    flat = tokens.reshape(2, SEG)
    nexts = lax.pad(flat, jnp.int32(0), ((0, 0, 0), (-1, PAD - SEG + 1, 0))).reshape(ROWS)
    flat = jnp.pad(flat, ((0, 0), (0, PAD - SEG))).reshape(ROWS)
    place = jnp.pad(dest.reshape(2, BEAM, STEPS), ((0, 0), (0, 0), (0, 1)), constant_values=-1).reshape(2, SEG)
    place = jnp.pad(place, ((0, 0), (0, PAD - SEG)), constant_values=-1).reshape(ROWS)
    rows = jnp.stack([flat, nexts, place, place, place, place, place, place])
    cols = rows.T
    states, at_rank, done = call(
        attend_body,
        [((ROWS, WIDTH), bf16), ((ROWS, LANES), bf16), ((16, LANES), bf16)],
        scratch=[
            pltpu.VMEM((ROWS, WIDTH), bf16),
            pltpu.VMEM((6, WIDTH, WIDTH), bf16),
            pltpu.SemaphoreType.DMA((6,)),
        ],
        n_in=7, n_any=6, limit=61_300_000, cost=8, name="attend",
    )(
        cols, rows, mem_keys, mem_values, embed, gain_self.reshape(1, WIDTH), gain_cross.reshape(1, WIDTH),
        w_query, w_key, w_value, w_self, cross_query, cross_out,
    )
    own_w, done = lax.optimization_barrier((own_w, done))
    other_w = lax.ppermute(own_w, "core", swap)
    hidden, slope, partial = call(
        own_body, [(half, bf16), (half, f32), ((ROWS, WIDTH), f32)], n_in=3, cost=2, name="own"
    )(states, own_w, done)
    gain = gain_ff.reshape(1, WIDTH)
    head = head.T
    message, keep, send = call(
        train_body,
        [((N_DP, 2, LANES), f32), ((ROWS, PAY), bf16), ((ROWS, PAY), bf16)],
        scratch=[pltpu.VMEM(half, bf16), pltpu.VMEM(half, f32), pltpu.VMEM((ROWS, WIDTH), f32)],
        n_smem=1, n_in=11, cost=5, name="train",
    )(accept, cols, rows, at_rank, states, partial, hidden, slope, own_w, other_w, gain, head)
    got = lax.all_to_all(message, DP, 0, 0)
    other = lax.ppermute(send, "core", swap)
    term, loss = call(
        term_body,
        [((N_X, LANES, 2 * WIDTH), bf16), ((N_DP, LANES), f32)],
        scratch=[pltpu.VMEM((2 * ROWS, 4 * WIDTH), bf16)],
        n_in=3, cost=4, name="term",
    )(keep, other, got)
    got = lax.all_to_all(term, EVERY, 0, 0, axis_index_groups=STAGE_1)
    middle = call(
        middle_body, [((64, 16, LANES), bf16)], scratch=[pltpu.VMEM((64, 16, LANES), f32)], n_in=1, cost=1, name="middle"
    )(got)
    got = lax.all_to_all(middle, EVERY, 0, 0, axis_index_groups=STAGE_2)
    return tuple(
        call(final_body, [((2, 2 * WIDTH), f32), ((1, N_DP * CAP), f32)], n_in=3, cost=1, name="final")(got, momentum, loss)
    )


def solution(mesh):
    n_dp, n_mp = mesh.devices.shape
    side = int(np.sqrt(n_dp // 2))
    fine = Mesh(mesh.devices.reshape(side, side, 2, n_mp), EVERY)
    placed = (
        P(EVERY, None, None),
        P(EVERY),
        P(EVERY, None),
        P(EVERY, None, None),
        P(EVERY, None, None),
        P(),
        P(),
        P(),
        P(),
        P(),
        P(),
        P(),
        P(),
        P(),
        P(None, "x"),
        P("x", None),
        P(),
        P(),
        P(EVERY, None),
    )
    return jax.shard_map(
        per_device,
        mesh=fine,
        in_specs=placed,
        out_specs=(P(EVERY, None), P(EVERY, None)),
        check_vma=False,
    )
```

```python
import jax
import jax.numpy as jnp
import numpy as np
from jax import lax
from jax.experimental import pallas as pl
from jax.experimental.pallas import tpu as pltpu
from jax.sharding import Mesh
from jax.sharding import PartitionSpec as P

HEADS = 8
BEAM = 5
STEPS = 30
CAP = 5
SEG = BEAM * (STEPS + 1)
PAD = 160
ROWS = 2 * PAD
WIDTH = 512
FF = 1024
VOCAB = 28
PEAKS = 150
LANES = 128
N_DP = 128
N_X = 4
PART = FF // N_X
HALF = FF // 2
PAY = 4 * WIDTH + LANES
f32 = jnp.float32
bf16 = jnp.bfloat16
FLIP = (((1,), (1,)), ((), ()))
TALL = (((0,), (0,)), ((), ()))
DP = ("z", "y", "core")
EVERY = ("z", "y", "core", "x")
SIDE = 8


def index(z, y, core, x):
    return ((z * SIDE + y) * 2 + core) * N_X + x


def stages():
    side, half, pair, ring = range(SIDE), range(SIDE // 2), range(2), range(N_X)
    one = [[index(z, y, 0, x) for x in ring] for z in side for y in side]
    two = [[index(z, y, 0, x) for z in side for y in side] for x in ring]
    for a in half:
        for b in half:
            for x in ring:
                one.append([index(2 * a + z, 2 * b + y, 1, x) for z in pair for y in pair])
    for z in pair:
        for y in pair:
            two.append([index(2 * a + z, 2 * b + y, 1, x) for a in half for b in half for x in ring])
    return one, two


STAGE_1, STAGE_2 = stages()


def mm(a, b):
    return jnp.dot(a, b, preferred_element_type=f32)


def mm_flip(a, b):
    return lax.dot_general(a, b, FLIP, preferred_element_type=f32)


def mm_tall(a, b):
    return lax.dot_general(a, b, TALL, preferred_element_type=f32)


def iota(shape, dim):
    return lax.broadcasted_iota(jnp.int32, shape, dim)


def norm_parts(values):
    mean = jnp.mean(values, -1, keepdims=True)
    centered = values - mean
    scale = lax.rsqrt(jnp.mean(centered * centered, -1, keepdims=True) + 1e-05)
    return centered * scale, scale


def split(v):
    high = v.astype(bf16)
    return high, (v - high.astype(f32)).astype(bf16)


def call(body, outs, scratch=(), cost=4.0, n_smem=0, n_in=0, n_any=0, out_hbm=False, limit=16 << 20, name=None):
    smem = [pl.BlockSpec(memory_space=pltpu.SMEM)] * n_smem
    vmem = [pl.BlockSpec(memory_space=pltpu.VMEM)] * n_in + [pl.BlockSpec(memory_space=pltpu.HBM)] * n_any
    shapes = [jax.ShapeDtypeStruct(s, d) for s, d in outs]
    specs = [pl.BlockSpec(memory_space=pltpu.HBM if out_hbm else pltpu.VMEM)] * len(outs)
    single = len(outs) == 1
    return pl.pallas_call(
        body,
        out_shape=shapes[0] if single else shapes,
        in_specs=smem + vmem,
        out_specs=specs[0] if single else specs,
        scratch_shapes=list(scratch),
        compiler_params=pltpu.CompilerParams(vmem_limit_bytes=limit),
        cost_estimate=pl.CostEstimate(flops=int(cost * 5e8), bytes_accessed=int(cost * 2e6), transcendentals=0),
        name=name,
    )


def start(sems, first, *pairs):
    copies = [pltpu.make_async_copy(src, dst, sems.at[first + k]) for k, (src, dst) in enumerate(pairs)]
    for copy in copies:
        copy.start()
    return copies


def finish(copies):
    for copy in copies:
        copy.wait()


def prepare_body(ids_ref, w_in_hbm, w_down_hbm, out_hbm, w_in, w_down, mine, sems):
    loads = start(sems, 0, (w_in_hbm, w_in), (w_down_hbm, w_down))
    place, unit = iota((LANES, PART), 0), iota((LANES, PART), 1)
    block, row, rest = place // 32, place // 16 % 2, place % 16
    first = rest * 16 + block * 2 + row
    second = (block // 2 * 8 + rest // 4 * 2 + block % 2) * 16 + 8 + rest % 4 * 2 + row
    own = ids_ref[0] == 0
    chosen = [(unit == jnp.where(own, first, second)).astype(bf16), (unit == jnp.where(own, second, first)).astype(bf16)]
    loads[0].wait()
    for k in range(2):
        mine[k, 0] = mm_flip(chosen[k], w_in[...]).astype(bf16)
    stores = start(sems, 2, *[(mine.at[k, 0], out_hbm.at[k, 0]) for k in range(2)])
    loads[1].wait()
    for k in range(2):
        mine[k, 1] = mm(chosen[k], w_down[...]).astype(bf16)
    stores += start(sems, 4, *[(mine.at[k, 1], out_hbm.at[k, 1]) for k in range(2)])
    finish(stores)


def self_body(
    cols_ref, rows_ref, embed_ref, gain_self_ref, w_query_hbm, w_key_hbm, w_value_hbm, w_self_hbm,
    attended_ref, at_rank_ref, done_ref, held, sems,
):
    sources = (w_query_hbm, w_key_hbm, w_value_hbm, w_self_hbm)
    loads = start(sems, 0, *[(source, held.at[k]) for k, source in enumerate(sources)])
    lane = iota((ROWS, LANES), 1)
    hits = cols_ref[:, 2:3] == lane
    earlier = (iota((ROWS, ROWS), 0) > iota((ROWS, ROWS), 1)).astype(bf16)
    before = mm(earlier, hits.astype(bf16))
    same = (beam_of(0) == beam_of(1)) & (iota((ROWS, ROWS), 0) <= iota((ROWS, ROWS), 1))
    same = same.astype(bf16)
    rank = jnp.sum(jnp.where(hits, before, 0.0), -1, keepdims=True).astype(jnp.int32)
    at_rank_ref[...] = (rank == lane).astype(bf16)
    embed = embed_ref[...]
    names = (iota((32, VOCAB), 0) == iota((32, VOCAB), 1)).astype(bf16)
    table = mm(names, embed).astype(bf16)
    picks = (cols_ref[:, 0:1] == iota((ROWS, 32), 1)).astype(bf16)
    picks_t = (rows_ref[0:1, :] == iota((32, ROWS), 0)).astype(bf16)
    embedded = mm(picks, table)
    finish(loads)
    query = mm(embedded.astype(bf16), held[0]).astype(bf16)
    keyed = mm(table, held[1])
    valued = mm(table, held[2])
    own = iota((HEADS * 32, WIDTH), 0) // 32 == iota((HEADS * 32, WIDTH), 1) // 64
    key_blocks = jnp.where(own, jnp.concatenate([keyed] * HEADS, 0), 0.0).astype(bf16)
    value_blocks = jnp.where(own, jnp.concatenate([valued] * HEADS, 0), 0.0).astype(bf16)
    scores = (mm_flip(key_blocks, query) * 0.125).reshape(HEADS, 32, ROWS)
    counts = mm(picks_t, same)[None]
    scores = jnp.where(counts > 0.0, scores, -1e30)
    probs = jnp.exp(scores - jnp.max(scores, 1, keepdims=True)) * counts
    probs = probs / jnp.sum(probs, 1, keepdims=True)
    context = mm_tall(probs.reshape(HEADS * 32, ROWS).astype(bf16), value_blocks).astype(bf16)
    unit, _ = norm_parts(embedded + mm(context, held[3]))
    attended = (unit * gain_self_ref[...]).astype(bf16)
    attended_ref[...] = attended
    done_ref[...] = attended[:16, :LANES]


def cross_body(
    attended_ref, gain_cross_ref, cross_query_hbm, keys_hbm, values_hbm, cross_out_hbm, states_ref, done_ref,
    ctx_ref, held, keys_ref, values_ref, sems,
):
    loads = start(
        sems, 0, (cross_query_hbm, held.at[0]), (keys_hbm, keys_ref), (values_hbm, values_ref), (cross_out_hbm, held.at[1])
    )
    attended = attended_ref[...]
    loads[0].wait()
    cross_q = mm(attended, held[0]).astype(bf16)
    finish(loads[1:3])
    left = iota((PAD, LANES), 1) < 64
    for s in range(2):
        for pair in range(HEADS // 2):
            lanes = slice(pair * LANES, (pair + 1) * LANES)
            q = cross_q[s * PAD : (s + 1) * PAD, lanes]
            k = keys_ref[s, :, lanes]
            v = values_ref[s, :, lanes]
            both = []
            for mine in (left, jnp.logical_not(left)):
                logit = mm_flip(jnp.where(mine, q, jnp.zeros_like(q)), k) * 0.125
                e = jnp.exp(logit - jnp.max(logit, -1, keepdims=True))
                p = (e / jnp.sum(e, -1, keepdims=True)).astype(bf16)
                both.append(mm(p, v))
            ctx_ref[s * PAD : (s + 1) * PAD, lanes] = jnp.where(left, both[0], both[1]).astype(bf16)
    loads[3].wait()
    unit, _ = norm_parts(attended.astype(f32) + mm(ctx_ref[...], held[1]))
    states = (unit * gain_cross_ref[...]).astype(bf16)
    states_ref[...] = states
    done_ref[...] = states[:16, :LANES]


def beam_of(dim):
    shape = (ROWS, 1) if dim == 0 else (1, ROWS)
    row = iota(shape, dim)
    second = (row >= PAD).astype(jnp.int32)
    inside = row - second * PAD
    beam = second * (BEAM + 1)
    for k in range(1, BEAM + 1):
        beam = beam + (inside >= k * (STEPS + 1)).astype(jnp.int32)
    return beam


def part_forward(states, blocks, hidden_ref, slope_ref):
    w_in = jnp.concatenate([ref[at + (0,)] for ref, at in blocks], 0)
    w_down = jnp.concatenate([ref[at + (1,)] for ref, at in blocks], 0)
    pre = mm_flip(states, w_in)
    square = pre * pre
    tanh = jnp.tanh(pre * (0.7978845608028654 + 0.035677408136300125 * square))
    gate = 0.5 * (1.0 + tanh)
    hidden = (pre * gate).astype(bf16)
    hidden_ref[...] = hidden
    slope_ref[...] = gate * (1.0 + pre * (1.0 - tanh) * (0.7978845608028654 + 0.10703222440890037 * square))
    return mm(hidden, w_down)


def own_body(states_ref, mine_ref, next_ref, last_ref, hidden_ref, slope_ref, total_ref):
    states = states_ref[...]
    blocks = [(ref, (k,)) for ref in (mine_ref, next_ref, last_ref) for k in range(2)]
    total_ref[...] = states.astype(f32) + part_forward(states, blocks, hidden_ref, slope_ref)


def train_body(
    accept_ref, ids_ref, cols_ref, rows_ref, at_rank_ref, states_ref, partial_ref, hidden_1_ref, slope_1_ref, mine_ref, next_ref,
    last_ref, far_ref, far_2_ref, gain_ref, head_ref, message_ref, keep_ref, send_ref, hidden_ref, slope_ref, unit_ref,
):
    states = states_ref[...]
    total = partial_ref[...] + part_forward(states, [(far_ref, ()), (far_2_ref, ())], hidden_ref, slope_ref)
    unit, scale = norm_parts(total)
    unit_ref[...] = unit
    gain = gain_ref[...]
    high, low = split(unit * gain)
    names = (iota((32, VOCAB), 0) == iota((32, VOCAB), 1)).astype(bf16)
    head = mm(names, head_ref[...]).astype(bf16)
    logits = mm_flip(head, high) + mm_flip(head, low)
    word = iota((32, ROWS), 0)
    logits = jnp.where(word < VOCAB, logits, -1e30)
    top = jnp.max(logits, 0, keepdims=True)
    grown = jnp.exp(logits - top)
    mass = jnp.sum(grown, 0, keepdims=True)
    is_label = rows_ref[1:2, :] == word
    taken = jnp.sum(jnp.where(is_label, logits, 0.0), 0, keepdims=True) - top - jnp.log(mass)
    row = iota((1, ROWS), 1)
    second = (row >= PAD).astype(jnp.int32)
    beam = beam_of(1) - second
    inside = row - second * PAD
    step = inside
    for k in range(1, BEAM + 1):
        step = step - (step >= STEPS + 1).astype(jnp.int32) * (STEPS + 1)
    beams = jnp.where((beam == iota((16, ROWS), 0)) & (step < STEPS) & (inside < SEG), 1.0, 0.0)
    score = jnp.sum(beams * taken, 1, keepdims=True) / STEPS
    place = iota((16, 1), 0)
    shares = jnp.zeros((16, 1), f32)
    for s in range(2):
        mine = (place >= s * BEAM) & (place < (s + 1) * BEAM)
        e = jnp.where(mine, jnp.exp(score - jnp.max(jnp.where(mine, score, -1e30), 0, keepdims=True)), 0.0)
        share = e / jnp.sum(e, 0, keepdims=True) * accept_ref[s].astype(f32)
        shares = jnp.where(mine, share, shares)
    weight = jnp.sum(beams * shares, 0, keepdims=True)
    to = rows_ref[2:3, :] == iota((LANES, ROWS), 0)
    high, low = split(-weight * taken)
    zero = jnp.zeros((1, ROWS), bf16)
    at_rank = at_rank_ref[...]
    slots = mm(jnp.where(to, high, zero), at_rank) + mm(jnp.where(to, low, zero), at_rank)
    high, low = split(jnp.broadcast_to(weight, (8, ROWS)))
    hits = (cols_ref[:, 2:3] == iota((ROWS, LANES), 1)).astype(bf16)
    sums = mm(high, hits) + mm(low, hits)
    message_ref[:, 0, :] = jnp.broadcast_to(sums[0:1], (N_DP, LANES))
    message_ref[:, 1, :] = slots

    high, low = split(weight * (grown / mass - is_label.astype(f32)))
    unit = unit_ref[...]
    d_unit = gain * mm_tall(jnp.concatenate([high, low], 0), jnp.concatenate([head, head], 0))
    along = jnp.mean(d_unit * unit, -1, keepdims=True)
    d_total = scale * (d_unit - jnp.mean(d_unit, -1, keepdims=True) - unit * along)
    d_out = d_total.astype(bf16)
    dest = jnp.broadcast_to(cols_ref[:, 2:3], (ROWS, LANES)).astype(f32).astype(bf16)
    core, x = ids_ref[0], ids_ref[1]
    one, three = lax.bitwise_xor(x, 1), lax.bitwise_xor(x, 3)
    places = (x, jnp.where(core == 0, one, three), jnp.where(core == 0, three, one), lax.bitwise_xor(x, 2))
    for k, ref, far in ((1, send_ref, far_2_ref), (0, keep_ref, far_ref)):
        w_down = jnp.concatenate([mine_ref[k, 1], next_ref[k, 1], last_ref[1 - k, 1], far[1]], 0)
        d_hidden = mm_flip(d_out, w_down)
        blocks = (
            (hidden_1_ref, slope_1_ref, k),
            (hidden_1_ref, slope_1_ref, 2 + k),
            (hidden_1_ref, slope_1_ref, 5 - k),
            (hidden_ref, slope_ref, k),
        )
        for q, (hidden, slope, at) in enumerate(blocks):
            lanes = slice(at * LANES, (at + 1) * LANES)
            d_pre = (d_hidden[:, q * LANES : (q + 1) * LANES] * slope[:, lanes]).astype(bf16)
            ref[:, pl.ds(pl.multiple_of(places[q] * LANES, LANES), LANES)] = d_pre
            ref[:, pl.ds(pl.multiple_of(WIDTH + places[q] * LANES, LANES), LANES)] = hidden[:, lanes]
        ref[:, 2 * WIDTH : 3 * WIDTH] = states
        ref[:, 3 * WIDTH : 4 * WIDTH] = d_out
        ref[:, 4 * WIDTH :] = dest


def term_body(keep_ref, other_ref, got_ref, term_ref, loss_ref, all_ref):
    sums = jnp.sum(got_ref[:, 0, :], 0, keepdims=True)
    loss_ref[...] = got_ref[:, 1, :]
    inverse = 1.0 / jnp.maximum(sums, 1.0)
    lane = iota((ROWS, LANES), 1).astype(f32)
    for place, ref in ((0, keep_ref), (1, other_ref)):
        rows = slice(place * ROWS, (place + 1) * ROWS)
        hits = ref[:, 4 * WIDTH :].astype(f32) == lane
        factor = jnp.sum(jnp.where(hits, inverse, 0.0), -1, keepdims=True)
        all_ref[rows, : 2 * WIDTH] = ref[:, : 2 * WIDTH]
        all_ref[rows, 2 * WIDTH :] = (ref[:, 2 * WIDTH : 4 * WIDTH].astype(f32) * factor).astype(bf16)
    for k in range(2):
        grad = mm_tall(all_ref[:, k * WIDTH : (k + 1) * WIDTH], all_ref[:, (k + 2) * WIDTH : (k + 3) * WIDTH])
        grad = grad.astype(bf16)
        for m in range(N_X):
            for x in range(N_X):
                start = m * LANES + x * 32
                term_ref[x, m * 32 : (m + 1) * 32, k * WIDTH : (k + 1) * WIDTH] = grad[start : start + 32]


def middle_body(got_ref, out_ref, held_ref):
    for m in range(N_X):
        rows = slice(m * 32, (m + 1) * 32)
        total = got_ref[0, rows].astype(f32) + got_ref[1, rows].astype(f32)
        total = total + (got_ref[2, rows].astype(f32) + got_ref[3, rows].astype(f32))
        here = slice(m * 16, (m + 1) * 16)
        for r in range(2):
            for c in range(8):
                held_ref[here, r * 8 + c, :] = total[r * 16 : (r + 1) * 16, c * LANES : (c + 1) * LANES]
        out_ref[here] = held_ref[here].astype(bf16)


def final_body(got_ref, momentum_ref, loss_ref, done_ref, done_2_ref, out_ref, slots_ref):
    total = jnp.sum(got_ref[...].astype(f32), 0)
    for r in range(2):
        for c in range(8):
            lanes = slice(c * LANES, (c + 1) * LANES)
            out_ref[r : r + 1, lanes] = 0.9 * momentum_ref[r : r + 1, lanes] + total[r * 8 + c : r * 8 + c + 1]
    slot, source = iota((N_DP, N_DP * CAP), 1), iota((N_DP, N_DP * CAP), 0)
    offset = slot - source * CAP
    spread = jnp.zeros((N_DP, N_DP * CAP), f32)
    for k in range(CAP):
        spread = jnp.where(offset == k, loss_ref[:, k : k + 1], spread)
    slots_ref[...] = jnp.sum(spread, 0, keepdims=True)


def per_device(
    tokens, accept, dest, mem_keys, mem_values, embed, w_query, w_key, w_value, w_self, cross_query, cross_out,
    gain_self, gain_cross, w_in, w_down, gain_ff, head, momentum,
):
    ids = jnp.stack([lax.axis_index("core"), lax.axis_index("x")]).astype(jnp.int32)
    chip = ("core", "x")
    swap = [(0, 1), (1, 0)]
    ring = range(N_X)
    near = [(x, x ^ 1) for x in ring] + [(N_X + x, N_X + (x ^ 3)) for x in ring]
    far = [(x, N_X + (x ^ 3)) for x in ring] + [(N_X + x, x ^ 1) for x in ring]
    shard = (2, 2, LANES, WIDTH)

    mine = call(
        prepare_body,
        [(shard, bf16)],
        scratch=[
            pltpu.VMEM((WIDTH, PART), bf16),
            pltpu.VMEM((PART, WIDTH), bf16),
            pltpu.VMEM(shard, bf16),
            pltpu.SemaphoreType.DMA((6,)),
        ],
        n_smem=1, n_any=2, out_hbm=True, limit=63_300_000, cost=1, name="prepare",
    )(ids, w_in, w_down)
    next_w = lax.ppermute(mine, chip, near)

    flat = tokens.reshape(2, SEG)
    nexts = lax.pad(flat, jnp.int32(0), ((0, 0, 0), (-1, PAD - SEG + 1, 0))).reshape(ROWS)
    flat = jnp.pad(flat, ((0, 0), (0, PAD - SEG))).reshape(ROWS)
    place = jnp.pad(dest.reshape(2, BEAM, STEPS), ((0, 0), (0, 0), (0, 1)), constant_values=-1).reshape(2, SEG)
    place = jnp.pad(place, ((0, 0), (0, PAD - SEG)), constant_values=-1).reshape(ROWS)
    rows = jnp.stack([flat, nexts, place, place, place, place, place, place])
    cols = rows.T
    attended, at_rank, done = call(
        self_body,
        [((ROWS, WIDTH), bf16), ((ROWS, LANES), bf16), ((16, LANES), bf16)],
        scratch=[pltpu.VMEM((4, WIDTH, WIDTH), bf16), pltpu.SemaphoreType.DMA((4,))],
        n_in=4, n_any=4, limit=61_300_000, cost=5, name="self",
    )(cols, rows, embed, gain_self.reshape(1, WIDTH), w_query, w_key, w_value, w_self)
    next_w, done = lax.optimization_barrier((next_w, done))
    far_w = lax.ppermute(next_w[1], chip, far)
    last_w = lax.ppermute(next_w, "core", swap)
    states, done_2 = call(
        cross_body,
        [((ROWS, WIDTH), bf16), ((16, LANES), bf16)],
        scratch=[
            pltpu.VMEM((ROWS, WIDTH), bf16),
            pltpu.VMEM((2, WIDTH, WIDTH), bf16),
            pltpu.VMEM((2, PEAKS, WIDTH), bf16),
            pltpu.VMEM((2, PEAKS, WIDTH), bf16),
            pltpu.SemaphoreType.DMA((4,)),
        ],
        n_in=2, n_any=4, limit=61_300_000, cost=5, name="cross",
    )(attended, gain_cross.reshape(1, WIDTH), cross_query, mem_keys, mem_values, cross_out)
    far_w, done_2 = lax.optimization_barrier((far_w, done_2))
    far_2_w = lax.ppermute(far_w, "core", swap)
    most = (ROWS, 6 * LANES)
    rest = (ROWS, 2 * LANES)
    hidden, slope, partial = call(
        own_body, [(most, bf16), (most, f32), ((ROWS, WIDTH), f32)], n_in=4, cost=2, name="own"
    )(states, mine, next_w, last_w)
    gain = gain_ff.reshape(1, WIDTH)
    head = head.T
    message, keep, send = call(
        train_body,
        [((N_DP, 2, LANES), f32), ((ROWS, PAY), bf16), ((ROWS, PAY), bf16)],
        scratch=[pltpu.VMEM(rest, bf16), pltpu.VMEM(rest, f32), pltpu.VMEM((ROWS, WIDTH), f32)],
        n_smem=2, n_in=14, cost=5, name="train",
    )(
        accept, ids, cols, rows, at_rank, states, partial, hidden, slope, mine, next_w, last_w, far_w, far_2_w, gain, head
    )
    got = lax.all_to_all(message, DP, 0, 0)
    other = lax.ppermute(send, "core", swap)
    term, loss = call(
        term_body,
        [((N_X, LANES, 2 * WIDTH), bf16), ((N_DP, LANES), f32)],
        scratch=[pltpu.VMEM((2 * ROWS, 4 * WIDTH), bf16)],
        n_in=3, cost=4, name="term",
    )(keep, other, got)
    got = lax.all_to_all(term, EVERY, 0, 0, axis_index_groups=STAGE_1)
    middle = call(
        middle_body, [((64, 16, LANES), bf16)], scratch=[pltpu.VMEM((64, 16, LANES), f32)], n_in=1, cost=1, name="middle"
    )(got)
    got = lax.all_to_all(middle, EVERY, 0, 0, axis_index_groups=STAGE_2)
    return tuple(
        call(final_body, [((2, 2 * WIDTH), f32), ((1, N_DP * CAP), f32)], n_in=5, cost=1, name="final")(
            got, momentum, loss, done, done_2
        )
    )


def solution(mesh):
    n_dp, n_mp = mesh.devices.shape
    side = int(np.sqrt(n_dp // 2))
    fine = Mesh(mesh.devices.reshape(side, side, 2, n_mp), EVERY)
    placed = (
        P(EVERY, None, None),
        P(EVERY),
        P(EVERY, None),
        P(EVERY, None, None),
        P(EVERY, None, None),
        P(),
        P(),
        P(),
        P(),
        P(),
        P(),
        P(),
        P(),
        P(),
        P(None, "x"),
        P("x", None),
        P(),
        P(),
        P(EVERY, None),
    )
    return jax.shard_map(
        per_device,
        mesh=fine,
        in_specs=placed,
        out_specs=(P(EVERY, None), P(EVERY, None)),
        check_vma=False,
    )
```

```python
import jax
import jax.numpy as jnp
import numpy as np
from jax import lax
from jax.experimental import pallas as pl
from jax.experimental.pallas import tpu as pltpu
from jax.sharding import Mesh
from jax.sharding import PartitionSpec as P

HEADS = 8
BEAM = 5
STEPS = 30
CAP = 5
SEG = BEAM * (STEPS + 1)
PAD = 160
ROWS = 2 * PAD
WIDTH = 512
FF = 1024
VOCAB = 28
PEAKS = 150
LANES = 128
N_DP = 128
N_X = 4
PART = FF // N_X
HALF = FF // 2
PAY = 4 * WIDTH + LANES
f32 = jnp.float32
bf16 = jnp.bfloat16
FLIP = (((1,), (1,)), ((), ()))
TALL = (((0,), (0,)), ((), ()))
DP = ("z", "y", "core")
EVERY = ("z", "y", "core", "x")
SIDE = 8


def index(z, y, core, x):
    return ((z * SIDE + y) * 2 + core) * N_X + x


def stages():
    side, half, pair, ring = range(SIDE), range(SIDE // 2), range(2), range(N_X)
    one, two = [], []
    for a in half:
        for b in half:
            for x in ring:
                one.append([index(2 * a + z, 2 * b + y, 0, x) for z in pair for y in pair])
    for z in pair:
        for y in pair:
            two.append([index(2 * a + z, 2 * b + y, 0, x) for a in half for b in half for x in ring])
    one += [[index(z, y, 1, x) for x in ring] for z in side for y in side]
    two += [[index(z, y, 1, x) for z in side for y in side] for x in ring]
    return one, two


STAGE_1, STAGE_2 = stages()


def mm(a, b):
    return jnp.dot(a, b, preferred_element_type=f32)


def mm_flip(a, b):
    return lax.dot_general(a, b, FLIP, preferred_element_type=f32)


def mm_tall(a, b):
    return lax.dot_general(a, b, TALL, preferred_element_type=f32)


def iota(shape, dim):
    return lax.broadcasted_iota(jnp.int32, shape, dim)


def norm_parts(values):
    mean = jnp.mean(values, -1, keepdims=True)
    centered = values - mean
    scale = lax.rsqrt(jnp.mean(centered * centered, -1, keepdims=True) + 1e-05)
    return centered * scale, scale


def split(v):
    high = v.astype(bf16)
    return high, (v - high.astype(f32)).astype(bf16)


def call(body, outs, scratch=(), cost=4.0, n_smem=0, n_in=0, n_any=0, out_hbm=False, limit=16 << 20, name=None):
    smem = [pl.BlockSpec(memory_space=pltpu.SMEM)] * n_smem
    vmem = [pl.BlockSpec(memory_space=pltpu.VMEM)] * n_in + [pl.BlockSpec(memory_space=pltpu.HBM)] * n_any
    shapes = [jax.ShapeDtypeStruct(s, d) for s, d in outs]
    specs = [pl.BlockSpec(memory_space=pltpu.HBM if out_hbm else pltpu.VMEM)] * len(outs)
    single = len(outs) == 1
    return pl.pallas_call(
        body,
        out_shape=shapes[0] if single else shapes,
        in_specs=smem + vmem,
        out_specs=specs[0] if single else specs,
        scratch_shapes=list(scratch),
        compiler_params=pltpu.CompilerParams(vmem_limit_bytes=limit),
        cost_estimate=pl.CostEstimate(flops=int(cost * 5e8), bytes_accessed=int(cost * 2e6), transcendentals=0),
        name=name,
    )


def start(sems, first, *pairs):
    copies = [pltpu.make_async_copy(src, dst, sems.at[first + k]) for k, (src, dst) in enumerate(pairs)]
    for copy in copies:
        copy.start()
    return copies


def finish(copies):
    for copy in copies:
        copy.wait()


def prepare_body(core_ref, w_in_hbm, w_down_hbm, out_hbm, w_in, w_down, mine, sems):
    loads = start(sems, 0, (w_in_hbm, w_in), (w_down_hbm, w_down))
    place, unit = iota((LANES, PART), 0), iota((LANES, PART), 1)
    block, row, rest = place // 32, place // 16 % 2, place % 16
    first = (block // 2 * 8 + rest // 4 * 2 + block % 2) * 16 + rest % 4 * 2 + row
    second = rest * 16 + 8 + block * 2 + row
    wanted = jnp.where(core_ref[0] == 0, first, second)
    chosen = (unit == wanted).astype(bf16)
    loads[0].wait()
    mine[0] = mm_flip(chosen, w_in[...]).astype(bf16)
    stores = start(sems, 2, *[(mine.at[0], out_hbm.at[k, 0]) for k in range(N_X)])
    loads[1].wait()
    mine[1] = mm(chosen, w_down[...]).astype(bf16)
    stores += start(sems, 2 + N_X, *[(mine.at[1], out_hbm.at[k, 1]) for k in range(N_X)])
    finish(stores)


def attend_body(
    cols_ref, rows_ref, keys_ref, values_ref, embed_ref, gain_self_ref, gain_cross_ref, w_query_hbm, w_key_hbm,
    w_value_hbm, w_self_hbm, cross_query_hbm, cross_out_hbm, states_ref, at_rank_ref, done_ref, ctx_ref, held, sems,
):
    sources = (w_query_hbm, w_key_hbm, w_value_hbm, w_self_hbm, cross_query_hbm, cross_out_hbm)
    loads = [pltpu.make_async_copy(source, held.at[k], sems.at[k]) for k, source in enumerate(sources)]
    for load in loads:
        load.start()
    lane = iota((ROWS, LANES), 1)
    hits = cols_ref[:, 2:3] == lane
    earlier = (iota((ROWS, ROWS), 0) > iota((ROWS, ROWS), 1)).astype(bf16)
    before = mm(earlier, hits.astype(bf16))
    same = (beam_of(0) == beam_of(1)) & (iota((ROWS, ROWS), 0) <= iota((ROWS, ROWS), 1))
    same = same.astype(bf16)
    rank = jnp.sum(jnp.where(hits, before, 0.0), -1, keepdims=True).astype(jnp.int32)
    at_rank_ref[...] = (rank == lane).astype(bf16)
    embed = embed_ref[...]
    names = (iota((32, VOCAB), 0) == iota((32, VOCAB), 1)).astype(bf16)
    table = mm(names, embed).astype(bf16)
    picks = (cols_ref[:, 0:1] == iota((ROWS, 32), 1)).astype(bf16)
    picks_t = (rows_ref[0:1, :] == iota((32, ROWS), 0)).astype(bf16)
    embedded = mm(picks, table)
    for load in loads:
        load.wait()
    query = mm(embedded.astype(bf16), held[0]).astype(bf16)
    keyed = mm(table, held[1])
    valued = mm(table, held[2])
    own = iota((HEADS * 32, WIDTH), 0) // 32 == iota((HEADS * 32, WIDTH), 1) // 64
    key_blocks = jnp.where(own, jnp.concatenate([keyed] * HEADS, 0), 0.0).astype(bf16)
    value_blocks = jnp.where(own, jnp.concatenate([valued] * HEADS, 0), 0.0).astype(bf16)
    scores = (mm_flip(key_blocks, query) * 0.125).reshape(HEADS, 32, ROWS)
    counts = mm(picks_t, same)[None]
    scores = jnp.where(counts > 0.0, scores, -1e30)
    probs = jnp.exp(scores - jnp.max(scores, 1, keepdims=True)) * counts
    probs = probs / jnp.sum(probs, 1, keepdims=True)
    context = mm_tall(probs.reshape(HEADS * 32, ROWS).astype(bf16), value_blocks).astype(bf16)
    unit, _ = norm_parts(embedded + mm(context, held[3]))
    attended = (unit * gain_self_ref[...]).astype(bf16)
    cross_q = mm(attended, held[4]).astype(bf16)
    left = iota((PAD, LANES), 1) < 64
    for s in range(2):
        for pair in range(HEADS // 2):
            lanes = slice(pair * LANES, (pair + 1) * LANES)
            q = cross_q[s * PAD : (s + 1) * PAD, lanes]
            k = keys_ref[s, :, lanes]
            v = values_ref[s, :, lanes]
            both = []
            for mine in (left, jnp.logical_not(left)):
                logit = mm_flip(jnp.where(mine, q, jnp.zeros_like(q)), k) * 0.125
                e = jnp.exp(logit - jnp.max(logit, -1, keepdims=True))
                p = (e / jnp.sum(e, -1, keepdims=True)).astype(bf16)
                both.append(mm(p, v))
            ctx_ref[s * PAD : (s + 1) * PAD, lanes] = jnp.where(left, both[0], both[1]).astype(bf16)
    unit, _ = norm_parts(attended.astype(f32) + mm(ctx_ref[...], held[5]))
    states = (unit * gain_cross_ref[...]).astype(bf16)
    states_ref[...] = states
    done_ref[...] = states[:16, :LANES]


def beam_of(dim):
    shape = (ROWS, 1) if dim == 0 else (1, ROWS)
    row = iota(shape, dim)
    second = (row >= PAD).astype(jnp.int32)
    inside = row - second * PAD
    beam = second * (BEAM + 1)
    for k in range(1, BEAM + 1):
        beam = beam + (inside >= k * (STEPS + 1)).astype(jnp.int32)
    return beam


def half_forward(states, weights_ref, hidden_ref, slope_ref):
    w_in = jnp.concatenate([weights_ref[m, 0] for m in range(N_X)], 0)
    w_down = jnp.concatenate([weights_ref[m, 1] for m in range(N_X)], 0)
    pre = mm_flip(states, w_in)
    square = pre * pre
    tanh = jnp.tanh(pre * (0.7978845608028654 + 0.035677408136300125 * square))
    gate = 0.5 * (1.0 + tanh)
    hidden = (pre * gate).astype(bf16)
    hidden_ref[...] = hidden
    slope_ref[...] = gate * (1.0 + pre * (1.0 - tanh) * (0.7978845608028654 + 0.10703222440890037 * square))
    return mm(hidden, w_down)


def own_body(states_ref, weights_ref, done_ref, hidden_ref, slope_ref, total_ref):
    states = states_ref[...]
    total_ref[...] = states.astype(f32) + half_forward(states, weights_ref, hidden_ref, slope_ref)


def train_body(
    accept_ref, cols_ref, rows_ref, at_rank_ref, states_ref, partial_ref, hidden_1_ref, slope_1_ref, own_ref, other_ref, gain_ref,
    head_ref, message_ref, keep_ref, send_ref, hidden_ref, slope_ref, unit_ref,
):
    states = states_ref[...]
    total = partial_ref[...] + half_forward(states, other_ref, hidden_ref, slope_ref)
    unit, scale = norm_parts(total)
    unit_ref[...] = unit
    gain = gain_ref[...]
    high, low = split(unit * gain)
    names = (iota((32, VOCAB), 0) == iota((32, VOCAB), 1)).astype(bf16)
    head = mm(names, head_ref[...]).astype(bf16)
    logits = mm_flip(head, high) + mm_flip(head, low)
    word = iota((32, ROWS), 0)
    logits = jnp.where(word < VOCAB, logits, -1e30)
    top = jnp.max(logits, 0, keepdims=True)
    grown = jnp.exp(logits - top)
    mass = jnp.sum(grown, 0, keepdims=True)
    is_label = rows_ref[1:2, :] == word
    taken = jnp.sum(jnp.where(is_label, logits, 0.0), 0, keepdims=True) - top - jnp.log(mass)
    row = iota((1, ROWS), 1)
    second = (row >= PAD).astype(jnp.int32)
    beam = beam_of(1) - second
    inside = row - second * PAD
    step = inside
    for k in range(1, BEAM + 1):
        step = step - (step >= STEPS + 1).astype(jnp.int32) * (STEPS + 1)
    beams = jnp.where((beam == iota((16, ROWS), 0)) & (step < STEPS) & (inside < SEG), 1.0, 0.0)
    score = jnp.sum(beams * taken, 1, keepdims=True) / STEPS
    place = iota((16, 1), 0)
    shares = jnp.zeros((16, 1), f32)
    for s in range(2):
        mine = (place >= s * BEAM) & (place < (s + 1) * BEAM)
        e = jnp.where(mine, jnp.exp(score - jnp.max(jnp.where(mine, score, -1e30), 0, keepdims=True)), 0.0)
        share = e / jnp.sum(e, 0, keepdims=True) * accept_ref[s].astype(f32)
        shares = jnp.where(mine, share, shares)
    weight = jnp.sum(beams * shares, 0, keepdims=True)
    to = rows_ref[2:3, :] == iota((LANES, ROWS), 0)
    high, low = split(-weight * taken)
    zero = jnp.zeros((1, ROWS), bf16)
    at_rank = at_rank_ref[...]
    slots = mm(jnp.where(to, high, zero), at_rank) + mm(jnp.where(to, low, zero), at_rank)
    high, low = split(jnp.broadcast_to(weight, (8, ROWS)))
    hits = (cols_ref[:, 2:3] == iota((ROWS, LANES), 1)).astype(bf16)
    sums = mm(high, hits) + mm(low, hits)
    message_ref[:, 0, :] = jnp.broadcast_to(sums[0:1], (N_DP, LANES))
    message_ref[:, 1, :] = slots

    high, low = split(weight * (grown / mass - is_label.astype(f32)))
    unit = unit_ref[...]
    d_unit = gain * mm_tall(jnp.concatenate([high, low], 0), jnp.concatenate([head, head], 0))
    along = jnp.mean(d_unit * unit, -1, keepdims=True)
    d_total = scale * (d_unit - jnp.mean(d_unit, -1, keepdims=True) - unit * along)
    d_out = d_total.astype(bf16)
    dest = jnp.broadcast_to(cols_ref[:, 2:3], (ROWS, LANES)).astype(f32).astype(bf16)
    for ref, hidden, slope, weights in (
        (send_ref, hidden_ref, slope_ref, other_ref),
        (keep_ref, hidden_1_ref, slope_1_ref, own_ref),
    ):
        w_down = jnp.concatenate([weights[m, 1] for m in range(N_X)], 0)
        ref[:, 0:WIDTH] = (mm_flip(d_out, w_down) * slope[...]).astype(bf16)
        ref[:, WIDTH : 2 * WIDTH] = hidden[...]
        ref[:, 2 * WIDTH : 3 * WIDTH] = states
        ref[:, 3 * WIDTH : 4 * WIDTH] = d_out
        ref[:, 4 * WIDTH :] = dest


def term_body(keep_ref, other_ref, got_ref, term_ref, loss_ref, all_ref):
    sums = jnp.sum(got_ref[:, 0, :], 0, keepdims=True)
    loss_ref[...] = got_ref[:, 1, :]
    inverse = 1.0 / jnp.maximum(sums, 1.0)
    lane = iota((ROWS, LANES), 1).astype(f32)
    for place, ref in ((0, keep_ref), (1, other_ref)):
        rows = slice(place * ROWS, (place + 1) * ROWS)
        hits = ref[:, 4 * WIDTH :].astype(f32) == lane
        factor = jnp.sum(jnp.where(hits, inverse, 0.0), -1, keepdims=True)
        all_ref[rows, : 2 * WIDTH] = ref[:, : 2 * WIDTH]
        all_ref[rows, 2 * WIDTH :] = (ref[:, 2 * WIDTH : 4 * WIDTH].astype(f32) * factor).astype(bf16)
    for k in range(2):
        grad = mm_tall(all_ref[:, k * WIDTH : (k + 1) * WIDTH], all_ref[:, (k + 2) * WIDTH : (k + 3) * WIDTH])
        grad = grad.astype(bf16)
        for m in range(N_X):
            for x in range(N_X):
                start = m * LANES + x * 32
                term_ref[x, m * 32 : (m + 1) * 32, k * WIDTH : (k + 1) * WIDTH] = grad[start : start + 32]


def middle_body(got_ref, out_ref, held_ref):
    for m in range(N_X):
        rows = slice(m * 32, (m + 1) * 32)
        total = got_ref[0, rows].astype(f32) + got_ref[1, rows].astype(f32)
        total = total + (got_ref[2, rows].astype(f32) + got_ref[3, rows].astype(f32))
        here = slice(m * 16, (m + 1) * 16)
        for r in range(2):
            for c in range(8):
                held_ref[here, r * 8 + c, :] = total[r * 16 : (r + 1) * 16, c * LANES : (c + 1) * LANES]
        out_ref[here] = held_ref[here].astype(bf16)


def final_body(got_ref, momentum_ref, loss_ref, out_ref, slots_ref):
    total = jnp.sum(got_ref[...].astype(f32), 0)
    for r in range(2):
        for c in range(8):
            lanes = slice(c * LANES, (c + 1) * LANES)
            out_ref[r : r + 1, lanes] = 0.9 * momentum_ref[r : r + 1, lanes] + total[r * 8 + c : r * 8 + c + 1]
    slot, source = iota((N_DP, N_DP * CAP), 1), iota((N_DP, N_DP * CAP), 0)
    offset = slot - source * CAP
    spread = jnp.zeros((N_DP, N_DP * CAP), f32)
    for k in range(CAP):
        spread = jnp.where(offset == k, loss_ref[:, k : k + 1], spread)
    slots_ref[...] = jnp.sum(spread, 0, keepdims=True)


def per_device(
    tokens, accept, dest, mem_keys, mem_values, embed, w_query, w_key, w_value, w_self, cross_query, cross_out,
    gain_self, gain_cross, w_in, w_down, gain_ff, head, momentum,
):
    core = lax.axis_index("core").astype(jnp.int32).reshape(1)
    swap = [(0, 1), (1, 0)]
    half = (ROWS, HALF)

    mine = call(
        prepare_body,
        [((N_X, 2, LANES, WIDTH), bf16)],
        scratch=[
            pltpu.VMEM((WIDTH, PART), bf16),
            pltpu.VMEM((PART, WIDTH), bf16),
            pltpu.VMEM((2, LANES, WIDTH), bf16),
            pltpu.SemaphoreType.DMA((2 + 2 * N_X,)),
        ],
        n_smem=1, n_any=2, out_hbm=True, limit=63_300_000, cost=1, name="prepare",
    )(core, w_in, w_down)
    own_w = lax.all_to_all(mine, "x", 0, 0)

    flat = tokens.reshape(2, SEG)
    nexts = lax.pad(flat, jnp.int32(0), ((0, 0, 0), (-1, PAD - SEG + 1, 0))).reshape(ROWS)
    flat = jnp.pad(flat, ((0, 0), (0, PAD - SEG))).reshape(ROWS)
    place = jnp.pad(dest.reshape(2, BEAM, STEPS), ((0, 0), (0, 0), (0, 1)), constant_values=-1).reshape(2, SEG)
    place = jnp.pad(place, ((0, 0), (0, PAD - SEG)), constant_values=-1).reshape(ROWS)
    rows = jnp.stack([flat, nexts, place, place, place, place, place, place])
    cols = rows.T
    states, at_rank, done = call(
        attend_body,
        [((ROWS, WIDTH), bf16), ((ROWS, LANES), bf16), ((16, LANES), bf16)],
        scratch=[
            pltpu.VMEM((ROWS, WIDTH), bf16),
            pltpu.VMEM((6, WIDTH, WIDTH), bf16),
            pltpu.SemaphoreType.DMA((6,)),
        ],
        n_in=7, n_any=6, limit=61_300_000, cost=8, name="attend",
    )(
        cols, rows, mem_keys, mem_values, embed, gain_self.reshape(1, WIDTH), gain_cross.reshape(1, WIDTH),
        w_query, w_key, w_value, w_self, cross_query, cross_out,
    )
    own_w, done = lax.optimization_barrier((own_w, done))
    other_w = lax.ppermute(own_w, "core", swap)
    hidden, slope, partial = call(
        own_body, [(half, bf16), (half, f32), ((ROWS, WIDTH), f32)], n_in=3, cost=2, name="own"
    )(states, own_w, done)
    gain = gain_ff.reshape(1, WIDTH)
    head = head.T
    message, keep, send = call(
        train_body,
        [((N_DP, 2, LANES), f32), ((ROWS, PAY), bf16), ((ROWS, PAY), bf16)],
        scratch=[pltpu.VMEM(half, bf16), pltpu.VMEM(half, f32), pltpu.VMEM((ROWS, WIDTH), f32)],
        n_smem=1, n_in=11, cost=5, name="train",
    )(accept, cols, rows, at_rank, states, partial, hidden, slope, own_w, other_w, gain, head)
    got = lax.all_to_all(message, DP, 0, 0)
    other = lax.ppermute(send, "core", swap)
    term, loss = call(
        term_body,
        [((N_X, LANES, 2 * WIDTH), bf16), ((N_DP, LANES), f32)],
        scratch=[pltpu.VMEM((2 * ROWS, 4 * WIDTH), bf16)],
        n_in=3, cost=4, name="term",
    )(keep, other, got)
    got = lax.all_to_all(term, EVERY, 0, 0, axis_index_groups=STAGE_1)
    middle = call(
        middle_body, [((64, 16, LANES), bf16)], scratch=[pltpu.VMEM((64, 16, LANES), f32)], n_in=1, cost=1, name="middle"
    )(got)
    got = lax.all_to_all(middle, EVERY, 0, 0, axis_index_groups=STAGE_2)
    return tuple(
        call(final_body, [((2, 2 * WIDTH), f32), ((1, N_DP * CAP), f32)], n_in=3, cost=1, name="final")(got, momentum, loss)
    )


def solution(mesh):
    n_dp, n_mp = mesh.devices.shape
    side = int(np.sqrt(n_dp // 2))
    fine = Mesh(mesh.devices.reshape(side, side, 2, n_mp), EVERY)
    placed = (
        P(EVERY, None, None),
        P(EVERY),
        P(EVERY, None),
        P(EVERY, None, None),
        P(EVERY, None, None),
        P(),
        P(),
        P(),
        P(),
        P(),
        P(),
        P(),
        P(),
        P(),
        P(None, "x"),
        P("x", None),
        P(),
        P(),
        P(EVERY, None),
    )
    return jax.shard_map(
        per_device,
        mesh=fine,
        in_specs=placed,
        out_specs=(P(EVERY, None), P(EVERY, None)),
        check_vma=False,
    )
```

```python
import jax
import jax.numpy as jnp
import numpy as np
from jax import lax
from jax.experimental import pallas as pl
from jax.experimental.pallas import tpu as pltpu
from jax.sharding import Mesh
from jax.sharding import PartitionSpec as P

HEADS = 8
BEAM = 5
STEPS = 30
CAP = 5
SEG = BEAM * (STEPS + 1)
PAD = 160
ROWS = 2 * PAD
WIDTH = 512
FF = 1024
VOCAB = 28
PEAKS = 150
LANES = 128
N_DP = 128
N_X = 4
PART = FF // N_X
HALF = FF // 2
PAY = 4 * WIDTH + LANES
f32 = jnp.float32
bf16 = jnp.bfloat16
FLIP = (((1,), (1,)), ((), ()))
TALL = (((0,), (0,)), ((), ()))
DP = ("z", "y", "core")
EVERY = ("z", "y", "core", "x")
SIDE = 8


def index(z, y, core, x):
    return ((z * SIDE + y) * 2 + core) * N_X + x


def stages():
    side, half, pair, ring = range(SIDE), range(SIDE // 2), range(2), range(N_X)
    one, two = [], []
    for a in half:
        for b in half:
            for x in ring:
                one.append([index(2 * a + z, 2 * b + y, 0, x) for z in pair for y in pair])
    for z in pair:
        for y in pair:
            two.append([index(2 * a + z, 2 * b + y, 0, x) for a in half for b in half for x in ring])
    one += [[index(z, y, 1, x) for x in ring] for z in side for y in side]
    two += [[index(z, y, 1, x) for z in side for y in side] for x in ring]
    return one, two


STAGE_1, STAGE_2 = stages()


def mm(a, b):
    return jnp.dot(a, b, preferred_element_type=f32)


def mm_flip(a, b):
    return lax.dot_general(a, b, FLIP, preferred_element_type=f32)


def mm_tall(a, b):
    return lax.dot_general(a, b, TALL, preferred_element_type=f32)


def iota(shape, dim):
    return lax.broadcasted_iota(jnp.int32, shape, dim)


def norm_parts(values):
    mean = jnp.mean(values, -1, keepdims=True)
    centered = values - mean
    scale = lax.rsqrt(jnp.mean(centered * centered, -1, keepdims=True) + 1e-05)
    return centered * scale, scale


def split(v):
    high = v.astype(bf16)
    return high, (v - high.astype(f32)).astype(bf16)


def call(body, outs, scratch=(), cost=4.0, n_smem=0, n_in=0, n_any=0, out_hbm=False, limit=16 << 20, name=None):
    smem = [pl.BlockSpec(memory_space=pltpu.SMEM)] * n_smem
    vmem = [pl.BlockSpec(memory_space=pltpu.VMEM)] * n_in + [pl.BlockSpec(memory_space=pltpu.HBM)] * n_any
    shapes = [jax.ShapeDtypeStruct(s, d) for s, d in outs]
    specs = [pl.BlockSpec(memory_space=pltpu.HBM if out_hbm else pltpu.VMEM)] * len(outs)
    single = len(outs) == 1
    return pl.pallas_call(
        body,
        out_shape=shapes[0] if single else shapes,
        in_specs=smem + vmem,
        out_specs=specs[0] if single else specs,
        scratch_shapes=list(scratch),
        compiler_params=pltpu.CompilerParams(vmem_limit_bytes=limit),
        cost_estimate=pl.CostEstimate(flops=int(cost * 5e8), bytes_accessed=int(cost * 2e6), transcendentals=0),
        name=name,
    )


def start(sems, first, *pairs):
    copies = [pltpu.make_async_copy(src, dst, sems.at[first + k]) for k, (src, dst) in enumerate(pairs)]
    for copy in copies:
        copy.start()
    return copies


def finish(copies):
    for copy in copies:
        copy.wait()


def prepare_body(core_ref, w_in_hbm, w_down_hbm, out_hbm, w_in, w_down, mine, sems):
    loads = start(sems, 0, (w_in_hbm, w_in), (w_down_hbm, w_down))
    place, unit = iota((LANES, PART), 0), iota((LANES, PART), 1)
    block, row, rest = place // 32, place // 16 % 2, place % 16
    first = (block // 2 * 8 + rest // 4 * 2 + block % 2) * 16 + rest % 4 * 2 + row
    second = rest * 16 + 8 + block * 2 + row
    wanted = jnp.where(core_ref[0] == 0, first, second)
    chosen = (unit == wanted).astype(bf16)
    loads[0].wait()
    mine[0] = mm_flip(chosen, w_in[...]).astype(bf16)
    stores = start(sems, 2, *[(mine.at[0], out_hbm.at[k, 0]) for k in range(N_X)])
    loads[1].wait()
    mine[1] = mm(chosen, w_down[...]).astype(bf16)
    stores += start(sems, 2 + N_X, *[(mine.at[1], out_hbm.at[k, 1]) for k in range(N_X)])
    finish(stores)


def attend_body(
    cols_ref, rows_ref, keys_ref, values_ref, embed_ref, gain_self_ref, gain_cross_ref, w_query_hbm, w_key_hbm,
    w_value_hbm, w_self_hbm, cross_query_hbm, cross_out_hbm, states_ref, at_rank_ref, done_ref, ctx_ref, held, sems,
):
    sources = (w_query_hbm, w_key_hbm, w_value_hbm, w_self_hbm, cross_query_hbm, cross_out_hbm)
    loads = [pltpu.make_async_copy(source, held.at[k], sems.at[k]) for k, source in enumerate(sources)]
    for load in loads:
        load.start()
    lane = iota((ROWS, LANES), 1)
    hits = cols_ref[:, 2:3] == lane
    earlier = (iota((ROWS, ROWS), 0) > iota((ROWS, ROWS), 1)).astype(bf16)
    before = mm(earlier, hits.astype(bf16))
    same = (beam_of(0) == beam_of(1)) & (iota((ROWS, ROWS), 0) <= iota((ROWS, ROWS), 1))
    same = same.astype(bf16)
    rank = jnp.sum(jnp.where(hits, before, 0.0), -1, keepdims=True).astype(jnp.int32)
    at_rank_ref[...] = (rank == lane).astype(bf16)
    embed = embed_ref[...]
    names = (iota((32, VOCAB), 0) == iota((32, VOCAB), 1)).astype(bf16)
    table = mm(names, embed).astype(bf16)
    picks = (cols_ref[:, 0:1] == iota((ROWS, 32), 1)).astype(bf16)
    picks_t = (rows_ref[0:1, :] == iota((32, ROWS), 0)).astype(bf16)
    embedded = mm(picks, table)
    for load in loads:
        load.wait()
    query = mm(embedded.astype(bf16), held[0]).astype(bf16)
    keyed = mm(table, held[1])
    valued = mm(table, held[2])
    own = iota((HEADS * 32, WIDTH), 0) // 32 == iota((HEADS * 32, WIDTH), 1) // 64
    key_blocks = jnp.where(own, jnp.concatenate([keyed] * HEADS, 0), 0.0).astype(bf16)
    value_blocks = jnp.where(own, jnp.concatenate([valued] * HEADS, 0), 0.0).astype(bf16)
    scores = (mm_flip(key_blocks, query) * 0.125).reshape(HEADS, 32, ROWS)
    counts = mm(picks_t, same)[None]
    scores = jnp.where(counts > 0.0, scores, -1e30)
    probs = jnp.exp(scores - jnp.max(scores, 1, keepdims=True)) * counts
    probs = probs / jnp.sum(probs, 1, keepdims=True)
    context = mm_tall(probs.reshape(HEADS * 32, ROWS).astype(bf16), value_blocks).astype(bf16)
    unit, _ = norm_parts(embedded + mm(context, held[3]))
    attended = (unit * gain_self_ref[...]).astype(bf16)
    cross_q = mm(attended, held[4]).astype(bf16)
    left = iota((PAD, LANES), 1) < 64
    for s in range(2):
        for pair in range(HEADS // 2):
            lanes = slice(pair * LANES, (pair + 1) * LANES)
            q = cross_q[s * PAD : (s + 1) * PAD, lanes]
            k = keys_ref[s, :, lanes]
            v = values_ref[s, :, lanes]
            both = []
            for mine in (left, jnp.logical_not(left)):
                logit = mm_flip(jnp.where(mine, q, jnp.zeros_like(q)), k) * 0.125
                e = jnp.exp(logit - jnp.max(logit, -1, keepdims=True))
                p = (e / jnp.sum(e, -1, keepdims=True)).astype(bf16)
                both.append(mm(p, v))
            ctx_ref[s * PAD : (s + 1) * PAD, lanes] = jnp.where(left, both[0], both[1]).astype(bf16)
    unit, _ = norm_parts(attended.astype(f32) + mm(ctx_ref[...], held[5]))
    states = (unit * gain_cross_ref[...]).astype(bf16)
    states_ref[...] = states
    done_ref[...] = states[:16, :LANES]


def beam_of(dim):
    shape = (ROWS, 1) if dim == 0 else (1, ROWS)
    row = iota(shape, dim)
    second = (row >= PAD).astype(jnp.int32)
    inside = row - second * PAD
    beam = second * (BEAM + 1)
    for k in range(1, BEAM + 1):
        beam = beam + (inside >= k * (STEPS + 1)).astype(jnp.int32)
    return beam


def half_forward(states, weights_ref, hidden_ref, slope_ref):
    w_in = jnp.concatenate([weights_ref[m, 0] for m in range(N_X)], 0)
    w_down = jnp.concatenate([weights_ref[m, 1] for m in range(N_X)], 0)
    pre = mm_flip(states, w_in)
    square = pre * pre
    tanh = jnp.tanh(pre * (0.7978845608028654 + 0.035677408136300125 * square))
    gate = 0.5 * (1.0 + tanh)
    hidden = (pre * gate).astype(bf16)
    hidden_ref[...] = hidden
    slope_ref[...] = gate * (1.0 + pre * (1.0 - tanh) * (0.7978845608028654 + 0.10703222440890037 * square))
    return mm(hidden, w_down)


def own_body(states_ref, weights_ref, done_ref, hidden_ref, slope_ref, total_ref):
    states = states_ref[...]
    total_ref[...] = states.astype(f32) + half_forward(states, weights_ref, hidden_ref, slope_ref)


def train_body(
    accept_ref, cols_ref, rows_ref, at_rank_ref, states_ref, partial_ref, hidden_1_ref, slope_1_ref, own_ref, other_ref, gain_ref,
    head_ref, message_ref, keep_ref, send_ref, hidden_ref, slope_ref, unit_ref,
):
    states = states_ref[...]
    total = partial_ref[...] + half_forward(states, other_ref, hidden_ref, slope_ref)
    unit, scale = norm_parts(total)
    unit_ref[...] = unit
    gain = gain_ref[...]
    high, low = split(unit * gain)
    names = (iota((32, VOCAB), 0) == iota((32, VOCAB), 1)).astype(bf16)
    head = mm(names, head_ref[...]).astype(bf16)
    logits = mm_flip(head, high) + mm_flip(head, low)
    word = iota((32, ROWS), 0)
    logits = jnp.where(word < VOCAB, logits, -1e30)
    top = jnp.max(logits, 0, keepdims=True)
    grown = jnp.exp(logits - top)
    mass = jnp.sum(grown, 0, keepdims=True)
    is_label = rows_ref[1:2, :] == word
    taken = jnp.sum(jnp.where(is_label, logits, 0.0), 0, keepdims=True) - top - jnp.log(mass)
    row = iota((1, ROWS), 1)
    second = (row >= PAD).astype(jnp.int32)
    beam = beam_of(1) - second
    inside = row - second * PAD
    step = inside
    for k in range(1, BEAM + 1):
        step = step - (step >= STEPS + 1).astype(jnp.int32) * (STEPS + 1)
    beams = jnp.where((beam == iota((16, ROWS), 0)) & (step < STEPS) & (inside < SEG), 1.0, 0.0)
    score = jnp.sum(beams * taken, 1, keepdims=True) / STEPS
    place = iota((16, 1), 0)
    shares = jnp.zeros((16, 1), f32)
    for s in range(2):
        mine = (place >= s * BEAM) & (place < (s + 1) * BEAM)
        e = jnp.where(mine, jnp.exp(score - jnp.max(jnp.where(mine, score, -1e30), 0, keepdims=True)), 0.0)
        share = e / jnp.sum(e, 0, keepdims=True) * accept_ref[s].astype(f32)
        shares = jnp.where(mine, share, shares)
    weight = jnp.sum(beams * shares, 0, keepdims=True)
    to = rows_ref[2:3, :] == iota((LANES, ROWS), 0)
    high, low = split(-weight * taken)
    zero = jnp.zeros((1, ROWS), bf16)
    at_rank = at_rank_ref[...]
    slots = mm(jnp.where(to, high, zero), at_rank) + mm(jnp.where(to, low, zero), at_rank)
    high, low = split(jnp.broadcast_to(weight, (8, ROWS)))
    hits = (cols_ref[:, 2:3] == iota((ROWS, LANES), 1)).astype(bf16)
    sums = mm(high, hits) + mm(low, hits)
    message_ref[:, 0, :] = jnp.broadcast_to(sums[0:1], (N_DP, LANES))
    message_ref[:, 1, :] = slots

    high, low = split(weight * (grown / mass - is_label.astype(f32)))
    unit = unit_ref[...]
    d_unit = gain * mm_tall(jnp.concatenate([high, low], 0), jnp.concatenate([head, head], 0))
    along = jnp.mean(d_unit * unit, -1, keepdims=True)
    d_total = scale * (d_unit - jnp.mean(d_unit, -1, keepdims=True) - unit * along)
    d_out = d_total.astype(bf16)
    dest = jnp.broadcast_to(cols_ref[:, 2:3], (ROWS, LANES)).astype(f32).astype(bf16)
    for ref, hidden, slope, weights in (
        (send_ref, hidden_ref, slope_ref, other_ref),
        (keep_ref, hidden_1_ref, slope_1_ref, own_ref),
    ):
        w_down = jnp.concatenate([weights[m, 1] for m in range(N_X)], 0)
        ref[:, 0:WIDTH] = (mm_flip(d_out, w_down) * slope[...]).astype(bf16)
        ref[:, WIDTH : 2 * WIDTH] = hidden[...]
        ref[:, 2 * WIDTH : 3 * WIDTH] = states
        ref[:, 3 * WIDTH : 4 * WIDTH] = d_out
        ref[:, 4 * WIDTH :] = dest


def first_body(got_ref, inverse_ref, loss_ref):
    sums = jnp.sum(got_ref[:, 0, :], 0, keepdims=True)
    inverse_ref[...] = jnp.broadcast_to(1.0 / jnp.maximum(sums, 1.0), (8, LANES))
    loss_ref[...] = got_ref[:, 1, :]


def term_body(keep_ref, other_ref, inverse_ref, term_ref, all_ref):
    inverse = inverse_ref[0:1, :]
    lane = iota((ROWS, LANES), 1).astype(f32)
    for place, ref in ((0, keep_ref), (1, other_ref)):
        rows = slice(place * ROWS, (place + 1) * ROWS)
        hits = ref[:, 4 * WIDTH :].astype(f32) == lane
        factor = jnp.sum(jnp.where(hits, inverse, 0.0), -1, keepdims=True)
        all_ref[rows, : 2 * WIDTH] = ref[:, : 2 * WIDTH]
        all_ref[rows, 2 * WIDTH :] = (ref[:, 2 * WIDTH : 4 * WIDTH].astype(f32) * factor).astype(bf16)
    for k in range(2):
        grad = mm_tall(all_ref[:, k * WIDTH : (k + 1) * WIDTH], all_ref[:, (k + 2) * WIDTH : (k + 3) * WIDTH])
        grad = grad.astype(bf16)
        for m in range(N_X):
            for x in range(N_X):
                start = m * LANES + x * 32
                term_ref[x, m * 32 : (m + 1) * 32, k * WIDTH : (k + 1) * WIDTH] = grad[start : start + 32]


def middle_body(got_ref, out_ref, held_ref):
    for m in range(N_X):
        rows = slice(m * 32, (m + 1) * 32)
        total = got_ref[0, rows].astype(f32) + got_ref[1, rows].astype(f32)
        total = total + (got_ref[2, rows].astype(f32) + got_ref[3, rows].astype(f32))
        here = slice(m * 16, (m + 1) * 16)
        for r in range(2):
            for c in range(8):
                held_ref[here, r * 8 + c, :] = total[r * 16 : (r + 1) * 16, c * LANES : (c + 1) * LANES]
        out_ref[here] = held_ref[here].astype(bf16)


def final_body(got_ref, momentum_ref, loss_ref, out_ref, slots_ref):
    total = jnp.sum(got_ref[...].astype(f32), 0)
    for r in range(2):
        for c in range(8):
            lanes = slice(c * LANES, (c + 1) * LANES)
            out_ref[r : r + 1, lanes] = 0.9 * momentum_ref[r : r + 1, lanes] + total[r * 8 + c : r * 8 + c + 1]
    slot, source = iota((N_DP, N_DP * CAP), 1), iota((N_DP, N_DP * CAP), 0)
    offset = slot - source * CAP
    spread = jnp.zeros((N_DP, N_DP * CAP), f32)
    for k in range(CAP):
        spread = jnp.where(offset == k, loss_ref[:, k : k + 1], spread)
    slots_ref[...] = jnp.sum(spread, 0, keepdims=True)


def per_device(
    tokens, accept, dest, mem_keys, mem_values, embed, w_query, w_key, w_value, w_self, cross_query, cross_out,
    gain_self, gain_cross, w_in, w_down, gain_ff, head, momentum,
):
    core = lax.axis_index("core").astype(jnp.int32).reshape(1)
    swap = [(0, 1), (1, 0)]
    half = (ROWS, HALF)

    mine = call(
        prepare_body,
        [((N_X, 2, LANES, WIDTH), bf16)],
        scratch=[
            pltpu.VMEM((WIDTH, PART), bf16),
            pltpu.VMEM((PART, WIDTH), bf16),
            pltpu.VMEM((2, LANES, WIDTH), bf16),
            pltpu.SemaphoreType.DMA((2 + 2 * N_X,)),
        ],
        n_smem=1, n_any=2, out_hbm=True, limit=63_300_000, cost=1, name="prepare",
    )(core, w_in, w_down)
    own_w = lax.all_to_all(mine, "x", 0, 0)

    flat = tokens.reshape(2, SEG)
    nexts = lax.pad(flat, jnp.int32(0), ((0, 0, 0), (-1, PAD - SEG + 1, 0))).reshape(ROWS)
    flat = jnp.pad(flat, ((0, 0), (0, PAD - SEG))).reshape(ROWS)
    place = jnp.pad(dest.reshape(2, BEAM, STEPS), ((0, 0), (0, 0), (0, 1)), constant_values=-1).reshape(2, SEG)
    place = jnp.pad(place, ((0, 0), (0, PAD - SEG)), constant_values=-1).reshape(ROWS)
    rows = jnp.stack([flat, nexts, place, place, place, place, place, place])
    cols = rows.T
    states, at_rank, done = call(
        attend_body,
        [((ROWS, WIDTH), bf16), ((ROWS, LANES), bf16), ((16, LANES), bf16)],
        scratch=[
            pltpu.VMEM((ROWS, WIDTH), bf16),
            pltpu.VMEM((6, WIDTH, WIDTH), bf16),
            pltpu.SemaphoreType.DMA((6,)),
        ],
        n_in=7, n_any=6, limit=61_300_000, cost=8, name="attend",
    )(
        cols, rows, mem_keys, mem_values, embed, gain_self.reshape(1, WIDTH), gain_cross.reshape(1, WIDTH),
        w_query, w_key, w_value, w_self, cross_query, cross_out,
    )
    own_w, done = lax.optimization_barrier((own_w, done))
    other_w = lax.ppermute(own_w, "core", swap)
    hidden, slope, partial = call(
        own_body, [(half, bf16), (half, f32), ((ROWS, WIDTH), f32)], n_in=3, cost=2, name="own"
    )(states, own_w, done)
    gain = gain_ff.reshape(1, WIDTH)
    head = head.T
    message, keep, send = call(
        train_body,
        [((N_DP, 2, LANES), f32), ((ROWS, PAY), bf16), ((ROWS, PAY), bf16)],
        scratch=[pltpu.VMEM(half, bf16), pltpu.VMEM(half, f32), pltpu.VMEM((ROWS, WIDTH), f32)],
        n_smem=1, n_in=11, limit=51500000, cost=5, name="train",
    )(accept, cols, rows, at_rank, states, partial, hidden, slope, own_w, other_w, gain, head)
    got = lax.all_to_all(message, DP, 0, 0)
    other = lax.ppermute(send, "core", swap)
    inverse, loss = call(first_body, [((8, LANES), f32), ((N_DP, LANES), f32)], n_in=1, cost=40, name="first")(got)
    term = call(
        term_body,
        [((N_X, LANES, 2 * WIDTH), bf16)],
        scratch=[pltpu.VMEM((2 * ROWS, 4 * WIDTH), bf16)],
        n_in=3, cost=4, name="term",
    )(keep, other, inverse)
    got = lax.all_to_all(term, EVERY, 0, 0, axis_index_groups=STAGE_1)
    middle = call(
        middle_body, [((64, 16, LANES), bf16)], scratch=[pltpu.VMEM((64, 16, LANES), f32)], n_in=1, cost=1, name="middle"
    )(got)
    got = lax.all_to_all(middle, EVERY, 0, 0, axis_index_groups=STAGE_2)
    return tuple(
        call(final_body, [((2, 2 * WIDTH), f32), ((1, N_DP * CAP), f32)], n_in=3, cost=1, name="final")(got, momentum, loss)
    )


def solution(mesh):
    n_dp, n_mp = mesh.devices.shape
    side = int(np.sqrt(n_dp // 2))
    fine = Mesh(mesh.devices.reshape(side, side, 2, n_mp), EVERY)
    placed = (
        P(EVERY, None, None),
        P(EVERY),
        P(EVERY, None),
        P(EVERY, None, None),
        P(EVERY, None, None),
        P(),
        P(),
        P(),
        P(),
        P(),
        P(),
        P(),
        P(),
        P(),
        P(None, "x"),
        P("x", None),
        P(),
        P(),
        P(EVERY, None),
    )
    return jax.shard_map(
        per_device,
        mesh=fine,
        in_specs=placed,
        out_specs=(P(EVERY, None), P(EVERY, None)),
        check_vma=False,
    )
```

```python
import jax
import jax.numpy as jnp
import numpy as np
from jax import lax
from jax.experimental import pallas as pl
from jax.experimental.pallas import tpu as pltpu
from jax.sharding import Mesh
from jax.sharding import PartitionSpec as P

HEADS = 8
BEAM = 5
STEPS = 30
CAP = 5
SEG = BEAM * (STEPS + 1)
PAD = 160
ROWS = 2 * PAD
WIDTH = 512
FF = 1024
VOCAB = 28
PEAKS = 150
LANES = 128
N_DP = 128
N_X = 4
PART = FF // N_X
HALF = FF // 2
PAY = 4 * WIDTH + LANES
f32 = jnp.float32
bf16 = jnp.bfloat16
FLIP = (((1,), (1,)), ((), ()))
TALL = (((0,), (0,)), ((), ()))
DP = ("z", "y", "core")
EVERY = ("z", "y", "core", "x")
SIDE = 8


def index(z, y, core, x):
    return ((z * SIDE + y) * 2 + core) * N_X + x


def stages():
    side, half, pair, ring = range(SIDE), range(SIDE // 2), range(2), range(N_X)
    one, two = [], []
    for a in half:
        for b in half:
            for x in ring:
                one.append([index(2 * a + z, 2 * b + y, 0, x) for z in pair for y in pair])
    for z in pair:
        for y in pair:
            two.append([index(2 * a + z, 2 * b + y, 0, x) for a in half for b in half for x in ring])
    one += [[index(z, y, 1, x) for x in ring] for z in side for y in side]
    two += [[index(z, y, 1, x) for z in side for y in side] for x in ring]
    weights = [[index(z, y, core, x) for core in pair for z in side for y in side] for x in ring]
    return one, two, weights


STAGE_1, STAGE_2, SUMS = stages()


def mm(a, b):
    return jnp.dot(a, b, preferred_element_type=f32)


def mm_flip(a, b):
    return lax.dot_general(a, b, FLIP, preferred_element_type=f32)


def mm_tall(a, b):
    return lax.dot_general(a, b, TALL, preferred_element_type=f32)


def iota(shape, dim):
    return lax.broadcasted_iota(jnp.int32, shape, dim)


def norm_parts(values):
    mean = jnp.mean(values, -1, keepdims=True)
    centered = values - mean
    scale = lax.rsqrt(jnp.mean(centered * centered, -1, keepdims=True) + 1e-05)
    return centered * scale, scale


def split(v):
    high = v.astype(bf16)
    return high, (v - high.astype(f32)).astype(bf16)


def call(body, outs, scratch=(), cost=4.0, n_smem=0, n_in=0, n_any=0, out_hbm=False, limit=16 << 20, name=None):
    smem = [pl.BlockSpec(memory_space=pltpu.SMEM)] * n_smem
    vmem = [pl.BlockSpec(memory_space=pltpu.VMEM)] * n_in + [pl.BlockSpec(memory_space=pltpu.HBM)] * n_any
    shapes = [jax.ShapeDtypeStruct(s, d) for s, d in outs]
    specs = [pl.BlockSpec(memory_space=pltpu.HBM if out_hbm else pltpu.VMEM)] * len(outs)
    single = len(outs) == 1
    return pl.pallas_call(
        body,
        out_shape=shapes[0] if single else shapes,
        in_specs=smem + vmem,
        out_specs=specs[0] if single else specs,
        scratch_shapes=list(scratch),
        compiler_params=pltpu.CompilerParams(vmem_limit_bytes=limit),
        cost_estimate=pl.CostEstimate(flops=int(cost * 5e8), bytes_accessed=int(cost * 2e6), transcendentals=0),
        name=name,
    )


def start(sems, first, *pairs):
    copies = [pltpu.make_async_copy(src, dst, sems.at[first + k]) for k, (src, dst) in enumerate(pairs)]
    for copy in copies:
        copy.start()
    return copies


def finish(copies):
    for copy in copies:
        copy.wait()


def prepare_body(core_ref, w_in_hbm, w_down_hbm, out_hbm, w_in, w_down, mine, sems):
    loads = start(sems, 0, (w_in_hbm, w_in), (w_down_hbm, w_down))
    place, unit = iota((LANES, PART), 0), iota((LANES, PART), 1)
    block, row, rest = place // 32, place // 16 % 2, place % 16
    first = (block // 2 * 8 + rest // 4 * 2 + block % 2) * 16 + rest % 4 * 2 + row
    second = rest * 16 + 8 + block * 2 + row
    wanted = jnp.where(core_ref[0] == 0, first, second)
    chosen = (unit == wanted).astype(bf16)
    loads[0].wait()
    mine[0] = mm_flip(chosen, w_in[...]).astype(bf16)
    stores = start(sems, 2, *[(mine.at[0], out_hbm.at[k, 0]) for k in range(N_X)])
    loads[1].wait()
    mine[1] = mm(chosen, w_down[...]).astype(bf16)
    stores += start(sems, 2 + N_X, *[(mine.at[1], out_hbm.at[k, 1]) for k in range(N_X)])
    finish(stores)


def attend_body(
    cols_ref, rows_ref, keys_ref, values_ref, embed_ref, gain_self_ref, gain_cross_ref, w_query_hbm, w_key_hbm,
    w_value_hbm, w_self_hbm, cross_query_hbm, cross_out_hbm, states_ref, at_rank_ref, done_ref, ctx_ref, held, sems,
):
    sources = (w_query_hbm, w_key_hbm, w_value_hbm, w_self_hbm, cross_query_hbm, cross_out_hbm)
    loads = [pltpu.make_async_copy(source, held.at[k], sems.at[k]) for k, source in enumerate(sources)]
    for load in loads:
        load.start()
    lane = iota((ROWS, LANES), 1)
    hits = cols_ref[:, 2:3] == lane
    earlier = (iota((ROWS, ROWS), 0) > iota((ROWS, ROWS), 1)).astype(bf16)
    before = mm(earlier, hits.astype(bf16))
    same = (beam_of(0) == beam_of(1)) & (iota((ROWS, ROWS), 0) <= iota((ROWS, ROWS), 1))
    same = same.astype(bf16)
    rank = jnp.sum(jnp.where(hits, before, 0.0), -1, keepdims=True).astype(jnp.int32)
    at_rank_ref[...] = (rank == lane).astype(bf16)
    embed = embed_ref[...]
    names = (iota((32, VOCAB), 0) == iota((32, VOCAB), 1)).astype(bf16)
    table = mm(names, embed).astype(bf16)
    picks = (cols_ref[:, 0:1] == iota((ROWS, 32), 1)).astype(bf16)
    picks_t = (rows_ref[0:1, :] == iota((32, ROWS), 0)).astype(bf16)
    embedded = mm(picks, table)
    for load in loads:
        load.wait()
    query = mm(embedded.astype(bf16), held[0]).astype(bf16)
    keyed = mm(table, held[1])
    valued = mm(table, held[2])
    own = iota((HEADS * 32, WIDTH), 0) // 32 == iota((HEADS * 32, WIDTH), 1) // 64
    key_blocks = jnp.where(own, jnp.concatenate([keyed] * HEADS, 0), 0.0).astype(bf16)
    value_blocks = jnp.where(own, jnp.concatenate([valued] * HEADS, 0), 0.0).astype(bf16)
    scores = (mm_flip(key_blocks, query) * 0.125).reshape(HEADS, 32, ROWS)
    counts = mm(picks_t, same)[None]
    scores = jnp.where(counts > 0.0, scores, -1e30)
    probs = jnp.exp(scores - jnp.max(scores, 1, keepdims=True)) * counts
    probs = probs / jnp.sum(probs, 1, keepdims=True)
    context = mm_tall(probs.reshape(HEADS * 32, ROWS).astype(bf16), value_blocks).astype(bf16)
    unit, _ = norm_parts(embedded + mm(context, held[3]))
    attended = (unit * gain_self_ref[...]).astype(bf16)
    cross_q = mm(attended, held[4]).astype(bf16)
    left = iota((PAD, LANES), 1) < 64
    for s in range(2):
        for pair in range(HEADS // 2):
            lanes = slice(pair * LANES, (pair + 1) * LANES)
            q = cross_q[s * PAD : (s + 1) * PAD, lanes]
            k = keys_ref[s, :, lanes]
            v = values_ref[s, :, lanes]
            both = []
            for mine in (left, jnp.logical_not(left)):
                logit = mm_flip(jnp.where(mine, q, jnp.zeros_like(q)), k) * 0.125
                e = jnp.exp(logit - jnp.max(logit, -1, keepdims=True))
                p = (e / jnp.sum(e, -1, keepdims=True)).astype(bf16)
                both.append(mm(p, v))
            ctx_ref[s * PAD : (s + 1) * PAD, lanes] = jnp.where(left, both[0], both[1]).astype(bf16)
    unit, _ = norm_parts(attended.astype(f32) + mm(ctx_ref[...], held[5]))
    states = (unit * gain_cross_ref[...]).astype(bf16)
    states_ref[...] = states
    done_ref[...] = states[:16, :LANES]


def beam_of(dim):
    shape = (ROWS, 1) if dim == 0 else (1, ROWS)
    row = iota(shape, dim)
    second = (row >= PAD).astype(jnp.int32)
    inside = row - second * PAD
    beam = second * (BEAM + 1)
    for k in range(1, BEAM + 1):
        beam = beam + (inside >= k * (STEPS + 1)).astype(jnp.int32)
    return beam


def half_forward(states, weights_ref, hidden_ref, slope_ref):
    w_in = jnp.concatenate([weights_ref[m, 0] for m in range(N_X)], 0)
    w_down = jnp.concatenate([weights_ref[m, 1] for m in range(N_X)], 0)
    pre = mm_flip(states, w_in)
    square = pre * pre
    tanh = jnp.tanh(pre * (0.7978845608028654 + 0.035677408136300125 * square))
    gate = 0.5 * (1.0 + tanh)
    hidden = (pre * gate).astype(bf16)
    hidden_ref[...] = hidden
    slope_ref[...] = gate * (1.0 + pre * (1.0 - tanh) * (0.7978845608028654 + 0.10703222440890037 * square))
    return mm(hidden, w_down)


def own_body(states_ref, weights_ref, done_ref, hidden_ref, slope_ref, total_ref):
    states = states_ref[...]
    total_ref[...] = states.astype(f32) + half_forward(states, weights_ref, hidden_ref, slope_ref)


def train_body(
    accept_ref, cols_ref, rows_ref, at_rank_ref, states_ref, partial_ref, hidden_1_ref, slope_1_ref, own_ref, other_ref, gain_ref,
    head_ref, message_ref, keep_ref, send_ref, hidden_ref, slope_ref, unit_ref,
):
    states = states_ref[...]
    total = partial_ref[...] + half_forward(states, other_ref, hidden_ref, slope_ref)
    unit, scale = norm_parts(total)
    unit_ref[...] = unit
    gain = gain_ref[...]
    high, low = split(unit * gain)
    names = (iota((32, VOCAB), 0) == iota((32, VOCAB), 1)).astype(bf16)
    head = mm(names, head_ref[...]).astype(bf16)
    logits = mm_flip(head, high) + mm_flip(head, low)
    word = iota((32, ROWS), 0)
    logits = jnp.where(word < VOCAB, logits, -1e30)
    top = jnp.max(logits, 0, keepdims=True)
    grown = jnp.exp(logits - top)
    mass = jnp.sum(grown, 0, keepdims=True)
    is_label = rows_ref[1:2, :] == word
    taken = jnp.sum(jnp.where(is_label, logits, 0.0), 0, keepdims=True) - top - jnp.log(mass)
    row = iota((1, ROWS), 1)
    second = (row >= PAD).astype(jnp.int32)
    beam = beam_of(1) - second
    inside = row - second * PAD
    step = inside
    for k in range(1, BEAM + 1):
        step = step - (step >= STEPS + 1).astype(jnp.int32) * (STEPS + 1)
    beams = jnp.where((beam == iota((16, ROWS), 0)) & (step < STEPS) & (inside < SEG), 1.0, 0.0)
    score = jnp.sum(beams * taken, 1, keepdims=True) / STEPS
    place = iota((16, 1), 0)
    shares = jnp.zeros((16, 1), f32)
    for s in range(2):
        mine = (place >= s * BEAM) & (place < (s + 1) * BEAM)
        e = jnp.where(mine, jnp.exp(score - jnp.max(jnp.where(mine, score, -1e30), 0, keepdims=True)), 0.0)
        share = e / jnp.sum(e, 0, keepdims=True) * accept_ref[s].astype(f32)
        shares = jnp.where(mine, share, shares)
    weight = jnp.sum(beams * shares, 0, keepdims=True)
    to = rows_ref[2:3, :] == iota((LANES, ROWS), 0)
    high, low = split(-weight * taken)
    zero = jnp.zeros((1, ROWS), bf16)
    at_rank = at_rank_ref[...]
    slots = mm(jnp.where(to, high, zero), at_rank) + mm(jnp.where(to, low, zero), at_rank)
    high, low = split(jnp.broadcast_to(weight, (8, ROWS)))
    hits = (cols_ref[:, 2:3] == iota((ROWS, LANES), 1)).astype(bf16)
    sums = mm(high, hits) + mm(low, hits)
    message_ref[:, 0, :] = jnp.broadcast_to(sums[0:1], (N_DP, LANES))
    message_ref[:, 1, :] = slots

    high, low = split(weight * (grown / mass - is_label.astype(f32)))
    unit = unit_ref[...]
    d_unit = gain * mm_tall(jnp.concatenate([high, low], 0), jnp.concatenate([head, head], 0))
    along = jnp.mean(d_unit * unit, -1, keepdims=True)
    d_total = scale * (d_unit - jnp.mean(d_unit, -1, keepdims=True) - unit * along)
    d_out = d_total.astype(bf16)
    dest = jnp.broadcast_to(cols_ref[:, 2:3], (ROWS, LANES)).astype(f32).astype(bf16)
    for ref, hidden, slope, weights in (
        (send_ref, hidden_ref, slope_ref, other_ref),
        (keep_ref, hidden_1_ref, slope_1_ref, own_ref),
    ):
        w_down = jnp.concatenate([weights[m, 1] for m in range(N_X)], 0)
        ref[:, 0:WIDTH] = (mm_flip(d_out, w_down) * slope[...]).astype(bf16)
        ref[:, WIDTH : 2 * WIDTH] = hidden[...]
        ref[:, 2 * WIDTH : 3 * WIDTH] = states
        ref[:, 3 * WIDTH : 4 * WIDTH] = d_out
        ref[:, 4 * WIDTH :] = dest


def term_body(keep_ref, other_ref, got_ref, term_ref, loss_ref, all_ref):
    sums = jnp.sum(got_ref[:, 0, :], 0, keepdims=True)
    loss_ref[...] = got_ref[:, 1, :]
    inverse = 1.0 / jnp.maximum(sums, 1.0)
    lane = iota((ROWS, LANES), 1).astype(f32)
    for place, ref in ((0, keep_ref), (1, other_ref)):
        rows = slice(place * ROWS, (place + 1) * ROWS)
        hits = ref[:, 4 * WIDTH :].astype(f32) == lane
        factor = jnp.sum(jnp.where(hits, inverse, 0.0), -1, keepdims=True)
        all_ref[rows, : 2 * WIDTH] = ref[:, : 2 * WIDTH]
        all_ref[rows, 2 * WIDTH :] = (ref[:, 2 * WIDTH : 4 * WIDTH].astype(f32) * factor).astype(bf16)
    for k in range(2):
        grad = mm_tall(all_ref[:, k * WIDTH : (k + 1) * WIDTH], all_ref[:, (k + 2) * WIDTH : (k + 3) * WIDTH])
        grad = grad.astype(bf16)
        for m in range(N_X):
            for x in range(N_X):
                start = m * LANES + x * 32
                term_ref[x, m * 32 : (m + 1) * 32, k * WIDTH : (k + 1) * WIDTH] = grad[start : start + 32]


def middle_body(got_ref, out_ref, held_ref):
    for m in range(N_X):
        rows = slice(m * 32, (m + 1) * 32)
        total = got_ref[0, rows].astype(f32) + got_ref[1, rows].astype(f32)
        total = total + (got_ref[2, rows].astype(f32) + got_ref[3, rows].astype(f32))
        here = slice(m * 16, (m + 1) * 16)
        for r in range(2):
            for c in range(8):
                held_ref[here, r * 8 + c, :] = total[r * 16 : (r + 1) * 16, c * LANES : (c + 1) * LANES]
        out_ref[here] = held_ref[here].astype(bf16)


def final_body(got_ref, momentum_ref, loss_ref, out_ref, slots_ref):
    total = jnp.sum(got_ref[...].astype(f32), 0)
    for r in range(2):
        for c in range(8):
            lanes = slice(c * LANES, (c + 1) * LANES)
            out_ref[r : r + 1, lanes] = 0.9 * momentum_ref[r : r + 1, lanes] + total[r * 8 + c : r * 8 + c + 1]
    slot, source = iota((N_DP, N_DP * CAP), 1), iota((N_DP, N_DP * CAP), 0)
    offset = slot - (source % (N_DP // 2) * 2 + source // (N_DP // 2)) * CAP
    spread = jnp.zeros((N_DP, N_DP * CAP), f32)
    for k in range(CAP):
        spread = jnp.where(offset == k, loss_ref[:, k : k + 1], spread)
    slots_ref[...] = jnp.sum(spread, 0, keepdims=True)


def per_device(
    tokens, accept, dest, mem_keys, mem_values, embed, w_query, w_key, w_value, w_self, cross_query, cross_out,
    gain_self, gain_cross, w_in, w_down, gain_ff, head, momentum,
):
    core = lax.axis_index("core").astype(jnp.int32).reshape(1)
    swap = [(0, 1), (1, 0)]
    half = (ROWS, HALF)

    mine = call(
        prepare_body,
        [((N_X, 2, LANES, WIDTH), bf16)],
        scratch=[
            pltpu.VMEM((WIDTH, PART), bf16),
            pltpu.VMEM((PART, WIDTH), bf16),
            pltpu.VMEM((2, LANES, WIDTH), bf16),
            pltpu.SemaphoreType.DMA((2 + 2 * N_X,)),
        ],
        n_smem=1, n_any=2, out_hbm=True, limit=63_300_000, cost=1, name="prepare",
    )(core, w_in, w_down)
    own_w = lax.all_to_all(mine, "x", 0, 0)

    flat = tokens.reshape(2, SEG)
    nexts = lax.pad(flat, jnp.int32(0), ((0, 0, 0), (-1, PAD - SEG + 1, 0))).reshape(ROWS)
    flat = jnp.pad(flat, ((0, 0), (0, PAD - SEG))).reshape(ROWS)
    dest = dest % 2 * (N_DP // 2) + dest // 2
    place = jnp.pad(dest.reshape(2, BEAM, STEPS), ((0, 0), (0, 0), (0, 1)), constant_values=-1).reshape(2, SEG)
    place = jnp.pad(place, ((0, 0), (0, PAD - SEG)), constant_values=-1).reshape(ROWS)
    rows = jnp.stack([flat, nexts, place, place, place, place, place, place])
    cols = rows.T
    states, at_rank, done = call(
        attend_body,
        [((ROWS, WIDTH), bf16), ((ROWS, LANES), bf16), ((16, LANES), bf16)],
        scratch=[
            pltpu.VMEM((ROWS, WIDTH), bf16),
            pltpu.VMEM((6, WIDTH, WIDTH), bf16),
            pltpu.SemaphoreType.DMA((6,)),
        ],
        n_in=7, n_any=6, limit=61_300_000, cost=8, name="attend",
    )(
        cols, rows, mem_keys, mem_values, embed, gain_self.reshape(1, WIDTH), gain_cross.reshape(1, WIDTH),
        w_query, w_key, w_value, w_self, cross_query, cross_out,
    )
    own_w, done = lax.optimization_barrier((own_w, done))
    other_w = lax.ppermute(own_w, "core", swap)
    hidden, slope, partial = call(
        own_body, [(half, bf16), (half, f32), ((ROWS, WIDTH), f32)], n_in=3, cost=2, name="own"
    )(states, own_w, done)
    gain = gain_ff.reshape(1, WIDTH)
    head = head.T
    message, keep, send = call(
        train_body,
        [((N_DP, 2, LANES), f32), ((ROWS, PAY), bf16), ((ROWS, PAY), bf16)],
        scratch=[pltpu.VMEM(half, bf16), pltpu.VMEM(half, f32), pltpu.VMEM((ROWS, WIDTH), f32)],
        n_smem=1, n_in=11, cost=5, name="train",
    )(accept, cols, rows, at_rank, states, partial, hidden, slope, own_w, other_w, gain, head)
    got = lax.all_to_all(message, EVERY, 0, 0, axis_index_groups=SUMS)
    other = lax.ppermute(send, "core", swap)
    term, loss = call(
        term_body,
        [((N_X, LANES, 2 * WIDTH), bf16), ((N_DP, LANES), f32)],
        scratch=[pltpu.VMEM((2 * ROWS, 4 * WIDTH), bf16)],
        n_in=3, cost=4, name="term",
    )(keep, other, got)
    got = lax.all_to_all(term, EVERY, 0, 0, axis_index_groups=STAGE_1)
    middle = call(
        middle_body, [((64, 16, LANES), bf16)], scratch=[pltpu.VMEM((64, 16, LANES), f32)], n_in=1, cost=1, name="middle"
    )(got)
    got = lax.all_to_all(middle, EVERY, 0, 0, axis_index_groups=STAGE_2)
    return tuple(
        call(final_body, [((2, 2 * WIDTH), f32), ((1, N_DP * CAP), f32)], n_in=3, cost=1, name="final")(got, momentum, loss)
    )


def solution(mesh):
    n_dp, n_mp = mesh.devices.shape
    side = int(np.sqrt(n_dp // 2))
    fine = Mesh(mesh.devices.reshape(side, side, 2, n_mp), EVERY)
    placed = (
        P(EVERY, None, None),
        P(EVERY),
        P(EVERY, None),
        P(EVERY, None, None),
        P(EVERY, None, None),
        P(),
        P(),
        P(),
        P(),
        P(),
        P(),
        P(),
        P(),
        P(),
        P(None, "x"),
        P("x", None),
        P(),
        P(),
        P(EVERY, None),
    )
    return jax.shard_map(
        per_device,
        mesh=fine,
        in_specs=placed,
        out_specs=(P(EVERY, None), P(EVERY, None)),
        check_vma=False,
    )
```
